32 devices in a mesh: narrow: 4 (over y, core), wide: 8 (over z, x).
Axes of the slice: x: 2, y: 2, z: 4, core: 2. Of those that a mesh axis runs over, the one named last changes fastest.
Arguments:
- vis_pixels: bfloat16 [8192, 1536], P(('narrow', 'wide')), may hold values from -6 to 6
- target: bfloat16 [86016, 1536], P(('narrow', 'wide')), may hold values from -6 to 6
- clip_lens: int32 [32, 3], P(('narrow', 'wide')), may hold values from 0 to 2592, as said below
- vis_index: int32 [32, 256], P(('narrow', 'wide')), may hold values from 0 to 2687, as said below
- params_enc: float32 [8564736], P('wide'), may hold values from -2 to 2
- m_enc: float32 [8564736], P('wide'), may hold values from -2.670288e-05 to 2.670288e-05
- v_enc: float32 [8564736], P('wide'), may hold values from 1.20378065e-11 to 4.8114637e-11
- params_dec: float32 [2367488], P('wide'), may hold values from -2 to 2
- m_dec: float32 [2367488], P('wide'), may hold values from -2.670288e-05 to 2.670288e-05
- v_dec: float32 [2367488], P('wide'), may hold values from 1.20378065e-11 to 4.8114637e-11
Outputs:
- loss_sum: float32 [], replicated
- masked_count: float32 [], replicated
- grad_norm: float32 [], replicated
- new_m_enc: float32 [8564736], P('wide')
- new_v_enc: float32 [8564736], P('wide')
- new_params_enc: float32 [8564736], P('wide')
- new_m_dec: float32 [2367488], P('wide')
- new_v_dec: float32 [2367488], P('wide')
- new_params_dec: float32 [2367488], P('wide')
The draws below stay inside these ranges and needn't reach their ends.
Inputs may be any that keep to these rules, and one draw needn't show every extreme that they name: `clip_lens`: row p is one of (2592, 0, 0), (800, 1568, 0), (800, 800, 800): the clips packed on device p in order, 0 for no clip; every pattern occurs in every draw. `vis_index`: row p lists, clip by clip and within a clip frame by frame, the pack positions of the visible tubelets: a clip of 8 frames of S cells shows the same K cells in every frame (K = 10, 20, 32 for S = 100, 196, 324), increasing within a frame; the remaining slots hold 2687.
All inputs are finite; a program needn't handle non-finite values.
Results may differ from the reference program's by a relative error of at most 0.0005.
The reference program's roundings to bfloat16 on the way count: a program that leaves them out, or rounds other values in their place, can miss the bound.
Values may be sent and summed in bfloat16 or wider, within the bound.
No kernel may reach another device: no remote copies, remote signals or barrier semaphores. Data moves between devices by JAX's collectives and lax.ppermute only.
A program may use at most 512 MiB of HBM per device.

```python
import math
import jax
import jax.numpy as jnp
from jax import lax

D = 768
HEADS = 12
FF = 3072
DD = 384
DHEADS = 6
DFF = 1536
PIX = 1536
FRAMES = 8
S1 = 100
S2 = 196
S3 = 324
K1 = 10
K2 = 20
K3 = 32
QB = 896
STEP = 10
TOK_DEV = 2688
VIS_DEV = 256
PE = 8564736
PD = 2367488
DEVICES = 32


def tube_slots(key, cells, keep, offset):
    chosen = jnp.sort(jax.random.permutation(key, cells)[:keep]).astype(jnp.int32)
    frames = jnp.arange(FRAMES, dtype=jnp.int32)[:, None] * cells
    return (offset + frames + chosen[None, :]).reshape(-1).astype(jnp.int32)


def padded(indices):
    filler = jnp.full((VIS_DEV - indices.shape[0],), TOK_DEV - 1, jnp.int32)
    return jnp.concatenate([indices, filler])


def layout_draw(key):
    base_key = jax.random.fold_in(key, 11)
    offset_now = jax.random.randint(jax.random.fold_in(base_key, 1), (), 0, 3)
    pattern = (jnp.arange(DEVICES, dtype=jnp.int32) + offset_now) % 3
    length_table = jnp.array([[FRAMES * S3, 0, 0], [FRAMES * S1, FRAMES * S2, 0], [FRAMES * S1, FRAMES * S1, FRAMES * S1]], jnp.int32)
    lengths = length_table[pattern]

    def one_device(device_key):
        splits = jax.random.split(device_key, 6)
        first = padded(tube_slots(splits[0], S3, K3, 0))
        second = padded(jnp.concatenate([tube_slots(splits[1], S1, K1, 0), tube_slots(splits[2], S2, K2, FRAMES * S1)]))
        third = padded(jnp.concatenate([tube_slots(splits[3], S1, K1, 0), tube_slots(splits[4], S1, K1, FRAMES * S1), tube_slots(splits[5], S1, K1, 2 * FRAMES * S1)]))
        return jnp.stack([first, second, third])
    options = jax.vmap(one_device)(jax.random.split(jax.random.fold_in(base_key, 2), DEVICES))
    chosen = jnp.take_along_axis(options, pattern[:, None, None], axis=1)[:, 0]
    return (lengths, chosen)


def draw_clip_lens(key, part):
    return layout_draw(key)[0]


def draw_vis_index(key, part):
    return layout_draw(key)[1]


def fill_params(key, pieces, total_length):
    scales = []
    offsets = []
    filled = 0
    for amount, deviation, middle in pieces:
        scales.append(jnp.full((amount,), deviation, jnp.float32))
        offsets.append(jnp.full((amount,), middle, jnp.float32))
        filled = filled + amount
    scales.append(jnp.full((total_length - filled,), 0.02, jnp.float32))
    offsets.append(jnp.zeros((total_length - filled,), jnp.float32))
    noise = jax.random.normal(key, (total_length,), jnp.float32)
    return jnp.concatenate(offsets) + jnp.concatenate(scales) * noise


def draw_params_enc(key, part):
    pieces = [(PIX * D, PIX ** (-0.5), 0.0), (D, 0.2, 0.0), (D, 0.1, 1.0), (D, 0.2, 0.0), (3 * D * D, D ** (-0.5), 0.0), (D, 0.2, 0.0), (D, 0.2, 0.0), (D * D, 2.0 * D ** (-0.5), 0.0), (D, 0.2, 0.0), (D, 0.1, 1.0), (D, 0.2, 0.0), (D * FF, D ** (-0.5), 0.0), (FF, 0.2, 0.0), (FF * D, FF ** (-0.5), 0.0), (D, 0.2, 0.0), (D, 0.1, 1.0), (D, 0.2, 0.0), (D * DD, D ** (-0.5), 0.0)]
    return fill_params(jax.random.fold_in(key, 21), pieces, PE)


def draw_params_dec(key, part):
    pieces = [(DD, 0.3, 0.0), (DD, 0.1, 1.0), (DD, 0.2, 0.0), (3 * DD * DD, DD ** (-0.5), 0.0), (DD, 0.2, 0.0), (DD, 0.2, 0.0), (DD * DD, 2.0 * DD ** (-0.5), 0.0), (DD, 0.2, 0.0), (DD, 0.1, 1.0), (DD, 0.2, 0.0), (DD * DFF, DD ** (-0.5), 0.0), (DFF, 0.2, 0.0), (DFF * DD, DFF ** (-0.5), 0.0), (DD, 0.2, 0.0), (DD, 0.1, 1.0), (DD, 0.2, 0.0), (DD * PIX, DD ** (-0.5), 0.0), (PIX, 0.2, 0.0)]
    return fill_params(jax.random.fold_in(key, 22), pieces, PD)


def block_levels(key, dims, cuts, smallest, largest):
    def one(dim, shards_of):
        heights = jax.random.uniform(jax.random.fold_in(jax.random.fold_in(key, 6), dim), (shards_of,), jnp.float32, smallest / len(cuts), largest / len(cuts))
        return jnp.repeat(jnp.exp(heights), dims[dim] // shards_of).reshape((-1,) + (1,) * (len(dims) - dim - 1))

    factor_of = one(*cuts[0])
    for cut in cuts[1:]:
        factor_of = factor_of * one(*cut)
    return factor_of


def bell_draw(stream_key, shape, scale, most, cuts=(), kind=jnp.bfloat16):
    values = jax.random.normal(stream_key, shape, jnp.float32) * scale
    if len(cuts) > 0:
        values = block_levels(stream_key, shape, cuts, -0.22, 0.18) * values
    return jnp.clip(values, min=-most, max=most).astype(kind)


def setup_inputs(seed: int = 0) -> dict:
    streams_of = jax.random.split(jax.random.key(seed), 11)
    return {
        "vis_pixels": bell_draw(streams_of[0], (DEVICES * VIS_DEV, PIX), 1.0, 6.0, ((0, 32),)),
        "target": bell_draw(streams_of[1], (DEVICES * TOK_DEV, PIX), 1.0, 6.0, ((0, 32),)),
        "clip_lens": draw_clip_lens(jax.random.fold_in(streams_of[10], 71), 0),
        "vis_index": draw_vis_index(jax.random.fold_in(streams_of[10], 71), 0),
        "params_enc": draw_params_enc(jax.random.fold_in(streams_of[10], 71), 0),
        "m_enc": bell_draw(streams_of[5], (PE,), (0.0056 * (PE + PD) ** -0.5), 2.6702880859375e-05, ((0, 8),), jnp.float32),
        "v_enc": jnp.clip(jnp.exp(math.log(4.811463727438792e-11) - 1.3855342 * jax.random.uniform(streams_of[6], (PE,), jnp.float32) ** block_levels(streams_of[6], (PE,), ((0, 8),), -0.2, 0.2)), 1.2037806515485805e-11, 4.811463727438792e-11),
        "params_dec": draw_params_dec(jax.random.fold_in(streams_of[10], 71), 0),
        "m_dec": bell_draw(streams_of[8], (PD,), (0.0056 * (PE + PD) ** -0.5), 2.6702880859375e-05, ((0, 8),), jnp.float32),
        "v_dec": jnp.clip(jnp.exp(math.log(4.811463727438792e-11) - 1.3855342 * jax.random.uniform(streams_of[9], (PD,), jnp.float32) ** block_levels(streams_of[9], (PD,), ((0, 8),), -0.2, 0.2)), 1.2037806515485805e-11, 4.811463727438792e-11),
    }


learn_rate = 0.05
BETA_ONE = 0.9
BETA_TWO = 0.95
EPSILON = 1e-08
weight_decay = 0.05
clip_norm = 0.05

@jax.custom_vjp
def low(v):
    return lax.optimization_barrier(v.astype(jnp.bfloat16)).astype(jnp.float32)

@jax.custom_vjp
def low_back(v):
    return v

def low_keep(v):
    return (low(v), None)

def low_pass(kept, grad):
    return (grad,)

def back_keep(v):
    return (v, None)

def back_low(kept, grad):
    return (low(grad),)
low.defvjp(low_keep, low_pass)
low_back.defvjp(back_keep, back_low)

def product(left, right):
    return jnp.dot(left, right, precision=lax.Precision.HIGHEST)

def product_sum(form, left, right):
    return jnp.einsum(form, left, right, precision=lax.Precision.HIGHEST)

def unpack(vector, extents):
    pieces = []
    offset = 0
    for extent in extents:
        length = math.prod(extent)
        pieces.append(vector[offset:offset + length].reshape(extent))
        offset = offset + length
    return pieces

def encoder_shapes():
    return [(PIX, D), (D,), (D,), (D,), (D, 3 * D), (D,), (D,), (D, D), (D,), (D,), (D,), (D, FF), (FF,), (FF, D), (D,), (D,), (D,), (D, DD)]

def decoder_shapes():
    return [(DD,), (DD,), (DD,), (DD, 3 * DD), (DD,), (DD,), (DD, DD), (DD,), (DD,), (DD,), (DD, DFF), (DFF,), (DFF, DD), (DD,), (DD,), (DD,), (DD, PIX), (PIX,)]

def layer_norm(stream, scale_vec, offset_vec):
    center = stream - lax.optimization_barrier(jnp.mean(stream, axis=-1, keepdims=True))
    spread = lax.optimization_barrier(jnp.mean(center * center, axis=-1, keepdims=True))
    return center * lax.rsqrt(spread + 1e-06) * scale_vec + offset_vec

def sinusoid(places, columns):
    half_width = columns // 2
    frequency = jnp.exp(jnp.arange(half_width, dtype=jnp.float32) * (-math.log(10000.0) / half_width))
    angles = places[:, None] * frequency[None, :]
    return jnp.concatenate([jnp.sin(angles), jnp.cos(angles)], axis=1)

def layout(lengths, visible, row_count):
    positions = jnp.arange(row_count, dtype=jnp.int32)
    clip_ends = jnp.cumsum(lengths).astype(jnp.int32)
    starts = clip_ends - lengths
    segment = lax.optimization_barrier(jnp.sum((positions[:, None] >= clip_ends[None, :]).astype(jnp.int32), axis=1))
    member = segment[:, None] == jnp.arange(3, dtype=jnp.int32)[None, :]
    clip_begin = lax.optimization_barrier(jnp.sum(jnp.where(member, starts[None, :], 0), axis=1)).astype(jnp.int32)
    clip_place = (positions - clip_begin).astype(jnp.float32)
    pack_total = clip_ends[2]
    slot_live = (visible < pack_total).astype(jnp.float32)
    shown_flag = jnp.zeros((row_count,), jnp.float32).at[visible].add(slot_live)
    counted = jnp.where(positions < pack_total, 1.0 - shown_flag, 0.0)
    return (segment, clip_place, slot_live, shown_flag, counted)

def attend(queries, key_rows, value_rows, labels_all, head_count, block_rows):
    row_count, columns = queries.shape
    head_size = columns // head_count
    block_count = row_count // block_rows
    queries = queries.reshape(block_count, block_rows, head_count, head_size)
    row_labels = labels_all.reshape(block_count, block_rows)
    key_rows = key_rows.reshape(-1, head_count, head_size)
    value_rows = value_rows.reshape(-1, head_count, head_size)

    def one_block(couple):
        query_block, labels = couple
        scores = product_sum('qhd,khd->hqk', query_block, key_rows) * (1.0 / math.sqrt(head_size))
        allowed = labels[None, :, None] == labels_all[None, None, :]
        scores = jnp.where(allowed, scores, -1e+30)
        highest = lax.optimization_barrier(jnp.max(scores, axis=-1, keepdims=True))
        soft_weights = jnp.exp(scores - highest)
        soft_weights = soft_weights / lax.optimization_barrier(jnp.sum(soft_weights, axis=-1, keepdims=True))
        mixture = product_sum('hqk,khd->qhd', low(soft_weights), value_rows)
        return mixture.reshape(block_rows, columns)
    return lax.map(jax.checkpoint(one_block), (queries, row_labels)).reshape(row_count, columns)

def transformer_block(stream, weights, segment, head_count, block_rows):
    columns = stream.shape[1]
    normed = layer_norm(stream, weights[0], weights[1])
    bias_row = jnp.concatenate([weights[3], jnp.zeros_like(weights[3]), weights[4]])
    packed = low_back(product(low(normed), weights[2]) + bias_row)
    queries = low(packed[:, :columns])
    key_rows = low(packed[:, columns:2 * columns])
    value_rows = low(packed[:, 2 * columns:])
    mixture = attend(queries, key_rows, value_rows, segment, head_count, block_rows)
    stream = stream + product(low(mixture), weights[5]) + weights[6]
    normed = layer_norm(stream, weights[7], weights[8])
    hidden = jax.nn.gelu(product(low(normed), weights[9]) + weights[10], approximate=False)
    return stream + product(low(hidden), weights[11]) + weights[12]

def pack_loss(enc_vector, dec_vector, pixels, targets, lengths, visible):
    row_count = targets.shape[0]
    slot_count = pixels.shape[0]
    segment, clip_place, slot_live, shown_flag, counted = layout(lengths, visible, row_count)
    encoder = unpack(enc_vector, encoder_shapes())
    decoder = unpack(dec_vector, decoder_shapes())
    tokens = product(low(pixels), encoder[0]) + encoder[1] + sinusoid(clip_place[visible], D)
    tokens = transformer_block(tokens, encoder[2:15], segment[visible], HEADS, slot_count)
    latent = product(low(layer_norm(tokens, encoder[15], encoder[16])), encoder[17])
    placed = jnp.zeros((row_count, DD), jnp.float32).at[visible].add(latent * slot_live[:, None])
    stream = placed + (1.0 - shown_flag)[:, None] * decoder[0][None, :] + sinusoid(clip_place, DD)
    stream = transformer_block(stream, decoder[1:14], segment, DHEADS, QB)
    predicted = product(low(layer_norm(stream, decoder[14], decoder[15])), decoder[16]) + decoder[17]
    center = targets - lax.optimization_barrier(jnp.mean(targets, axis=1, keepdims=True))
    goal_norm = center * lax.rsqrt(lax.optimization_barrier(jnp.mean(center * center, axis=1, keepdims=True)) + 1e-06)
    errors = lax.optimization_barrier(jnp.mean((predicted - goal_norm) ** 2, axis=1))
    return jnp.sum(errors * counted)

def adamw_update(master, gradient, moment_one, moment_two, clip_scale):
    gradient = gradient * clip_scale
    moment_one = BETA_ONE * moment_one + (1.0 - BETA_ONE) * gradient
    moment_two = BETA_TWO * moment_two + (1.0 - BETA_TWO) * gradient * gradient
    first_hat = moment_one / (1.0 - BETA_ONE ** STEP)
    second_hat = moment_two / (1.0 - BETA_TWO ** STEP)
    updated = master - learn_rate * (first_hat / (jnp.sqrt(second_hat) + EPSILON) + weight_decay * master)
    return (moment_one, moment_two, updated)

def reference(vis_pixels, target, clip_lens, vis_index, params_enc, m_enc, v_enc, params_dec, m_dec, v_dec):
    pixels = vis_pixels.astype(jnp.float32).reshape(DEVICES, VIS_DEV, PIX)
    targets = target.astype(jnp.float32).reshape(DEVICES, TOK_DEV, PIX)

    def count_pack(lengths, visible):
        return layout(lengths, visible, TOK_DEV)[4]
    masked_count = jnp.sum(jax.vmap(count_pack)(clip_lens, vis_index))

    def total_loss(enc_vector, dec_vector):
        enc_low = low(enc_vector)
        dec_low = low(dec_vector)
        checked = jax.checkpoint(pack_loss)

        def visit_pack(running, pack_data):
            return (running + checked(enc_low, dec_low, pack_data[0], pack_data[1], pack_data[2], pack_data[3]), None)
        summed, unused = lax.scan(visit_pack, jnp.zeros((), jnp.float32), (pixels, targets, clip_lens, vis_index))
        return summed
    loss_sum, pullback = jax.vjp(total_loss, params_enc, params_dec)
    grad_enc, grad_dec = pullback(1.0 / masked_count)
    squares = jnp.sum(grad_enc * grad_enc) + jnp.sum(grad_dec * grad_dec)
    grad_norm = jnp.sqrt(squares)
    clip_scale = jnp.minimum(1.0, clip_norm / (grad_norm + 1e-06))
    enc_one, enc_two, enc_new = adamw_update(params_enc, grad_enc, m_enc, v_enc, clip_scale)
    dec_one, dec_two, dec_new = adamw_update(params_dec, grad_dec, m_dec, v_dec, clip_scale)
    return (loss_sum, masked_count, grad_norm, enc_one, enc_two, enc_new, dec_one, dec_two, dec_new)
```

```python
import functools
import math

import jax
import jax.numpy as jnp
from jax import lax
from jax.experimental import pallas as pl
from jax.experimental.pallas import tpu as pltpu
from jax.sharding import PartitionSpec as P

D = 768
HEADS = 12
FF = 3072
DD = 384
DHEADS = 6
DFF = 1536
PIX = 1536
STEP = 10
ROWS = 2592

learn_rate = 0.05
BETA_ONE = 0.9
BETA_TWO = 0.95
EPSILON = 1e-08
weight_decay = 0.05
clip_norm = 0.05

F = jnp.float32
B = jnp.bfloat16
AXES = ("narrow", "wide")
NT = (((1,), (1,)), ((), ()))
NN = (((1,), (0,)), ((), ()))
TN = (((0,), (0,)), ((), ()))
VMEM_LIMIT = 60 << 20


def mm(left, right, dims=NN):
    return lax.dot_general(left, right, dims, preferred_element_type=F)


def plain_round(value):
    return lax.optimization_barrier(value.astype(B)).astype(F)


def round_value(value):
    rounding = jax.custom_vjp(plain_round)
    rounding.defvjp(lambda given: (plain_round(given), None), lambda kept, grad: (grad,))
    return rounding(value)


def round_grad(value):
    passing = jax.custom_vjp(lambda given: given)
    passing.defvjp(lambda given: (given, None), lambda kept, grad: (plain_round(grad),))
    return passing(value)


def product(left, right):
    return jnp.dot(left, right, preferred_element_type=F)


def product_sum(form, left, right):
    return jnp.einsum(form, left, right, preferred_element_type=F)


def unpack(vector, extents):
    pieces = []
    offset = 0
    for extent in extents:
        length = math.prod(extent)
        pieces.append(vector[offset : offset + length].reshape(extent))
        offset = offset + length
    return pieces


ENC_SHAPES = [
    (PIX, D), (D,), (D,), (D,), (D, 3 * D), (D,), (D,), (D, D), (D,), (D,), (D,),
    (D, FF), (FF,), (FF, D), (D,), (D,), (D,), (D, DD),
]
DEC_SHAPES = [
    (DD,), (DD,), (DD,), (DD, 3 * DD), (DD,), (DD,), (DD, DD), (DD,), (DD,), (DD,),
    (DD, DFF), (DFF,), (DFF, DD), (DD,), (DD,), (DD,), (DD, PIX), (PIX,),
]


def layer_norm(stream, scale_vec, offset_vec):
    center = stream - jnp.mean(stream, axis=-1, keepdims=True)
    spread = jnp.mean(center * center, axis=-1, keepdims=True)
    return center * lax.rsqrt(spread + 1e-06) * scale_vec + offset_vec


def sinusoid(places, columns):
    half_width = columns // 2
    frequency = jnp.exp(jnp.arange(half_width, dtype=F) * (-math.log(10000.0) / half_width))
    angles = places[:, None] * frequency[None, :]
    return jnp.concatenate([jnp.sin(angles), jnp.cos(angles)], axis=1)


def layout(lengths, visible, row_count):
    positions = jnp.arange(row_count, dtype=jnp.int32)
    clip_ends = jnp.cumsum(lengths)
    starts = clip_ends - lengths
    segment = jnp.sum((positions[:, None] >= clip_ends[None, :]).astype(jnp.int32), axis=1)
    member = segment[:, None] == jnp.arange(3, dtype=jnp.int32)[None, :]
    clip_begin = jnp.sum(jnp.where(member, starts[None, :], 0), axis=1)
    clip_place = (positions - clip_begin).astype(F)
    pack_total = clip_ends[2]
    slot_live = (visible < pack_total).astype(F)
    shown_flag = jnp.zeros((row_count,), F).at[visible].add(slot_live)
    counted = jnp.where(positions < pack_total, 1.0 - shown_flag, 0.0)
    return (segment, clip_place, slot_live, shown_flag, counted)


def slot_layout(lengths, visible):
    clip_ends = jnp.cumsum(lengths)
    starts = clip_ends - lengths
    segment = jnp.sum((visible[:, None] >= clip_ends[None, :]).astype(jnp.int32), axis=1)
    member = segment[:, None] == jnp.arange(3, dtype=jnp.int32)[None, :]
    clip_begin = jnp.sum(jnp.where(member, starts[None, :], 0), axis=1)
    return segment, (visible - clip_begin).astype(F)


def encode(encoder, pixels, segment, places):
    tokens = product(pixels.astype(F), encoder[0]) + encoder[1] + places
    weights = encoder[2:15]
    rows, columns = tokens.shape
    normed = layer_norm(tokens, weights[0], weights[1])
    bias_row = jnp.concatenate([weights[3], jnp.zeros_like(weights[3]), weights[4]])
    packed = round_grad(product(round_value(normed), weights[2]) + bias_row)
    queries, key_rows, value_rows = (
        round_value(packed[:, i * columns : (i + 1) * columns]).reshape(rows, HEADS, columns // HEADS)
        for i in range(3)
    )
    scores = product_sum("qhd,khd->hqk", queries, key_rows) * (1.0 / math.sqrt(columns // HEADS))
    allowed = segment[None, :, None] == segment[None, None, :]
    scores = jnp.where(allowed, scores, -1e30)
    soft = jnp.exp(scores - jnp.max(scores, axis=-1, keepdims=True))
    soft = soft / jnp.sum(soft, axis=-1, keepdims=True)
    mixture = product_sum("hqk,khd->qhd", round_value(soft), value_rows).reshape(rows, columns)
    tokens = tokens + product(round_value(mixture), weights[5]) + weights[6]
    normed = layer_norm(tokens, weights[7], weights[8])
    hidden = jax.nn.gelu(product(round_value(normed), weights[9]) + weights[10], approximate=False)
    tokens = tokens + product(round_value(hidden), weights[11]) + weights[12]
    return product(round_value(layer_norm(tokens, encoder[15], encoder[16])), encoder[17])


def norm_rows(x):
    center = x - jnp.mean(x, axis=1, keepdims=True)
    inverse = lax.rsqrt(jnp.mean(center * center, axis=1, keepdims=True) + 1e-06)
    return center * inverse, inverse


def norm_back(grad, hat, inverse):
    return inverse * (
        grad
        - jnp.mean(grad, axis=1, keepdims=True)
        - hat * jnp.mean(grad * hat, axis=1, keepdims=True)
    )


def total(x):
    return jnp.sum(x, axis=0, keepdims=True)


def qkv_kernel(x_ref, w_ref, vec_ref, o_ref):
    hat, inverse = norm_rows(x_ref[...])
    normed = (hat * vec_ref[0:1, :DD] + vec_ref[1:2, :DD]).astype(B)
    o_ref[...] = (mm(normed, w_ref[...]) + vec_ref[2:3, :]).astype(B)


def qkv_forward(x, w, vec, bm=432):
    full = lambda a: pl.BlockSpec(a.shape, lambda i: (0, 0))
    return pl.pallas_call(
        qkv_kernel,
        grid=(ROWS // bm,),
        in_specs=[pl.BlockSpec((bm, DD), lambda i: (i, 0)), full(w), full(vec)],
        out_specs=pl.BlockSpec((bm, 3 * DD), lambda i: (i, 0)),
        out_shape=jax.ShapeDtypeStruct((ROWS, 3 * DD), B),
        compiler_params=pltpu.CompilerParams(vmem_limit_bytes=VMEM_LIMIT),
        name="dec_qkv",
    )(x, w, vec)


def lanes_low(rows):
    return lax.broadcasted_iota(jnp.int32, (rows, 128), 1) < 64


def attend_kernel(q_ref, k_ref, v_ref, qf_ref, kf_ref, o_ref, lse_ref, k0, k1):
    rows, bq = k_ref.shape[0], q_ref.shape[0]

    @pl.when(pl.program_id(1) == 0)
    def _():
        low = lanes_low(rows)
        keys, marks = k_ref[...], kf_ref[...]
        k0[...] = jnp.where(low, keys, marks)
        k1[...] = jnp.where(low, marks, keys)

    low = lanes_low(bq)
    q, qf = q_ref[...] * jnp.asarray(0.125, B), qf_ref[...]
    outs, logs = [], []
    for h in range(2):
        s = mm(jnp.where(low, q, qf) if h == 0 else jnp.where(low, qf, q), (k0, k1)[h][...], NT)
        m = jnp.max(s, axis=1, keepdims=True)
        e = jnp.exp(s - m)
        l = jnp.sum(e, axis=1, keepdims=True)
        outs.append(mm((e * (1.0 / l)).astype(B), v_ref[...]))
        logs.append(m + jnp.log(l))
    o_ref[...] = jnp.where(low, outs[0], outs[1]).astype(B)
    lse_ref[0] = jnp.where(low, logs[0], logs[1])


def attend_forward(qkv, qf, kf, bq=432):
    return pl.pallas_call(
        attend_kernel,
        grid=(3, ROWS // bq),
        in_specs=[
            pl.BlockSpec((bq, 128), lambda h, i: (i, h)),
            pl.BlockSpec((ROWS, 128), lambda h, i: (0, 3 + h)),
            pl.BlockSpec((ROWS, 128), lambda h, i: (0, 6 + h)),
            pl.BlockSpec((bq, 128), lambda h, i: (i, 0)),
            pl.BlockSpec((ROWS, 128), lambda h, i: (0, 0)),
        ],
        out_specs=[
            pl.BlockSpec((bq, 128), lambda h, i: (i, h)),
            pl.BlockSpec((1, bq, 128), lambda h, i: (h, i, 0)),
        ],
        out_shape=[
            jax.ShapeDtypeStruct((ROWS, DD), B),
            jax.ShapeDtypeStruct((3, ROWS, 128), F),
        ],
        scratch_shapes=[pltpu.VMEM((ROWS, 128), B)] * 2,
        compiler_params=pltpu.CompilerParams(vmem_limit_bytes=VMEM_LIMIT),
        name="dec_attend",
    )(qkv, qkv, qkv, qf, kf)


def attend_back_kernel(
    kc, q_ref, k_ref, v_ref, qf_ref, kf_ref, da_ref, st_ref, dq_ref, dk_ref, dv_ref,
    k0, k1, z0, z1, dk_sum, dv_sum,
):
    rows, bq = k_ref.shape[0], q_ref.shape[0]
    step = pl.program_id(1)

    @pl.when(step == 0)
    def _():
        low = lanes_low(rows)
        keys, marks = k_ref[...], kf_ref[...]
        zero = jnp.zeros_like(keys)
        k0[...] = jnp.where(low, keys, marks)
        k1[...] = jnp.where(low, marks, keys)
        z0[...] = jnp.where(low, keys, zero)
        z1[...] = jnp.where(low, zero, keys)
        dk_sum[...] = jnp.zeros_like(dk_sum)
        dv_sum[...] = jnp.zeros_like(dv_sum)

    low = lanes_low(bq)
    q, qf, da = q_ref[...] * jnp.asarray(0.125, B), qf_ref[...], da_ref[...]
    zero = jnp.zeros_like(q)
    qs = (jnp.where(low, q, qf), jnp.where(low, qf, q))
    qz = (jnp.where(low, q, zero), jnp.where(low, zero, q))
    dz = (jnp.where(low, da, zero), jnp.where(low, zero, da))
    stats = st_ref[0]
    dq = jnp.zeros((bq, 128), F)
    for c in range(rows // kc):
        part = slice(c * kc, (c + 1) * kc)
        v = v_ref[part, :]
        for h in range(2):
            s = mm((k0, k1)[h][part, :], qs[h], NT)
            p = jnp.exp(s - stats[h : h + 1, :])
            dv_sum[part, :] += mm(p.astype(B), dz[h])
            dp = mm(v, dz[h], NT)
            ds = (p * (dp - stats[2 + h : 3 + h, :])).astype(B)
            dk_sum[part, :] += mm(ds, qz[h])
            dq += mm(ds, (z0, z1)[h][part, :], TN)
    dq_ref[...] = (dq * 0.125).astype(B)

    @pl.when(step == pl.num_programs(1) - 1)
    def _():
        dk_ref[...] = dk_sum[...].astype(B)
        dv_ref[...] = dv_sum[...].astype(B)


def attend_back(qkv, qf, kf, da, stats, bq=432, kc=864):
    nq = ROWS // bq
    return pl.pallas_call(
        functools.partial(attend_back_kernel, kc),
        grid=(3, nq),
        in_specs=[
            pl.BlockSpec((bq, 128), lambda h, i: (i, h)),
            pl.BlockSpec((ROWS, 128), lambda h, i: (0, 3 + h)),
            pl.BlockSpec((ROWS, 128), lambda h, i: (0, 6 + h)),
            pl.BlockSpec((bq, 128), lambda h, i: (i, 0)),
            pl.BlockSpec((ROWS, 128), lambda h, i: (0, 0)),
            pl.BlockSpec((bq, 128), lambda h, i: (i, h)),
            pl.BlockSpec((1, 8, bq), lambda h, i: (h * nq + i, 0, 0)),
        ],
        out_specs=[
            pl.BlockSpec((bq, 128), lambda h, i: (i, h)),
            pl.BlockSpec((ROWS, 128), lambda h, i: (0, h)),
            pl.BlockSpec((ROWS, 128), lambda h, i: (0, h)),
        ],
        out_shape=[jax.ShapeDtypeStruct((ROWS, DD), B)] * 3,
        scratch_shapes=[pltpu.VMEM((ROWS, 128), B)] * 4 + [pltpu.VMEM((ROWS, 128), F)] * 2,
        compiler_params=pltpu.CompilerParams(vmem_limit_bytes=VMEM_LIMIT),
        name="dec_attend_back",
    )(qkv, qkv, qkv, qf, kf, da, stats)


def mlp_kernel(
    x_ref, a_ref, t_ref, row_ref, wo_ref, wu_ref, wd_ref, wh_ref, vec_ref,
    da_ref, dx_ref, dd_ref, go_ref, gu_ref, gd_ref, gh_ref, gv_ref,
):
    @pl.when(pl.program_id(0) == 0)
    def _():
        for ref in (go_ref, gu_ref, gd_ref, gh_ref, gv_ref):
            ref[...] = jnp.zeros_like(ref)

    a = a_ref[...]
    x1 = x_ref[...] + mm(a, wo_ref[...]) + vec_ref[0:1, :DD]
    hat2, inv2 = norm_rows(x1)
    n2 = (hat2 * vec_ref[1:2, :DD] + vec_ref[2:3, :DD]).astype(B)
    h = mm(n2, wu_ref[...]) + vec_ref[3:4, :]
    cdf = 0.5 * (1.0 + lax.erf(h * (1.0 / math.sqrt(2.0))))
    u = (h * cdf).astype(B)
    slope = cdf + h * jnp.exp(-0.5 * h * h) * (1.0 / math.sqrt(2.0 * math.pi))
    x2 = x1 + mm(u, wd_ref[...]) + vec_ref[4:5, :DD]
    hatf, invf = norm_rows(x2)
    nf = (hatf * vec_ref[5:6, :DD] + vec_ref[6:7, :DD]).astype(B)
    pred = mm(nf, wh_ref[...]) + vec_ref[7:8, :]
    goal, unused = norm_rows(t_ref[...].astype(F))
    err = pred - goal
    gv_ref[8:9, :] += total(err * err * row_ref[:, 0:1])
    dpred = err * row_ref[:, 1:2]
    gv_ref[7:8, :] += total(dpred)
    dpred = dpred.astype(B)
    gh_ref[...] += mm(nf, dpred, TN)
    dnf = mm(dpred, wh_ref[...], NT)
    gv_ref[5:6, :DD] += total(dnf * hatf)
    gv_ref[6:7, :DD] += total(dnf)
    dx2 = norm_back(dnf * vec_ref[5:6, :DD], hatf, invf)
    gv_ref[4:5, :DD] += total(dx2)
    dx2b = dx2.astype(B)
    gd_ref[...] += mm(u, dx2b, TN)
    dh = mm(dx2b, wd_ref[...], NT) * slope
    gv_ref[3:4, :] += total(dh)
    dh = dh.astype(B)
    gu_ref[...] += mm(n2, dh, TN)
    dn2 = mm(dh, wu_ref[...], NT)
    gv_ref[1:2, :DD] += total(dn2 * hat2)
    gv_ref[2:3, :DD] += total(dn2)
    dx1 = dx2 + norm_back(dn2 * vec_ref[1:2, :DD], hat2, inv2)
    gv_ref[0:1, :DD] += total(dx1)
    dx_ref[...] = dx1
    dx1 = dx1.astype(B)
    go_ref[...] += mm(a, dx1, TN)
    da = mm(dx1, wo_ref[...], NT).astype(B)
    da_ref[...] = da
    head_of = lax.broadcasted_iota(jnp.int32, (DD, 128), 0) // 64
    pick = (head_of == lax.broadcasted_iota(jnp.int32, (DD, 128), 1)).astype(F)
    dd_ref[...] = lax.dot_general(
        da.astype(F) * a.astype(F), pick, NN, precision=lax.Precision.HIGHEST, preferred_element_type=F
    )


def mlp_both(x, a, target, rows, wo, wu, wd, wh, vec, bm=432):
    full = lambda shape: pl.BlockSpec(shape, lambda i: (0, 0))
    part = lambda width: pl.BlockSpec((bm, width), lambda i: (i, 0))
    sums = [wo.shape, wu.shape, wd.shape, wh.shape, vec.shape]
    return pl.pallas_call(
        mlp_kernel,
        grid=(ROWS // bm,),
        in_specs=[part(DD), part(DD), part(PIX), part(128)]
        + [full(w.shape) for w in (wo, wu, wd, wh, vec)],
        out_specs=[part(DD), part(DD), part(128)] + [full(s) for s in sums],
        out_shape=[
            jax.ShapeDtypeStruct((ROWS, DD), B),
            jax.ShapeDtypeStruct((ROWS, DD), F),
            jax.ShapeDtypeStruct((ROWS, 128), F),
        ]
        + [jax.ShapeDtypeStruct(s, F) for s in sums],
        compiler_params=pltpu.CompilerParams(vmem_limit_bytes=VMEM_LIMIT),
        name="dec_mlp",
    )(x, a, target, rows, wo, wu, wd, wh, vec)


def qkv_back_kernel(x_ref, dx_ref, dq_ref, dk_ref, dv_ref, row_ref, w_ref, vec_ref, o_ref, g_ref, gv_ref):
    @pl.when(pl.program_id(0) == 0)
    def _():
        for ref in (g_ref, gv_ref):
            ref[...] = jnp.zeros_like(ref)

    hat, inverse = norm_rows(x_ref[...])
    normed = (hat * vec_ref[0:1, :DD] + vec_ref[1:2, :DD]).astype(B)
    dn = jnp.zeros(hat.shape, F)
    for i, ref in enumerate((dq_ref, dk_ref, dv_ref)):
        part = slice(i * DD, (i + 1) * DD)
        dp = ref[...]
        g_ref[:, part] += mm(normed, dp, TN)
        dn += mm(dp, w_ref[:, part], NT)
        if i != 1:
            gv_ref[2:3, part] += total(dp.astype(F))
    gv_ref[0:1, :DD] += total(dn * hat)
    gv_ref[1:2, :DD] += total(dn)
    dx = dx_ref[...] + norm_back(dn * vec_ref[0:1, :DD], hat, inverse)
    o_ref[...] = dx
    gv_ref[3:4, :DD] += total(dx * row_ref[:, 2:3])


def qkv_back(x, dx, dq, dk, dv, rows, w, vec, bm=432):
    full = lambda shape: pl.BlockSpec(shape, lambda i: (0, 0))
    part = lambda width: pl.BlockSpec((bm, width), lambda i: (i, 0))
    return pl.pallas_call(
        qkv_back_kernel,
        grid=(ROWS // bm,),
        in_specs=[part(DD)] * 5 + [part(128), full(w.shape), full(vec.shape)],
        out_specs=[part(DD), full(w.shape), full(vec.shape)],
        out_shape=[
            jax.ShapeDtypeStruct((ROWS, DD), F),
            jax.ShapeDtypeStruct(w.shape, F),
            jax.ShapeDtypeStruct(vec.shape, F),
        ],
        compiler_params=pltpu.CompilerParams(vmem_limit_bytes=VMEM_LIMIT),
        name="dec_qkv_back",
    )(x, dx, dq, dk, dv, rows, w, vec)


def stack_rows(pieces, width, count=8):
    rows = [jnp.pad(p.astype(F), (0, width - p.shape[0])) for p in pieces]
    rows += [jnp.zeros((width,), F)] * (count - len(rows))
    return jnp.stack(rows)


class Links:
    def __init__(self, mesh):
        self.narrow, self.wide = mesh.shape["narrow"], mesh.shape["wide"]
        self.wide_bits = self.wide.bit_length() - 1
        self.narrow_bits = self.narrow.bit_length() - 1

    def bits(self):
        return [("wide", b) for b in reversed(range(self.wide_bits))] + [
            ("narrow", b) for b in reversed(range(self.narrow_bits))
        ]

    def mine(self, bit):
        return (lax.axis_index(bit[0]) >> bit[1]) & 1

    def swap(self, value, bit):
        mask = 1 << bit[1] if bit[0] == "wide" else self.wide << bit[1]
        pairs = [(i, i ^ mask) for i in range(self.narrow * self.wide)]
        return lax.ppermute(value, AXES, pairs)

    def add_all(self, value, bits):
        for bit in bits:
            value = value + self.swap(value, bit)
        return value

    def scatter_sum(self, value, axes, order):
        axes = list(axes)
        for bit in order:
            place = axes.index(bit)
            mine = self.mine(bit)
            away = lax.dynamic_index_in_dim(value, 1 - mine, place, keepdims=False)
            kept = lax.dynamic_index_in_dim(value, mine, place, keepdims=False)
            value = kept + self.swap(away, bit)
            axes.pop(place)
        return value

    def gather(self, value, axes, order):
        have = []
        for bit in order:
            other = self.swap(value, bit)
            low = self.mine(bit) == 0
            after = [b for b in axes if b in have or b == bit]
            place = after.index(bit)
            value = jnp.stack([jnp.where(low, value, other), jnp.where(low, other, value)], axis=place)
            have.append(bit)
        return value


def piece_rows(length, links):
    rows = -(-length // (128 * links.wide * links.narrow))
    return -(-rows // 32) * 32


def gather_params(shard, links):
    rows = piece_rows(shard.shape[0] * links.wide, links)
    flat = jnp.pad(shard.astype(B), (0, links.narrow * rows * 128 - shard.shape[0]))
    piece = lax.dynamic_index_in_dim(
        flat.reshape(links.narrow, rows, 128), lax.axis_index("narrow"), 0, keepdims=False
    )
    bits = links.bits()
    x, upper = ("wide", 0), [("wide", b) for b in reversed(range(1, links.wide_bits))]
    y, core = ("narrow", 1), ("narrow", 0)
    half = rows // 2
    one = links.gather(piece[:half], bits, upper + [x, y, core])
    two = links.gather(piece[half:], bits, upper + [y, x, core])
    both = jnp.concatenate([one, two], axis=-2).reshape(links.wide, links.narrow * rows * 128)
    return both[:, : shard.shape[0]].reshape(-1)


def scatter_grads(flat, links):
    rows = piece_rows(flat.shape[0], links)
    shard = flat.shape[0] // links.wide
    value = jnp.pad(flat.reshape(links.wide, shard), ((0, 0), (0, links.narrow * rows * 128 - shard)))
    value = value.reshape((2,) * (links.wide_bits + links.narrow_bits) + (rows, 128))
    bits = links.bits()
    x, upper = ("wide", 0), [("wide", b) for b in reversed(range(1, links.wide_bits))]
    y, core = ("narrow", 1), ("narrow", 0)
    half = rows // 2
    one = links.scatter_sum(value[..., :half, :], bits, [core, x, y] + upper)
    two = links.scatter_sum(value[..., half:, :], bits, [core, y, x] + upper)
    return jnp.concatenate([one, two])


def join_shard(piece, shard, links):
    axes = [("narrow", b) for b in reversed(range(links.narrow_bits))]
    whole = links.gather(piece, axes, [("narrow", 1), ("narrow", 0)])
    return whole.reshape(-1)[:shard]


def adamw_update(master, gradient, moment_one, moment_two, clip_scale):
    gradient = gradient * clip_scale
    moment_one = BETA_ONE * moment_one + (1.0 - BETA_ONE) * gradient
    moment_two = BETA_TWO * moment_two + (1.0 - BETA_TWO) * gradient * gradient
    first_hat = moment_one / (1.0 - BETA_ONE**STEP)
    second_hat = moment_two / (1.0 - BETA_TWO**STEP)
    updated = master - learn_rate * (
        first_hat / (jnp.sqrt(second_hat) + EPSILON) + weight_decay * master
    )
    return (moment_one, moment_two, updated)


def body(
    links, vis_pixels, target, clip_lens, vis_index, params_enc, m_enc, v_enc, params_dec, m_dec, v_dec
):
    lengths = clip_lens[0]
    visible = vis_index[0]
    segment, clip_place, slot_live, shown_flag, counted = layout(lengths, visible, target.shape[0])
    masked_count = links.add_all(jnp.sum(counted), links.bits())
    cotangent = 1.0 / masked_count
    segment, clip_place, shown_flag, counted = (
        v[:ROWS] for v in (segment, clip_place, shown_flag, counted)
    )
    rows = jnp.stack([counted, counted * (cotangent * (2.0 / PIX)), 1.0 - shown_flag], axis=1)
    rows = jnp.pad(rows, ((0, 0), (0, 125)))
    lane = jnp.arange(128, dtype=jnp.int32)[None, :] % 64
    mark = lane == segment[:, None]
    q_marks = mark.astype(B)
    k_marks = jnp.where(mark | (lane > 3), 0.0, -1e30).astype(B)

    enc_full = gather_params(params_enc, links)
    dec_full = gather_params(params_dec, links)
    encoder = [w.astype(F) for w in unpack(enc_full, ENC_SHAPES)]
    dec = unpack(dec_full, DEC_SHAPES)
    slot_segment, slot_place = slot_layout(lengths, visible)
    latent, pull = jax.vjp(
        lambda weights: encode(weights, vis_pixels, slot_segment, sinusoid(slot_place, D)), encoder
    )

    place_rows = jnp.where(visible < ROWS, visible, ROWS)
    placed = jnp.zeros((ROWS, DD), F).at[place_rows].add(latent * slot_live[:, None], mode="drop")
    x0 = placed + (1.0 - shown_flag)[:, None] * dec[0].astype(F)[None, :] + sinusoid(clip_place, DD)
    bias = jnp.concatenate([dec[4], jnp.zeros_like(dec[4]), dec[5]])
    vec_one = stack_rows([dec[1], dec[2], bias], 3 * DD)
    vec_two = stack_rows([dec[7], dec[8], dec[9], dec[11], dec[13], dec[14], dec[15], dec[17]], DFF, 16)
    qkv = qkv_forward(x0, dec[3], vec_one)
    a, lse = attend_forward(qkv, q_marks, k_marks)
    da, dx1, dd, g_out, g_up, g_down, g_head, g_two = mlp_both(
        x0, a, target, rows, dec[6], dec[10], dec[12], dec[16], vec_two
    )
    loss_sum = links.add_all(jnp.sum(g_two[8]) / PIX, links.bits())
    blocks = ROWS // 432
    lse = jnp.stack([lse[:, :, 0], lse[:, :, 64]], axis=1)
    dd = dd[:, :DHEADS].T.reshape(3, 2, ROWS)
    stats = jnp.concatenate([lse, dd, jnp.zeros((3, 4, ROWS), F)], axis=1)
    stats = stats.reshape(3, 8, blocks, 432).transpose(0, 2, 1, 3).reshape(3 * blocks, 8, 432)
    dq, dk, dv = attend_back(qkv, q_marks, k_marks, da, stats)
    dx0, g_qkv, g_one = qkv_back(x0, dx1, dq, dk, dv, rows, dec[3], vec_one)
    grad_dec = jnp.concatenate(
        [
            g_one[3, :DD], g_one[0, :DD], g_one[1, :DD], g_qkv.reshape(-1),
            g_one[2, :DD], g_one[2, 2 * DD :], g_out.reshape(-1), g_two[0, :DD],
            g_two[1, :DD], g_two[2, :DD], g_up.reshape(-1), g_two[3],
            g_down.reshape(-1), g_two[4, :DD], g_two[5, :DD], g_two[6, :DD],
            g_head.reshape(-1), g_two[7],
        ]
    )
    grad_dec = jnp.pad(grad_dec, (0, dec_full.shape[0] - grad_dec.shape[0]))
    piece_dec = scatter_grads(grad_dec, links)

    d_latent = dx0[jnp.minimum(visible, ROWS - 1)] * slot_live[:, None]
    grad_enc = jnp.concatenate([g.reshape(-1) for g in pull(d_latent)[0]])
    grad_enc = jnp.pad(grad_enc, (0, enc_full.shape[0] - grad_enc.shape[0]))
    piece_enc = scatter_grads(grad_enc, links)

    squares = jnp.sum(piece_enc * piece_enc) + jnp.sum(piece_dec * piece_dec)
    grad_norm = jnp.sqrt(links.add_all(squares, links.bits()))
    clip_scale = jnp.minimum(1.0, clip_norm / (grad_norm + 1e-06))
    grad_enc = join_shard(piece_enc, params_enc.shape[0], links)
    grad_dec = join_shard(piece_dec, params_dec.shape[0], links)
    enc_one, enc_two, enc_new = adamw_update(params_enc, grad_enc, m_enc, v_enc, clip_scale)
    dec_one, dec_two, dec_new = adamw_update(params_dec, grad_dec, m_dec, v_dec, clip_scale)
    return (loss_sum, masked_count, grad_norm, enc_one, enc_two, enc_new, dec_one, dec_two, dec_new)


def solution(mesh):
    placed = (P(AXES, None),) * 4 + (P("wide"),) * 6
    return jax.shard_map(
        functools.partial(body, Links(mesh)),
        mesh=mesh,
        in_specs=placed,
        out_specs=(P(), P(), P()) + (P("wide"),) * 6,
        check_vma=False,
    )
```

```python
import functools
import math

import jax
import jax.numpy as jnp
from jax import lax
from jax.experimental import pallas as pl
from jax.experimental.pallas import tpu as pltpu
from jax.sharding import PartitionSpec as P

D = 768
HEADS = 12
FF = 3072
DD = 384
DHEADS = 6
DFF = 1536
PIX = 1536
STEP = 10
ROWS = 2592

learn_rate = 0.05
BETA_ONE = 0.9
BETA_TWO = 0.95
EPSILON = 1e-08
weight_decay = 0.05
clip_norm = 0.05

F = jnp.float32
B = jnp.bfloat16
AXES = ("narrow", "wide")
NT = (((1,), (1,)), ((), ()))
NN = (((1,), (0,)), ((), ()))
TN = (((0,), (0,)), ((), ()))
VMEM_LIMIT = 60 << 20


def mm(left, right, dims=NN):
    return lax.dot_general(left, right, dims, preferred_element_type=F)


def plain_round(value):
    return lax.optimization_barrier(value.astype(B)).astype(F)


def round_value(value):
    rounding = jax.custom_vjp(plain_round)
    rounding.defvjp(lambda given: (plain_round(given), None), lambda kept, grad: (grad,))
    return rounding(value)


def round_grad(value):
    passing = jax.custom_vjp(lambda given: given)
    passing.defvjp(lambda given: (given, None), lambda kept, grad: (plain_round(grad),))
    return passing(value)


def product(left, right):
    return jnp.dot(left, right, preferred_element_type=F)


def product_sum(form, left, right):
    return jnp.einsum(form, left, right, preferred_element_type=F)


ENC_SHAPES = [
    (PIX, D), (D,), (D,), (D,), (D, 3 * D), (D,), (D,), (D, D), (D,), (D,), (D,),
    (D, FF), (FF,), (FF, D), (D,), (D,), (D,), (D, DD),
]
DEC_SHAPES = [
    (DD,), (DD,), (DD,), (DD, 3 * DD), (DD,), (DD,), (DD, DD), (DD,), (DD,), (DD,),
    (DD, DFF), (DFF,), (DFF, DD), (DD,), (DD,), (DD,), (DD, PIX), (PIX,),
]


def layer_norm(stream, scale_vec, offset_vec):
    center = stream - jnp.mean(stream, axis=-1, keepdims=True)
    spread = jnp.mean(center * center, axis=-1, keepdims=True)
    return center * lax.rsqrt(spread + 1e-06) * scale_vec + offset_vec


def sinusoid(places, columns):
    half_width = columns // 2
    frequency = jnp.exp(jnp.arange(half_width, dtype=F) * (-math.log(10000.0) / half_width))
    angles = places[:, None] * frequency[None, :]
    return jnp.concatenate([jnp.sin(angles), jnp.cos(angles)], axis=1)


def layout(lengths, visible, row_count):
    positions = jnp.arange(row_count, dtype=jnp.int32)
    clip_ends = jnp.cumsum(lengths)
    starts = clip_ends - lengths
    segment = jnp.sum((positions[:, None] >= clip_ends[None, :]).astype(jnp.int32), axis=1)
    member = segment[:, None] == jnp.arange(3, dtype=jnp.int32)[None, :]
    clip_begin = jnp.sum(jnp.where(member, starts[None, :], 0), axis=1)
    clip_place = (positions - clip_begin).astype(F)
    pack_total = clip_ends[2]
    slot_live = (visible < pack_total).astype(F)
    shown_flag = jnp.zeros((row_count,), F).at[visible].add(slot_live)
    counted = jnp.where(positions < pack_total, 1.0 - shown_flag, 0.0)
    return (segment, clip_place, slot_live, shown_flag, counted)


def slot_layout(lengths, visible):
    clip_ends = jnp.cumsum(lengths)
    starts = clip_ends - lengths
    segment = jnp.sum((visible[:, None] >= clip_ends[None, :]).astype(jnp.int32), axis=1)
    member = segment[:, None] == jnp.arange(3, dtype=jnp.int32)[None, :]
    clip_begin = jnp.sum(jnp.where(member, starts[None, :], 0), axis=1)
    return segment, (visible - clip_begin).astype(F)


def encode(encoder, pixels, segment, places):
    tokens = product(pixels.astype(F), encoder[0]) + encoder[1] + places
    weights = encoder[2:15]
    rows, columns = tokens.shape
    normed = layer_norm(tokens, weights[0], weights[1])
    bias_row = jnp.concatenate([weights[3], jnp.zeros_like(weights[3]), weights[4]])
    packed = round_grad(product(round_value(normed), weights[2]) + bias_row)
    queries, key_rows, value_rows = (
        round_value(packed[:, i * columns : (i + 1) * columns]).reshape(rows, HEADS, columns // HEADS)
        for i in range(3)
    )
    scores = product_sum("qhd,khd->hqk", queries, key_rows) * (1.0 / math.sqrt(columns // HEADS))
    allowed = segment[None, :, None] == segment[None, None, :]
    scores = jnp.where(allowed, scores, -1e30)
    soft = jnp.exp(scores - jnp.max(scores, axis=-1, keepdims=True))
    soft = soft / jnp.sum(soft, axis=-1, keepdims=True)
    mixture = product_sum("hqk,khd->qhd", round_value(soft), value_rows).reshape(rows, columns)
    tokens = tokens + product(round_value(mixture), weights[5]) + weights[6]
    normed = layer_norm(tokens, weights[7], weights[8])
    hidden = jax.nn.gelu(product(round_value(normed), weights[9]) + weights[10], approximate=False)
    tokens = tokens + product(round_value(hidden), weights[11]) + weights[12]
    return product(round_value(layer_norm(tokens, encoder[15], encoder[16])), encoder[17])


def norm_rows(x):
    center = x - jnp.mean(x, axis=1, keepdims=True)
    inverse = lax.rsqrt(jnp.mean(center * center, axis=1, keepdims=True) + 1e-06)
    return center * inverse, inverse


def norm_back(grad, hat, inverse):
    return inverse * (
        grad
        - jnp.mean(grad, axis=1, keepdims=True)
        - hat * jnp.mean(grad * hat, axis=1, keepdims=True)
    )


def total(x):
    return jnp.sum(x, axis=0, keepdims=True)


def qkv_kernel(x_ref, w_ref, vec_ref, o_ref):
    hat, inverse = norm_rows(x_ref[...])
    normed = (hat * vec_ref[0:1, :DD] + vec_ref[1:2, :DD]).astype(B)
    o_ref[...] = (mm(normed, w_ref[...]) + vec_ref[2:3, :]).astype(B)


def qkv_forward(x, w, vec, bm=432):
    full = lambda a: pl.BlockSpec(a.shape, lambda i: (0, 0))
    return pl.pallas_call(
        qkv_kernel,
        grid=(ROWS // bm,),
        in_specs=[pl.BlockSpec((bm, DD), lambda i: (i, 0)), full(w), full(vec)],
        out_specs=pl.BlockSpec((bm, 3 * DD), lambda i: (i, 0)),
        out_shape=jax.ShapeDtypeStruct((ROWS, 3 * DD), B),
        compiler_params=pltpu.CompilerParams(vmem_limit_bytes=VMEM_LIMIT),
        name="dec_qkv",
    )(x, w, vec)


def lanes_low(rows):
    return lax.broadcasted_iota(jnp.int32, (rows, 128), 1) < 64


def attend_kernel(q_ref, k_ref, v_ref, qf_ref, kf_ref, o_ref, lse_ref, k0, k1):
    rows, bq = k_ref.shape[0], q_ref.shape[0]

    @pl.when(pl.program_id(1) == 0)
    def _():
        low = lanes_low(rows)
        keys, marks = k_ref[...], kf_ref[...]
        k0[...] = jnp.where(low, keys, marks)
        k1[...] = jnp.where(low, marks, keys)

    low = lanes_low(bq)
    q, qf = q_ref[...] * jnp.asarray(0.125, B), qf_ref[...]
    outs, logs = [], []
    for h in range(2):
        s = mm(jnp.where(low, q, qf) if h == 0 else jnp.where(low, qf, q), (k0, k1)[h][...], NT)
        m = jnp.max(s, axis=1, keepdims=True)
        e = jnp.exp(s - m)
        l = jnp.sum(e, axis=1, keepdims=True)
        outs.append(mm((e * (1.0 / l)).astype(B), v_ref[...]))
        logs.append(m + jnp.log(l))
    o_ref[...] = jnp.where(low, outs[0], outs[1]).astype(B)
    lse_ref[0] = jnp.where(low, logs[0], logs[1])


def attend_forward(qkv, qf, kf, bq=432):
    return pl.pallas_call(
        attend_kernel,
        grid=(3, ROWS // bq),
        in_specs=[
            pl.BlockSpec((bq, 128), lambda h, i: (i, h)),
            pl.BlockSpec((ROWS, 128), lambda h, i: (0, 3 + h)),
            pl.BlockSpec((ROWS, 128), lambda h, i: (0, 6 + h)),
            pl.BlockSpec((bq, 128), lambda h, i: (i, 0)),
            pl.BlockSpec((ROWS, 128), lambda h, i: (0, 0)),
        ],
        out_specs=[
            pl.BlockSpec((bq, 128), lambda h, i: (i, h)),
            pl.BlockSpec((1, bq, 128), lambda h, i: (h, i, 0)),
        ],
        out_shape=[
            jax.ShapeDtypeStruct((ROWS, DD), B),
            jax.ShapeDtypeStruct((3, ROWS, 128), F),
        ],
        scratch_shapes=[pltpu.VMEM((ROWS, 128), B)] * 2,
        compiler_params=pltpu.CompilerParams(vmem_limit_bytes=VMEM_LIMIT),
        name="dec_attend",
    )(qkv, qkv, qkv, qf, kf)


def attend_back_kernel(
    kc, q_ref, k_ref, v_ref, qf_ref, kf_ref, da_ref, st_ref, dq_ref, dk_ref, dv_ref,
    k0, k1, z0, z1, dk_sum, dv_sum,
):
    rows, bq = k_ref.shape[0], q_ref.shape[0]
    step = pl.program_id(1)

    @pl.when(step == 0)
    def _():
        low = lanes_low(rows)
        keys, marks = k_ref[...], kf_ref[...]
        zero = jnp.zeros_like(keys)
        k0[...] = jnp.where(low, keys, marks)
        k1[...] = jnp.where(low, marks, keys)
        z0[...] = jnp.where(low, keys, zero)
        z1[...] = jnp.where(low, zero, keys)
        dk_sum[...] = jnp.zeros_like(dk_sum)
        dv_sum[...] = jnp.zeros_like(dv_sum)

    low = lanes_low(bq)
    q, qf, da = q_ref[...] * jnp.asarray(0.125, B), qf_ref[...], da_ref[...]
    zero = jnp.zeros_like(q)
    qs = (jnp.where(low, q, qf), jnp.where(low, qf, q))
    qz = (jnp.where(low, q, zero), jnp.where(low, zero, q))
    dz = (jnp.where(low, da, zero), jnp.where(low, zero, da))
    stats = st_ref[0]
    dq = jnp.zeros((bq, 128), F)
    for c in range(rows // kc):
        part = slice(c * kc, (c + 1) * kc)
        v = v_ref[part, :]
        for h in range(2):
            s = mm((k0, k1)[h][part, :], qs[h], NT)
            p = jnp.exp(s - stats[h : h + 1, :])
            dv_sum[part, :] += mm(p.astype(B), dz[h])
            dp = mm(v, dz[h], NT)
            ds = (p * (dp - stats[2 + h : 3 + h, :])).astype(B)
            dk_sum[part, :] += mm(ds, qz[h])
            dq += mm(ds, (z0, z1)[h][part, :], TN)
    dq_ref[...] = (dq * 0.125).astype(B)

    @pl.when(step == pl.num_programs(1) - 1)
    def _():
        dk_ref[...] = dk_sum[...].astype(B)
        dv_ref[...] = dv_sum[...].astype(B)


def attend_back(qkv, qf, kf, da, stats, bq=432, kc=864):
    nq = ROWS // bq
    return pl.pallas_call(
        functools.partial(attend_back_kernel, kc),
        grid=(3, nq),
        in_specs=[
            pl.BlockSpec((bq, 128), lambda h, i: (i, h)),
            pl.BlockSpec((ROWS, 128), lambda h, i: (0, 3 + h)),
            pl.BlockSpec((ROWS, 128), lambda h, i: (0, 6 + h)),
            pl.BlockSpec((bq, 128), lambda h, i: (i, 0)),
            pl.BlockSpec((ROWS, 128), lambda h, i: (0, 0)),
            pl.BlockSpec((bq, 128), lambda h, i: (i, h)),
            pl.BlockSpec((1, 8, bq), lambda h, i: (h * nq + i, 0, 0)),
        ],
        out_specs=[
            pl.BlockSpec((bq, 128), lambda h, i: (i, h)),
            pl.BlockSpec((ROWS, 128), lambda h, i: (0, h)),
            pl.BlockSpec((ROWS, 128), lambda h, i: (0, h)),
        ],
        out_shape=[jax.ShapeDtypeStruct((ROWS, DD), B)] * 3,
        scratch_shapes=[pltpu.VMEM((ROWS, 128), B)] * 4 + [pltpu.VMEM((ROWS, 128), F)] * 2,
        compiler_params=pltpu.CompilerParams(vmem_limit_bytes=VMEM_LIMIT),
        name="dec_attend_back",
    )(qkv, qkv, qkv, qf, kf, da, stats)


def mlp_kernel(
    x_ref, a_ref, t_ref, row_ref, wo_ref, wu_ref, wd_ref, wh_ref, vec_ref,
    da_ref, dx_ref, dd_ref, go_ref, gu_ref, gd_ref, gh_ref, gv_ref,
):
    @pl.when(pl.program_id(0) == 0)
    def _():
        for ref in (go_ref, gu_ref, gd_ref, gh_ref, gv_ref):
            ref[...] = jnp.zeros_like(ref)

    a = a_ref[...]
    x1 = x_ref[...] + mm(a, wo_ref[...]) + vec_ref[0:1, :DD]
    hat2, inv2 = norm_rows(x1)
    n2 = (hat2 * vec_ref[1:2, :DD] + vec_ref[2:3, :DD]).astype(B)
    h = mm(n2, wu_ref[...]) + vec_ref[3:4, :]
    cdf = 0.5 * (1.0 + lax.erf(h * (1.0 / math.sqrt(2.0))))
    u = (h * cdf).astype(B)
    slope = cdf + h * jnp.exp(-0.5 * h * h) * (1.0 / math.sqrt(2.0 * math.pi))
    x2 = x1 + mm(u, wd_ref[...]) + vec_ref[4:5, :DD]
    hatf, invf = norm_rows(x2)
    nf = (hatf * vec_ref[5:6, :DD] + vec_ref[6:7, :DD]).astype(B)
    pred = mm(nf, wh_ref[...]) + vec_ref[7:8, :]
    goal, unused = norm_rows(t_ref[...].astype(F))
    err = pred - goal
    gv_ref[8:9, :] += total(err * err * row_ref[:, 0:1])
    dpred = err * row_ref[:, 1:2]
    gv_ref[7:8, :] += total(dpred)
    dpred = dpred.astype(B)
    gh_ref[...] += mm(nf, dpred, TN)
    dnf = mm(dpred, wh_ref[...], NT)
    gv_ref[5:6, :DD] += total(dnf * hatf)
    gv_ref[6:7, :DD] += total(dnf)
    dx2 = norm_back(dnf * vec_ref[5:6, :DD], hatf, invf)
    gv_ref[4:5, :DD] += total(dx2)
    dx2b = dx2.astype(B)
    gd_ref[...] += mm(u, dx2b, TN)
    dh = mm(dx2b, wd_ref[...], NT) * slope
    gv_ref[3:4, :] += total(dh)
    dh = dh.astype(B)
    gu_ref[...] += mm(n2, dh, TN)
    dn2 = mm(dh, wu_ref[...], NT)
    gv_ref[1:2, :DD] += total(dn2 * hat2)
    gv_ref[2:3, :DD] += total(dn2)
    dx1 = dx2 + norm_back(dn2 * vec_ref[1:2, :DD], hat2, inv2)
    gv_ref[0:1, :DD] += total(dx1)
    dx_ref[...] = dx1
    dx1 = dx1.astype(B)
    go_ref[...] += mm(a, dx1, TN)
    da = mm(dx1, wo_ref[...], NT).astype(B)
    da_ref[...] = da
    head_of = lax.broadcasted_iota(jnp.int32, (DD, 128), 0) // 64
    pick = (head_of == lax.broadcasted_iota(jnp.int32, (DD, 128), 1)).astype(F)
    dd_ref[...] = lax.dot_general(
        da.astype(F) * a.astype(F), pick, NN, precision=lax.Precision.HIGHEST, preferred_element_type=F
    )


def mlp_both(x, a, target, rows, wo, wu, wd, wh, vec, bm=432):
    full = lambda shape: pl.BlockSpec(shape, lambda i: (0, 0))
    part = lambda width: pl.BlockSpec((bm, width), lambda i: (i, 0))
    sums = [wo.shape, wu.shape, wd.shape, wh.shape, vec.shape]
    return pl.pallas_call(
        mlp_kernel,
        grid=(ROWS // bm,),
        in_specs=[part(DD), part(DD), part(PIX), part(128)]
        + [full(w.shape) for w in (wo, wu, wd, wh, vec)],
        out_specs=[part(DD), part(DD), part(128)] + [full(s) for s in sums],
        out_shape=[
            jax.ShapeDtypeStruct((ROWS, DD), B),
            jax.ShapeDtypeStruct((ROWS, DD), F),
            jax.ShapeDtypeStruct((ROWS, 128), F),
        ]
        + [jax.ShapeDtypeStruct(s, F) for s in sums],
        compiler_params=pltpu.CompilerParams(vmem_limit_bytes=VMEM_LIMIT),
        name="dec_mlp",
    )(x, a, target, rows, wo, wu, wd, wh, vec)


def qkv_back_kernel(x_ref, dx_ref, dq_ref, dk_ref, dv_ref, row_ref, w_ref, vec_ref, o_ref, g_ref, gv_ref):
    @pl.when(pl.program_id(0) == 0)
    def _():
        for ref in (g_ref, gv_ref):
            ref[...] = jnp.zeros_like(ref)

    hat, inverse = norm_rows(x_ref[...])
    normed = (hat * vec_ref[0:1, :DD] + vec_ref[1:2, :DD]).astype(B)
    dn = jnp.zeros(hat.shape, F)
    for i, ref in enumerate((dq_ref, dk_ref, dv_ref)):
        part = slice(i * DD, (i + 1) * DD)
        dp = ref[...]
        g_ref[:, part] += mm(normed, dp, TN)
        dn += mm(dp, w_ref[:, part], NT)
        if i != 1:
            gv_ref[2:3, part] += total(dp.astype(F))
    gv_ref[0:1, :DD] += total(dn * hat)
    gv_ref[1:2, :DD] += total(dn)
    dx = dx_ref[...] + norm_back(dn * vec_ref[0:1, :DD], hat, inverse)
    o_ref[...] = dx
    gv_ref[3:4, :DD] += total(dx * row_ref[:, 2:3])


def qkv_back(x, dx, dq, dk, dv, rows, w, vec, bm=432):
    full = lambda shape: pl.BlockSpec(shape, lambda i: (0, 0))
    part = lambda width: pl.BlockSpec((bm, width), lambda i: (i, 0))
    return pl.pallas_call(
        qkv_back_kernel,
        grid=(ROWS // bm,),
        in_specs=[part(DD)] * 5 + [part(128), full(w.shape), full(vec.shape)],
        out_specs=[part(DD), full(w.shape), full(vec.shape)],
        out_shape=[
            jax.ShapeDtypeStruct((ROWS, DD), F),
            jax.ShapeDtypeStruct(w.shape, F),
            jax.ShapeDtypeStruct(vec.shape, F),
        ],
        compiler_params=pltpu.CompilerParams(vmem_limit_bytes=VMEM_LIMIT),
        name="dec_qkv_back",
    )(x, dx, dq, dk, dv, rows, w, vec)


def stack_rows(pieces, width, count=8):
    rows = [jnp.pad(p.astype(F), (0, width - p.shape[0])) for p in pieces]
    rows += [jnp.zeros((width,), F)] * (count - len(rows))
    return jnp.stack(rows)


def table(shapes):
    out, row = [], 0
    for s in shapes:
        m, c = (s[0], s[1] // 128) if len(s) == 2 else (1, s[0] // 128)
        out.append((row, m, c))
        row += m * c
    return out

def job_rows(m, c, most=2304):
    return max(n for n in range(16, m + 1, 16) if m % n == 0 and n * c % 16 == 0 and n * c <= most)

def unpack_kernel(pieces, width, flat, *refs):
    mats = [p for p in pieces if p[1] > 1]
    outs, vec_ref = refs[: len(mats)], refs[len(mats)]
    buf, lin, in_sem, out_sem = refs[len(mats) + 1 : len(mats) + 5]
    stages = refs[len(mats) + 5 :]
    vbuf = buf
    vec_ref[...] = jnp.zeros_like(vec_ref)
    v = 0
    for row, m, c in pieces:
        if m > 1:
            continue
        start = row // 16 * 16
        size = -(-(row - start + c) // 16) * 16
        copy = pltpu.make_async_copy(flat.at[pl.ds(start, size)], buf.at[0, pl.ds(0, size)], in_sem.at[0])
        copy.start()
        copy.wait()
        lin[pl.ds(0, size), :] = buf[0, pl.ds(0, size), :].astype(F)
        for j in range(c):
            vec_ref[v : v + 1, j * 128 : (j + 1) * 128] = lin[pl.ds(row - start + j, 1), :]
        v += 1
    for k, (row, m, c) in enumerate(mats):
        n = job_rows(m, c)
        size = n * c
        start = row // 16 * 16
        delta = row - start
        reach = -(-(delta + size) // 16) * 16
        jobs = m // n
        stage, out = stages[k], outs[k]

        def load(j, slot):
            at = pl.multiple_of(start + j * size, 16)
            return pltpu.make_async_copy(flat.at[pl.ds(at, reach)], buf.at[slot, pl.ds(0, reach)], in_sem.at[slot])

        def store(j, slot):
            return pltpu.make_async_copy(stage.at[slot], out.at[pl.ds(pl.multiple_of(j * n, 16), n)], out_sem.at[slot])

        load(0, 0).start()

        def job(j, carry):
            slot = lax.rem(j, 2)

            @pl.when(j + 1 < jobs)
            def _():
                load(j + 1, 1 - slot).start()

            load(j, slot).wait()
            lin[pl.ds(0, reach), :] = buf[slot, pl.ds(0, reach), :].astype(F)

            @pl.when(j >= 2)
            def _():
                store(j - 2, slot).wait()

            for i in range(c):
                stage[slot, :, i * 128 : (i + 1) * 128] = lin[pl.ds(delta + i, n, stride=c), :].astype(B)
            store(j, slot).start()
            return carry

        lax.fori_loop(0, jobs, job, 0)
        for j in range(max(jobs - 2, 0), jobs):
            store(j, j % 2).wait()

def unpack_flat(flat, shapes, name):
    pieces = table(shapes)
    mats = [s for s in shapes if len(s) == 2]
    vectors = [s for s in shapes if len(s) == 1]
    width = max(s[0] for s in vectors)
    count = -(-len(vectors) // 8) * 8
    hbm = pl.BlockSpec(memory_space=pl.ANY)
    stages = [pltpu.VMEM((2, job_rows(s[0], s[1] // 128), s[1]), B) for s in mats]
    return pl.pallas_call(
        functools.partial(unpack_kernel, pieces, width),
        in_specs=[hbm],
        out_specs=[hbm] * len(mats) + [pl.BlockSpec(memory_space=pltpu.VMEM)],
        out_shape=[jax.ShapeDtypeStruct(s, B) for s in mats] + [jax.ShapeDtypeStruct((count, width), F)],
        scratch_shapes=[
            pltpu.VMEM((2, 2336, 128), B), pltpu.VMEM((2336, 128), F),
            pltpu.SemaphoreType.DMA((2,)), pltpu.SemaphoreType.DMA((2,)),
        ] + stages,
        compiler_params=pltpu.CompilerParams(vmem_limit_bytes=VMEM_LIMIT),
        name=name,
    )(flat)

def pack_kernel(pieces, shard, padded, wide, core_ref, *refs):
    mats = [p for p in pieces if p[1] > 1]
    ins, vec_ref = refs[: len(mats)], refs[len(mats)]
    kept, away, top_ref = refs[len(mats) + 1 : len(mats) + 4]
    lin, turn, in_sem, out_sem = refs[len(mats) + 4 : len(mats) + 8]
    stages = refs[len(mats) + 8 :]
    end = pieces[-1][0] + pieces[-1][1] * pieces[-1][2]
    lin[pl.ds(end, lin.shape[0] - end), :] = jnp.zeros((lin.shape[0] - end, 128), F)
    top_ref[...] = jnp.zeros_like(top_ref)
    top = jnp.max(jnp.abs(vec_ref[...]), axis=0, keepdims=True)
    for j in range(vec_ref.shape[1] // 128):
        top_ref[0:1, :] = jnp.maximum(top_ref[0:1, :], top[:, j * 128 : (j + 1) * 128])
    v = 0
    for row, m, c in pieces:
        if m == 1:
            for j in range(c):
                lin[pl.ds(row + j, 1), :] = vec_ref[v : v + 1, j * 128 : (j + 1) * 128]
            v += 1
    for k, (row, m, c) in enumerate(mats):
        n = job_rows(m, c)
        size = n * c
        jobs = m // n
        stage, source = stages[k], ins[k]

        def load(j, slot):
            return pltpu.make_async_copy(source.at[pl.ds(pl.multiple_of(j * n, 8), n)], stage.at[slot], in_sem.at[slot])

        load(0, 0).start()

        def job(j, carry):
            slot = lax.rem(j, 2)

            @pl.when(j + 1 < jobs)
            def _():
                load(j + 1, 1 - slot).start()

            load(j, slot).wait()
            most = top_ref[...]
            for i in range(c):
                value = stage[slot, :, i * 128 : (i + 1) * 128]
                most = jnp.maximum(most, jnp.max(jnp.abs(value).reshape(-1, 8, 128), axis=0))
                lin[pl.ds(row + i + j * size, n, stride=c), :] = value
            top_ref[...] = most
            return carry

        lax.fori_loop(0, jobs, job, 0)

    half = padded // 2
    core = core_ref[0]

    def sends(source, s, low, high):
        return [
            pltpu.make_async_copy(source.at[pl.ds(0, half)], low.at[s], out_sem.at[s % 2, 0]),
            pltpu.make_async_copy(source.at[pl.ds(half, half)], high.at[s], out_sem.at[s % 2, 1]),
        ]

    def source_of(s):
        at = s * shard
        return lin.at[pl.ds(at, padded)] if at % 8 == 0 else turn.at[s % 2]

    def run(s, act):
        @pl.when(core == 0)
        def _():
            for copy in sends(source_of(s), s, kept, away):
                act(copy)

        @pl.when(core == 1)
        def _():
            for copy in sends(source_of(s), s, away, kept):
                act(copy)

    for s in range(wide):
        if s >= 2:
            run(s - 2, lambda copy: copy.wait())
        if s * shard % 8:
            turn[s % 2] = lin[pl.ds(s * shard, padded), :]
        run(s, lambda copy: copy.start())
    for s in range(max(wide - 2, 0), wide):
        run(s, lambda copy: copy.wait())

def pack_grads(mats, vectors, shapes, total_rows, core, wide, padded, name):
    pieces = table(shapes)
    shard = total_rows // wide
    hbm = pl.BlockSpec(memory_space=pl.ANY)
    vmem = pl.BlockSpec(memory_space=pltpu.VMEM)
    length = -(-((wide - 1) * shard + padded) // 8) * 8
    stages = [pltpu.VMEM((2, job_rows(m.shape[0], m.shape[1] // 128), m.shape[1]), F) for m in mats]
    out = jax.ShapeDtypeStruct((wide, padded // 2, 128), F)
    kept, away, top = pl.pallas_call(
        functools.partial(pack_kernel, pieces, shard, padded, wide),
        in_specs=[pl.BlockSpec(memory_space=pltpu.SMEM)] + [hbm] * len(mats) + [vmem],
        out_specs=[hbm, hbm, vmem],
        out_shape=[out, out, jax.ShapeDtypeStruct((8, 128), F)],
        scratch_shapes=[
            pltpu.VMEM((length, 128), F), pltpu.VMEM((2, padded, 128), F),
            pltpu.SemaphoreType.DMA((2,)), pltpu.SemaphoreType.DMA((2, 2)),
        ] + stages,
        compiler_params=pltpu.CompilerParams(vmem_limit_bytes=VMEM_LIMIT),
        name=name,
    )(core, *mats, vectors)
    return kept, away, jnp.max(top)


class Links:
    def __init__(self, mesh):
        self.narrow, self.wide = mesh.shape["narrow"], mesh.shape["wide"]
        self.wide_bits = self.wide.bit_length() - 1
        self.narrow_bits = self.narrow.bit_length() - 1

    def bits(self):
        return [("wide", b) for b in reversed(range(self.wide_bits))] + [
            ("narrow", b) for b in reversed(range(self.narrow_bits))
        ]

    def mine(self, bit):
        return (lax.axis_index(bit[0]) >> bit[1]) & 1

    def swap(self, value, bit):
        mask = 1 << bit[1] if bit[0] == "wide" else self.wide << bit[1]
        pairs = [(i, i ^ mask) for i in range(self.narrow * self.wide)]
        return lax.ppermute(value, AXES, pairs)

    def add_all(self, value):
        for bit in self.bits():
            value = value + self.swap(value, bit)
        return value

    def max_all(self, value):
        for bit in self.bits():
            value = jnp.maximum(value, self.swap(value, bit))
        return value

    def scatter_sum(self, kept, other, axes, order, scale):
        axes = list(axes)
        for bit in order:
            place = axes.index(bit)
            mine = self.mine(bit)
            take = lambda value, index: lax.dynamic_index_in_dim(value, index, place, keepdims=False)
            away = ((take(kept, 1 - mine) + take(other, 1 - mine)) * scale).astype(jnp.float16)
            kept = take(kept, mine) + take(other, mine)
            other = self.swap(away, bit).astype(F) * (1.0 / scale)
            axes.pop(place)
        return kept + other

    def scale(self, top):
        count = self.narrow * self.wide
        return 32768.0 / (count * jnp.maximum(self.max_all(top), 1e-30))

    def gather(self, value, axes, order):
        have = []
        for bit in order:
            other = self.swap(value, bit)
            low = self.mine(bit) == 0
            after = [b for b in axes if b in have or b == bit]
            place = after.index(bit)
            value = jnp.stack([jnp.where(low, value, other), jnp.where(low, other, value)], axis=place)
            have.append(bit)
        return value


def piece_rows(length, links):
    rows = -(-length // (128 * links.wide * links.narrow))
    return -(-rows // 32) * 32


def gather_params(shard, links):
    rows = piece_rows(shard.shape[0] * links.wide, links)
    flat = jnp.pad(shard.astype(B), (0, links.narrow * rows * 128 - shard.shape[0]))
    piece = lax.dynamic_index_in_dim(
        flat.reshape(links.narrow, rows, 128), lax.axis_index("narrow"), 0, keepdims=False
    )
    bits = links.bits()
    x, upper = ("wide", 0), [("wide", b) for b in reversed(range(1, links.wide_bits))]
    y, core = ("narrow", 1), ("narrow", 0)
    half = rows // 2
    one = links.gather(piece[:half], bits, upper + [x, y, core])
    two = links.gather(piece[half:], bits, upper + [y, x, core])
    both = jnp.concatenate([one, two], axis=-2).reshape(links.wide, links.narrow * rows, 128)
    return both[:, : shard.shape[0] // 128].reshape(-1, 128)


def scatter_grads(kept, away, scale, links):
    rows = kept.shape[1] // 2
    y, core = ("narrow", 1), ("narrow", 0)
    x, upper = ("wide", 0), [("wide", b) for b in reversed(range(1, links.wide_bits))]
    axes = links.bits()[: links.wide_bits] + [y]
    shape = (2,) * len(axes) + (rows, 128)
    kept, other = kept.reshape(shape), links.swap(away, core).reshape(shape)
    half = rows // 2
    one = links.scatter_sum(kept[..., :half, :], other[..., :half, :], axes, [x, y] + upper, scale)
    two = links.scatter_sum(kept[..., half:, :], other[..., half:, :], axes, [y, x] + upper, scale)
    return jnp.concatenate([one, two])


def piece_squares(piece, shard_rows, links):
    rows = piece.shape[0]
    part = links.mine(("narrow", 0)) * 2 + links.mine(("narrow", 1))
    inside = part * rows + jnp.arange(rows, dtype=jnp.int32)[:, None] < shard_rows
    return jnp.sum(jnp.where(inside, piece * piece, 0.0))


def join_shard(piece, shard, links):
    axes = [("narrow", 0), ("narrow", 1)]
    return links.gather(piece, axes, [("narrow", 1), ("narrow", 0)]).reshape(-1)[:shard]


def adamw_update(master, gradient, moment_one, moment_two, clip_scale):
    gradient = gradient * clip_scale
    moment_one = BETA_ONE * moment_one + (1.0 - BETA_ONE) * gradient
    moment_two = BETA_TWO * moment_two + (1.0 - BETA_TWO) * gradient * gradient
    first_hat = moment_one / (1.0 - BETA_ONE**STEP)
    second_hat = moment_two / (1.0 - BETA_TWO**STEP)
    updated = master - learn_rate * (
        first_hat / (jnp.sqrt(second_hat) + EPSILON) + weight_decay * master
    )
    return (moment_one, moment_two, updated)


def body(
    links, vis_pixels, target, clip_lens, vis_index, params_enc, m_enc, v_enc, params_dec, m_dec, v_dec
):
    lengths = clip_lens[0]
    visible = vis_index[0]
    segment, clip_place, slot_live, shown_flag, counted = layout(lengths, visible, target.shape[0])
    masked_count = links.add_all(jnp.sum(counted))
    cotangent = 1.0 / masked_count
    segment, clip_place, shown_flag, counted = (
        v[:ROWS] for v in (segment, clip_place, shown_flag, counted)
    )
    rows = jnp.stack([counted, counted * (cotangent * (2.0 / PIX)), 1.0 - shown_flag], axis=1)
    rows = jnp.pad(rows, ((0, 0), (0, 125)))
    lane = jnp.arange(128, dtype=jnp.int32)[None, :] % 64
    mark = lane == segment[:, None]
    q_marks = mark.astype(B)
    k_marks = jnp.where(mark | (lane > 3), 0.0, -1e30).astype(B)

    *enc_mats, enc_vec = unpack_flat(gather_params(params_enc, links), ENC_SHAPES, "unpack_enc")
    *dec_mats, dec_vec = unpack_flat(gather_params(params_dec, links), DEC_SHAPES, "unpack_dec")
    w_qkv, w_out, w_up, w_down, w_head = dec_mats
    encoder, mats, vecs = [], list(enc_mats), [enc_vec[i] for i in range(12)]
    for extent in ENC_SHAPES:
        encoder.append(mats.pop(0).astype(F) if len(extent) == 2 else vecs.pop(0)[: extent[0]])
    slot_segment, slot_place = slot_layout(lengths, visible)
    latent, pull = jax.vjp(
        lambda weights: encode(weights, vis_pixels, slot_segment, sinusoid(slot_place, D)), encoder
    )

    place_rows = jnp.where(visible < ROWS, visible, ROWS)
    placed = jnp.zeros((ROWS, DD), F).at[place_rows].add(latent * slot_live[:, None], mode="drop")
    x0 = placed + (1.0 - shown_flag)[:, None] * dec_vec[0:1, :DD] + sinusoid(clip_place, DD)
    bias = jnp.concatenate([dec_vec[3, :DD], jnp.zeros((DD,), F), dec_vec[4, :DD]])
    vec_one = stack_rows([dec_vec[1, :DD], dec_vec[2, :DD], bias], 3 * DD)
    vec_two = jnp.concatenate([dec_vec[5:13], jnp.zeros((8, DFF), F)])
    qkv = qkv_forward(x0, w_qkv, vec_one)
    a, lse = attend_forward(qkv, q_marks, k_marks)
    da, dx1, dd, g_out, g_up, g_down, g_head, g_two = mlp_both(
        x0, a, target, rows, w_out, w_up, w_down, w_head, vec_two
    )
    loss_sum = links.add_all(jnp.sum(g_two[8]) / PIX)
    blocks = ROWS // 432
    lse = jnp.stack([lse[:, :, 0], lse[:, :, 64]], axis=1)
    dd = dd[:, :DHEADS].T.reshape(3, 2, ROWS)
    stats = jnp.concatenate([lse, dd, jnp.zeros((3, 4, ROWS), F)], axis=1)
    stats = stats.reshape(3, 8, blocks, 432).transpose(0, 2, 1, 3).reshape(3 * blocks, 8, 432)
    dq, dk, dv = attend_back(qkv, q_marks, k_marks, da, stats)
    dx0, g_qkv, g_one = qkv_back(x0, dx1, dq, dk, dv, rows, w_qkv, vec_one)
    core = (lax.axis_index("narrow") & 1).astype(jnp.int32).reshape(1)
    one_vec = jnp.stack(
        [g_one[3, :DD], g_one[0, :DD], g_one[1, :DD], g_one[2, :DD], g_one[2, 2 * DD :]]
    )
    dec_grads = jnp.concatenate([jnp.pad(one_vec, ((0, 0), (0, DFF - DD))), g_two[:8], jnp.zeros((3, DFF), F)])
    dec_rows, enc_rows = (v.shape[0] * links.wide // 128 for v in (params_dec, params_enc))
    dec_kept, dec_away, dec_top = pack_grads(
        [g_qkv, g_out, g_up, g_down, g_head], dec_grads, DEC_SHAPES, dec_rows, core, links.wide,
        links.narrow * piece_rows(dec_rows * 128, links), "pack_dec",
    )
    dec_scale = links.scale(dec_top)
    piece_dec = scatter_grads(dec_kept, dec_away, dec_scale, links)

    d_latent = dx0[jnp.minimum(visible, ROWS - 1)] * slot_live[:, None]
    grads = pull(d_latent)[0]
    enc_grads = stack_rows([g for g in grads if g.ndim == 1], FF, 16)
    enc_kept, enc_away, enc_top = pack_grads(
        [g for g in grads if g.ndim == 2], enc_grads, ENC_SHAPES, enc_rows, core, links.wide,
        links.narrow * piece_rows(enc_rows * 128, links), "pack_enc",
    )
    piece_enc = scatter_grads(enc_kept, enc_away, links.scale(enc_top), links)

    squares = piece_squares(piece_enc, enc_rows // links.wide, links)
    squares = squares + piece_squares(piece_dec, dec_rows // links.wide, links)
    grad_norm = jnp.sqrt(links.add_all(squares))
    clip_scale = jnp.minimum(1.0, clip_norm / (grad_norm + 1e-06))
    grad_enc = join_shard(piece_enc, params_enc.shape[0], links)
    grad_dec = join_shard(piece_dec, params_dec.shape[0], links)
    enc_one, enc_two, enc_new = adamw_update(params_enc, grad_enc, m_enc, v_enc, clip_scale)
    dec_one, dec_two, dec_new = adamw_update(params_dec, grad_dec, m_dec, v_dec, clip_scale)
    return (loss_sum, masked_count, grad_norm, enc_one, enc_two, enc_new, dec_one, dec_two, dec_new)


def solution(mesh):
    placed = (P(AXES, None),) * 4 + (P("wide"),) * 6
    return jax.shard_map(
        functools.partial(body, Links(mesh)),
        mesh=mesh,
        in_specs=placed,
        out_specs=(P(), P(), P()) + (P("wide"),) * 6,
        check_vma=False,
    )
```

```python
import functools
import math

import jax
import jax.numpy as jnp
from jax import lax
from jax.experimental import pallas as pl
from jax.experimental.pallas import tpu as pltpu
from jax.sharding import PartitionSpec as P

D = 768
HEADS = 12
FF = 3072
DD = 384
DHEADS = 6
DFF = 1536
PIX = 1536
STEP = 10
ROWS = 2592

learn_rate = 0.05
BETA_ONE = 0.9
BETA_TWO = 0.95
EPSILON = 1e-08
weight_decay = 0.05
clip_norm = 0.05

F = jnp.float32
B = jnp.bfloat16
AXES = ("narrow", "wide")
NT = (((1,), (1,)), ((), ()))
NN = (((1,), (0,)), ((), ()))
TN = (((0,), (0,)), ((), ()))
VMEM_LIMIT = 60 << 20


def mm(left, right, dims=NN):
    return lax.dot_general(left, right, dims, preferred_element_type=F)


ENC_SHAPES = [
    (PIX, D), (D,), (D,), (D,), (D, 3 * D), (D,), (D,), (D, D), (D,), (D,), (D,),
    (D, FF), (FF,), (FF, D), (D,), (D,), (D,), (D, DD),
]
DEC_SHAPES = [
    (DD,), (DD,), (DD,), (DD, 3 * DD), (DD,), (DD,), (DD, DD), (DD,), (DD,), (DD,),
    (DD, DFF), (DFF,), (DFF, DD), (DD,), (DD,), (DD,), (DD, PIX), (PIX,),
]


def sinusoid(places, columns):
    half_width = columns // 2
    frequency = jnp.exp(jnp.arange(half_width, dtype=F) * (-math.log(10000.0) / half_width))
    angles = places[:, None] * frequency[None, :]
    return jnp.concatenate([jnp.sin(angles), jnp.cos(angles)], axis=1)


def layout(lengths, visible, row_count):
    positions = jnp.arange(row_count, dtype=jnp.int32)
    clip_ends = jnp.cumsum(lengths)
    starts = clip_ends - lengths
    segment = jnp.sum((positions[:, None] >= clip_ends[None, :]).astype(jnp.int32), axis=1)
    member = segment[:, None] == jnp.arange(3, dtype=jnp.int32)[None, :]
    clip_begin = jnp.sum(jnp.where(member, starts[None, :], 0), axis=1)
    clip_place = (positions - clip_begin).astype(F)
    pack_total = clip_ends[2]
    slot_live = (visible < pack_total).astype(F)
    shown_flag = jnp.zeros((row_count,), F).at[visible].add(slot_live)
    counted = jnp.where(positions < pack_total, 1.0 - shown_flag, 0.0)
    return (segment, clip_place, slot_live, shown_flag, counted)


def slot_layout(lengths, visible):
    clip_ends = jnp.cumsum(lengths)
    starts = clip_ends - lengths
    segment = jnp.sum((visible[:, None] >= clip_ends[None, :]).astype(jnp.int32), axis=1)
    member = segment[:, None] == jnp.arange(3, dtype=jnp.int32)[None, :]
    clip_begin = jnp.sum(jnp.where(member, starts[None, :], 0), axis=1)
    return segment, (visible - clip_begin).astype(F)


def norm_rows(x):
    center = x - jnp.mean(x, axis=1, keepdims=True)
    inverse = lax.rsqrt(jnp.mean(center * center, axis=1, keepdims=True) + 1e-06)
    return center * inverse, inverse


def norm_back(grad, hat, inverse):
    return inverse * (
        grad
        - jnp.mean(grad, axis=1, keepdims=True)
        - hat * jnp.mean(grad * hat, axis=1, keepdims=True)
    )


def total(x):
    return jnp.sum(x, axis=0, keepdims=True)


def low_lanes(rows):
    return lax.broadcasted_iota(jnp.int32, (rows, 128), 1) < 64


def low_rows(columns):
    return lax.broadcasted_iota(jnp.int32, (128, columns), 0) < 64


def halves(low, value, other):
    return jnp.where(low, value, other), jnp.where(low, other, value)


def softmax_keys(s):
    m = jnp.max(s, axis=0, keepdims=True)
    e = jnp.exp(s - m)
    l = jnp.sum(e, axis=0, keepdims=True)
    return e * (1.0 / l), m + jnp.log(l)


def qkv_kernel(vis_ref, live_ref, latent_ref, place_ref, row_ref, w_ref, vec_ref, mask_ref, x_ref, o_ref):
    x_ref[...] = place_ref[...] + row_ref[:, 2:3] * mask_ref[0:1, :DD]

    def add_slot(i, carry):
        at = pl.ds(jnp.minimum(vis_ref[i], ROWS - 1), 1)
        x_ref[at, :] += latent_ref[pl.ds(i, 1), :] * live_ref[i]
        return carry

    lax.fori_loop(0, latent_ref.shape[0], add_slot, 0, unroll=8)
    bm = 432

    def block(i, carry):
        part = pl.ds(pl.multiple_of(i * bm, 16), bm)
        hat, inverse = norm_rows(x_ref[part, :])
        normed = (hat * vec_ref[0:1, :DD] + vec_ref[1:2, :DD]).astype(B)
        o_ref[part, :] = (mm(normed, w_ref[...]) + vec_ref[2:3, :]).astype(B)
        return carry

    lax.fori_loop(0, ROWS // bm, block, 0)


def qkv_forward(visible, live, latent, places, rows, w, vec, mask):
    smem, vmem = pl.BlockSpec(memory_space=pltpu.SMEM), pl.BlockSpec(memory_space=pltpu.VMEM)
    return pl.pallas_call(
        qkv_kernel,
        in_specs=[smem] * 2 + [vmem] * 6,
        out_specs=[vmem] * 2,
        out_shape=[jax.ShapeDtypeStruct((ROWS, DD), F), jax.ShapeDtypeStruct((ROWS, 3 * DD), B)],
        compiler_params=pltpu.CompilerParams(vmem_limit_bytes=VMEM_LIMIT),
        cost_estimate=pl.CostEstimate(flops=10 * 10**9, bytes_accessed=16 << 20, transcendentals=0),
        name="dec_qkv",
    )(visible, live, latent, places, rows, w, vec, mask)


def attend_kernel(q_ref, k_ref, v_ref, qf_ref, kf_ref, o_ref, lse_ref, k0, k1):
    rows, bq = k_ref.shape[0], q_ref.shape[0]

    @pl.when(pl.program_id(1) == 0)
    def _():
        k0[...], k1[...] = halves(low_lanes(rows), k_ref[...], kf_ref[...])

    qs = halves(low_lanes(bq), q_ref[...] * jnp.asarray(0.125, B), qf_ref[...])
    scores = [mm(keys[...], q, NT) for keys, q in zip((k0, k1), qs)]
    outs, logs = [], []
    for s in scores:
        p, log = softmax_keys(s)
        outs.append(mm(v_ref[...], p.astype(B), TN))
        logs.append(log)
    o_ref[...] = jnp.where(low_rows(bq), outs[0], outs[1]).T.astype(B)
    lse_ref[0] = jnp.concatenate(logs + [jnp.zeros((6, bq), F)], axis=0)


def attend_forward(qkv, qf, kf, bq=864):
    nq = ROWS // bq
    return pl.pallas_call(
        attend_kernel,
        grid=(3, nq),
        in_specs=[
            pl.BlockSpec((bq, 128), lambda h, i: (i, h)),
            pl.BlockSpec((ROWS, 128), lambda h, i: (0, 3 + h)),
            pl.BlockSpec((ROWS, 128), lambda h, i: (0, 6 + h)),
            pl.BlockSpec((bq, 128), lambda h, i: (i, 0)),
            pl.BlockSpec((ROWS, 128), lambda h, i: (0, 0)),
        ],
        out_specs=[
            pl.BlockSpec((bq, 128), lambda h, i: (i, h)),
            pl.BlockSpec((1, 8, bq), lambda h, i: (h * nq + i, 0, 0)),
        ],
        out_shape=[
            jax.ShapeDtypeStruct((ROWS, DD), B),
            jax.ShapeDtypeStruct((3 * nq, 8, bq), F),
        ],
        scratch_shapes=[pltpu.VMEM((ROWS, 128), B)] * 2,
        compiler_params=pltpu.CompilerParams(vmem_limit_bytes=VMEM_LIMIT),
        cost_estimate=pl.CostEstimate(flops=60 * 10**9, bytes_accessed=16 << 20, transcendentals=0),
        name="dec_attend",
    )(qkv, qkv, qkv, qf, kf)


def attend_back_kernel(
    h, kc, q_ref, k_ref, v_ref, qf_ref, kf_ref, da_ref, lse_ref, dd_ref, dq_ref, dk_ref, dv_ref,
    k0, k1, z0, z1, dk_sum, dv_sum,
):
    rows, bq = k_ref.shape[0], q_ref.shape[0]
    step = pl.program_id(0)

    @pl.when(step == 0)
    def _():
        low, keys = low_lanes(rows), k_ref[...]
        k0[...], k1[...] = halves(low, keys, kf_ref[...])
        z0[...], z1[...] = halves(low, keys, jnp.zeros_like(keys))
        dk_sum[...] = jnp.zeros_like(dk_sum)
        dv_sum[...] = jnp.zeros_like(dv_sum)

    low = low_lanes(bq)
    q, da = q_ref[...] * jnp.asarray(0.125, B), da_ref[...]
    zero = jnp.zeros_like(q)
    qs = halves(low, q, qf_ref[...])
    dz = halves(low, da, zero)
    q_both, d_both = jnp.concatenate(halves(low, q, zero), axis=0), jnp.concatenate(dz, axis=0)
    mean = jnp.concatenate([dd_ref[i] for i in range(dd_ref.shape[0])], axis=1)
    dq = jnp.zeros((128, bq), F)
    for c in range(rows // kc):
        part = slice(c * kc, (c + 1) * kc)
        scores = [mm(keys[part, :], q, NT) for keys, q in zip((k0, k1), qs)]
        dps = [mm(v_ref[part, :], d, NT) for d in dz]
        ps, dss = [], []
        for i in range(2):
            p = jnp.exp(scores[i] - lse_ref[0, i : i + 1, :])
            ps.append(p.astype(B))
            dss.append((p * (dps[i] - mean[2 * h + i : 2 * h + i + 1, :])).astype(B))
        dv_sum[part, :] += mm(jnp.concatenate(ps, axis=1), d_both)
        dk_sum[part, :] += mm(jnp.concatenate(dss, axis=1), q_both)
        for z, ds in zip((z0, z1), dss):
            dq += mm(z[part, :], ds, TN)
    dq_ref[...] = (dq.T * 0.125).astype(B)

    @pl.when(step == pl.num_programs(0) - 1)
    def _():
        dk_ref[...] = dk_sum[...].astype(B)
        dv_ref[...] = dv_sum[...].astype(B)


def attend_back(qkv, qf, kf, da, lse, dd, h, bq=864, kc=864):
    nq = ROWS // bq
    many = bq // dd.shape[2]
    return pl.pallas_call(
        functools.partial(attend_back_kernel, h, kc),
        grid=(nq,),
        in_specs=[
            pl.BlockSpec((bq, 128), lambda i: (i, h)),
            pl.BlockSpec((ROWS, 128), lambda i: (0, 3 + h)),
            pl.BlockSpec((ROWS, 128), lambda i: (0, 6 + h)),
            pl.BlockSpec((bq, 128), lambda i: (i, 0)),
            pl.BlockSpec((ROWS, 128), lambda i: (0, 0)),
            pl.BlockSpec((bq, 128), lambda i: (i, h)),
            pl.BlockSpec((1, 8, bq), lambda i: (h * nq + i, 0, 0)),
            pl.BlockSpec((many, 8, bq // many), lambda i: (i, 0, 0)),
        ],
        out_specs=[
            pl.BlockSpec((bq, 128), lambda i: (i, 0)),
            pl.BlockSpec((ROWS, 128), lambda i: (0, 0)),
            pl.BlockSpec((ROWS, 128), lambda i: (0, 0)),
        ],
        out_shape=[jax.ShapeDtypeStruct((ROWS, 128), B)] * 3,
        scratch_shapes=[pltpu.VMEM((ROWS, 128), B)] * 4 + [pltpu.VMEM((ROWS, 128), F)] * 2,
        compiler_params=pltpu.CompilerParams(vmem_limit_bytes=VMEM_LIMIT),
        cost_estimate=pl.CostEstimate(flops=40 * 10**9, bytes_accessed=8 << 20, transcendentals=0),
        name="dec_attend_back",
    )(qkv, qkv, qkv, qf, kf, da, lse, dd)


def mlp_kernel(
    x_ref, a_ref, t_ref, row_ref, wo_ref, wu_ref, wd_ref, wh_ref, vec_ref,
    da_ref, dx_ref, dd_ref, go_ref, gu_ref, gd_ref, gh_ref, gv_ref,
):
    @pl.when(pl.program_id(0) == 0)
    def _():
        for ref in (go_ref, gu_ref, gd_ref, gh_ref, gv_ref):
            ref[...] = jnp.zeros_like(ref)

    a = a_ref[...]
    x1 = x_ref[...] + mm(a, wo_ref[...]) + vec_ref[0:1, :DD]
    hat2, inv2 = norm_rows(x1)
    n2 = (hat2 * vec_ref[1:2, :DD] + vec_ref[2:3, :DD]).astype(B)
    h = mm(n2, wu_ref[...]) + vec_ref[3:4, :]
    cdf = 0.5 * (1.0 + lax.erf(h * (1.0 / math.sqrt(2.0))))
    u = (h * cdf).astype(B)
    slope = cdf + h * jnp.exp(-0.5 * h * h) * (1.0 / math.sqrt(2.0 * math.pi))
    x2 = x1 + mm(u, wd_ref[...]) + vec_ref[4:5, :DD]
    hatf, invf = norm_rows(x2)
    nf = (hatf * vec_ref[5:6, :DD] + vec_ref[6:7, :DD]).astype(B)
    pred = mm(nf, wh_ref[...]) + vec_ref[7:8, :]
    goal, unused = norm_rows(t_ref[...].astype(F))
    err = pred - goal
    gv_ref[8:9, :] += total(err * err * row_ref[:, 0:1])
    dpred = err * row_ref[:, 1:2]
    gv_ref[7:8, :] += total(dpred)
    dpred = dpred.astype(B)
    gh_ref[...] += mm(nf, dpred, TN)
    dnf = mm(dpred, wh_ref[...], NT)
    gv_ref[5:6, :DD] += total(dnf * hatf)
    gv_ref[6:7, :DD] += total(dnf)
    dx2 = norm_back(dnf * vec_ref[5:6, :DD], hatf, invf)
    gv_ref[4:5, :DD] += total(dx2)
    dx2b = dx2.astype(B)
    gd_ref[...] += mm(u, dx2b, TN)
    dh = mm(dx2b, wd_ref[...], NT) * slope
    gv_ref[3:4, :] += total(dh)
    dh = dh.astype(B)
    gu_ref[...] += mm(n2, dh, TN)
    dn2 = mm(dh, wu_ref[...], NT)
    gv_ref[1:2, :DD] += total(dn2 * hat2)
    gv_ref[2:3, :DD] += total(dn2)
    dx1 = dx2 + norm_back(dn2 * vec_ref[1:2, :DD], hat2, inv2)
    gv_ref[0:1, :DD] += total(dx1)
    dx_ref[...] = dx1
    dx1 = dx1.astype(B)
    go_ref[...] += mm(a, dx1, TN)
    da = mm(dx1, wo_ref[...], NT).astype(B)
    da_ref[...] = da
    head_of = lax.broadcasted_iota(jnp.int32, (8, DD), 1) // 64
    pick = (head_of == lax.broadcasted_iota(jnp.int32, (8, DD), 0)).astype(F)
    dd_ref[0] = lax.dot_general(
        pick, da.astype(F) * a.astype(F), NT, precision=lax.Precision.HIGHEST, preferred_element_type=F
    )


def mlp_both(x, a, target, rows, wo, wu, wd, wh, vec, bm=432):
    full = lambda shape: pl.BlockSpec(shape, lambda i: (0, 0))
    part = lambda width: pl.BlockSpec((bm, width), lambda i: (i, 0))
    sums = [wo.shape, wu.shape, wd.shape, wh.shape, vec.shape]
    return pl.pallas_call(
        mlp_kernel,
        grid=(ROWS // bm,),
        in_specs=[part(DD), part(DD), part(PIX), part(128)]
        + [full(w.shape) for w in (wo, wu, wd, wh, vec)],
        out_specs=[part(DD), part(DD), pl.BlockSpec((1, 8, bm), lambda i: (i, 0, 0))] + [full(s) for s in sums],
        out_shape=[
            jax.ShapeDtypeStruct((ROWS, DD), B),
            jax.ShapeDtypeStruct((ROWS, DD), F),
            jax.ShapeDtypeStruct((ROWS // bm, 8, bm), F),
        ]
        + [jax.ShapeDtypeStruct(s, F) for s in sums],
        compiler_params=pltpu.CompilerParams(vmem_limit_bytes=VMEM_LIMIT),
        name="dec_mlp",
    )(x, a, target, rows, wo, wu, wd, wh, vec)


def qkv_back_kernel(x_ref, dx_ref, *refs):
    parts, (row_ref, w_ref, vec_ref, o_ref, g_ref, gv_ref) = refs[:9], refs[9:]

    @pl.when(pl.program_id(0) == 0)
    def _():
        for ref in (g_ref, gv_ref):
            ref[...] = jnp.zeros_like(ref)

    hat, inverse = norm_rows(x_ref[...])
    normed = (hat * vec_ref[0:1, :DD] + vec_ref[1:2, :DD]).astype(B)
    dp = jnp.concatenate([parts[3 * h + i][...] for i in range(3) for h in range(3)], axis=1)
    g_ref[...] += mm(normed, dp, TN)
    dn = mm(dp, w_ref[...], NT)
    gv_ref[2:3, :] += total(dp.astype(F))
    gv_ref[0:1, :DD] += total(dn * hat)
    gv_ref[1:2, :DD] += total(dn)
    dx = dx_ref[...] + norm_back(dn * vec_ref[0:1, :DD], hat, inverse)
    o_ref[...] = dx
    gv_ref[3:4, :DD] += total(dx * row_ref[:, 2:3])


def qkv_back(x, dx, dqkv, rows, w, vec, bm=432):
    full = lambda shape: pl.BlockSpec(shape, lambda i: (0, 0))
    part = lambda width: pl.BlockSpec((bm, width), lambda i: (i, 0))
    return pl.pallas_call(
        qkv_back_kernel,
        grid=(ROWS // bm,),
        in_specs=[part(DD)] * 2 + [part(128)] * 10 + [full(w.shape), full(vec.shape)],
        out_specs=[part(DD), full(w.shape), full(vec.shape)],
        out_shape=[
            jax.ShapeDtypeStruct((ROWS, DD), F),
            jax.ShapeDtypeStruct(w.shape, F),
            jax.ShapeDtypeStruct(vec.shape, F),
        ],
        compiler_params=pltpu.CompilerParams(vmem_limit_bytes=VMEM_LIMIT),
        cost_estimate=pl.CostEstimate(flops=15 * 10**9, bytes_accessed=8 << 20, transcendentals=0),
        name="dec_qkv_back",
    )(x, dx, *[part for head in dqkv for part in head], rows, w, vec)


def stack_rows(pieces, width, count=8):
    rows = [jnp.pad(p.astype(F), (0, width - p.shape[0])) for p in pieces]
    rows += [jnp.zeros((width,), F)] * (count - len(rows))
    return jnp.stack(rows)


def gelu_parts(h):
    cdf = 0.5 * (1.0 + lax.erf(h * (1.0 / math.sqrt(2.0))))
    return cdf, cdf + h * jnp.exp(-0.5 * h * h) * (1.0 / math.sqrt(2.0 * math.pi))


def enc_pair(qkv_ref, marks, j):
    q, k, v = (qkv_ref[:, i * D + j * 128 : i * D + (j + 1) * 128] for i in range(3))
    q = q * jnp.asarray(0.125, B)
    low = low_lanes(q.shape[0])
    return q, k, v, halves(low, q, marks[0]), halves(low, k, marks[1])


def enc_forward_kernel(
    pix_ref, place_ref, qm_ref, km_ref, vec_ref, we_hbm, wq_hbm, wo_hbm, wu_hbm, wd_hbm, wp_hbm,
    latent_ref, e0_ref, qkv_ref, a_ref, x1_ref, h_ref, x2_ref,
    we, wq, wo, wu, wd, wp, sems,
):
    loads = [
        pltpu.make_async_copy(source, target, sems.at[i])
        for i, (source, target) in enumerate(
            zip((we_hbm, wq_hbm, wo_hbm, wu_hbm, wd_hbm, wp_hbm), (we, wq, wo, wu, wd, wp))
        )
    ]
    for load in loads:
        load.start()
    loads[0].wait()
    e0 = mm(pix_ref[...], we[...]) + vec_ref[0:1, :D] + place_ref[...]
    e0_ref[...] = e0
    hat, unused = norm_rows(e0)
    n1 = (hat * vec_ref[1:2, :D] + vec_ref[2:3, :D]).astype(B)
    loads[1].wait()
    for i, bias in enumerate((vec_ref[3:4, :D], 0.0, vec_ref[4:5, :D])):
        part = slice(i * D, (i + 1) * D)
        qkv_ref[:, part] = (mm(n1, wq[:, part]) + bias).astype(B)
    marks = (qm_ref[...], km_ref[...])
    for j in range(HEADS // 2):
        unused, unused, v, qs, ks = enc_pair(qkv_ref, marks, j)
        scores = [mm(ks[i], qs[i], NT) for i in range(2)]
        outs = [mm(v, softmax_keys(s)[0].astype(B), TN) for s in scores]
        a_ref[:, j * 128 : (j + 1) * 128] = jnp.where(low_rows(v.shape[0]), outs[0], outs[1]).T.astype(B)
    loads[2].wait()
    x1 = e0 + mm(a_ref[...], wo[...]) + vec_ref[5:6, :D]
    x1_ref[...] = x1
    hat, unused = norm_rows(x1)
    n2 = (hat * vec_ref[6:7, :D] + vec_ref[7:8, :D]).astype(B)
    loads[3].wait()
    loads[4].wait()
    x2 = x1 + vec_ref[9:10, :D]
    for i in range(4):
        part = slice(i * D, (i + 1) * D)
        h = mm(n2, wu[:, part]) + vec_ref[8:9, part]
        h_ref[:, part] = h
        x2 += mm((h * gelu_parts(h)[0]).astype(B), wd[part, :])
    x2_ref[...] = x2
    hat, unused = norm_rows(x2)
    loads[5].wait()
    latent_ref[...] = mm((hat * vec_ref[10:11, :D] + vec_ref[11:12, :D]).astype(B), wp[...])


def enc_forward(pixels, places, q_marks, k_marks, vec, mats):
    rows = pixels.shape[0]
    hbm, vmem = pl.BlockSpec(memory_space=pl.ANY), pl.BlockSpec(memory_space=pltpu.VMEM)
    outs = [(DD, F), (D, F), (3 * D, B), (D, B), (D, F), (FF, F), (D, F)]
    return pl.pallas_call(
        enc_forward_kernel,
        in_specs=[vmem] * 5 + [hbm] * 6,
        out_specs=[vmem] * 7,
        out_shape=[jax.ShapeDtypeStruct((rows, width), kind) for width, kind in outs],
        scratch_shapes=[pltpu.VMEM(m.shape, B) for m in mats] + [pltpu.SemaphoreType.DMA((6,))],
        compiler_params=pltpu.CompilerParams(vmem_limit_bytes=VMEM_LIMIT),
        cost_estimate=pl.CostEstimate(flops=15 * 10**9, bytes_accessed=20 << 20, transcendentals=0),
        name="enc_forward",
    )(pixels, places, q_marks, k_marks, vec, *mats)


def put_product(lin, top, row, left, right):
    m, c = left.shape[0], right.shape[1] // 128
    step = min(m, 768)
    most = top[...]
    for r in range(0, m, step):
        for first in range(0, c, 2):
            last = min(first + 2, c)
            value = mm(left[r : r + step, :], right[:, first * 128 : last * 128])
            for i in range(first, last):
                piece = value[:, (i - first) * 128 : (i - first + 1) * 128]
                lin[pl.ds(row + r * c + i, step, stride=c), :] = piece
                most = jnp.maximum(most, jnp.max(jnp.abs(piece).reshape(-1, 8, 128), axis=0))
    top[...] = most


def put_vector(lin, top, row, value):
    for i in range(value.shape[1] // 128):
        piece = value[:, i * 128 : (i + 1) * 128]
        lin[pl.ds(row + i, 1), :] = piece
        top[0:1, :] = jnp.maximum(top[0:1, :], jnp.abs(piece))


def turned(value):
    return value.astype(F).T.astype(B)


def flush_start(lin, base, segments, core, kept, away, sem):
    for c in range(2):

        @pl.when(core == c)
        def _():
            for source, count, s, h, k, y, to in segments:
                target = (kept if h == c else away)[k]
                pltpu.make_async_copy(
                    lin.at[pl.ds(source - base, count)], target.at[s, y, pl.ds(to, count)], sem
                ).start()


def flush_wait(lin, segments, sem):
    count = sum(segment[1] for segment in segments)
    pltpu.make_async_copy(lin.at[pl.ds(0, count)], lin.at[pl.ds(0, count)], sem).wait()


def enc_back_one_kernel(
    base, rows_of, cuts, core_ref, vis_ref, live_ref, dx0_ref, x1_ref, h_ref, x2_ref, vec_ref, wu_hbm, wd_hbm, wp_hbm,
    dx1_ref, top_ref, *refs,
):
    chunks = (len(refs) - 7) // 2
    kept, away = refs[:chunks], refs[chunks : 2 * chunks]
    lin, wu, wd, wp, dl_ref, dh_ref, sems = refs[-7:]
    loads = [
        pltpu.make_async_copy(source, target, sems.at[i])
        for i, (source, target) in enumerate(zip((wp_hbm, wd_hbm, wu_hbm), (wp, wd, wu)))
    ]
    for load in loads:
        load.start()
    top_ref[...] = jnp.zeros_like(top_ref)
    upb, down, db, fg, fb, proj, end, last = (r - base for r in rows_of[1:])

    def take_slot(i, carry):
        at = pl.ds(jnp.minimum(vis_ref[i], ROWS - 1), 1)
        dl_ref[pl.ds(i, 1), :] = dx0_ref[at, :] * live_ref[i]
        return carry

    lax.fori_loop(0, dl_ref.shape[0], take_slot, 0, unroll=8)
    dl = dl_ref[...].astype(B)
    hatf, invf = norm_rows(x2_ref[...])
    put_product(lin, top_ref, proj, turned(hatf * vec_ref[10:11, :D] + vec_ref[11:12, :D]), dl)
    lin[pl.ds(end, lin.shape[0] - end), :] = jnp.zeros((lin.shape[0] - end, 128), F)
    loads[0].wait()
    dnf = mm(dl, wp[...], NT)
    put_vector(lin, top_ref, fg, total(dnf * hatf))
    put_vector(lin, top_ref, fb, total(dnf))
    dx2 = norm_back(dnf * vec_ref[10:11, :D], hatf, invf)
    put_vector(lin, top_ref, db, total(dx2))
    dx2b = dx2.astype(B)
    loads[1].wait()
    for i in range(4):
        part = slice(i * D, (i + 1) * D)
        h = h_ref[:, part]
        kept_share, slope = gelu_parts(h)
        put_product(lin, top_ref, down + i * D * (D // 128), turned(h * kept_share), dx2b)
        dh = mm(dx2b, wd[part, :], NT) * slope
        put_vector(lin, top_ref, upb + i * (D // 128), total(dh))
        dh_ref[:, part] = dh.astype(B)
    flush_start(lin, base, cuts[0], core_ref[0], kept, away, sems.at[3])
    loads[2].wait()
    hat2, inv2 = norm_rows(x1_ref[...])
    put_product(lin, top_ref, 0, turned(hat2 * vec_ref[6:7, :D] + vec_ref[7:8, :D]), dh_ref[...])
    flush_start(lin, base, cuts[1], core_ref[0], kept, away, sems.at[4])
    dn2 = mm(dh_ref[...], wu[...], NT)
    dx1_ref[0:1, :] = jnp.zeros((1, D), F)
    dx1 = dx2 + norm_back(dn2 * vec_ref[6:7, :D], hat2, inv2)
    count = dx1.shape[0]
    dx1_ref[0:count, :] = dx1
    dx1_ref[count : count + 1, :] = total(dn2 * hat2)
    dx1_ref[count + 1 : count + 2, :] = total(dn2)
    flush_wait(lin, cuts[0], sems.at[3])
    flush_wait(lin, cuts[1], sems.at[4])


def enc_back_two_kernel(
    rows_of, early_of, base_early, cuts, core_ref, dx1_ref, pix_ref, e0_ref, qkv_ref, a_ref, qm_ref, km_ref, vec_ref,
    g_qkv_ref, g_one_ref, wq_hbm, wo_hbm, top_in, *refs,
):
    chunks = (len(refs) - 6) // 4
    top_ref = refs[2 * chunks]
    kept, away = refs[2 * chunks + 1 : 3 * chunks + 1], refs[3 * chunks + 1 : 4 * chunks + 1]
    lin, wq, wo, dp_ref, sems = refs[-5:]
    loads = [
        pltpu.make_async_copy(source, target, sems.at[i])
        for i, (source, target) in enumerate(zip((wo_hbm, wq_hbm), (wo, wq)))
    ]
    for load in loads:
        load.start()
    top_ref[...] = top_in[...]
    embed, eb, g1, b1, qkv, qbias, vbias, out, ob, g2, b2 = rows_of
    count = pix_ref.shape[0]
    dx1 = dx1_ref[0:count, :]
    put_vector(lin, top_ref, g2, dx1_ref[count : count + 1, :])
    put_vector(lin, top_ref, b2, dx1_ref[count + 1 : count + 2, :])
    put_vector(lin, top_ref, ob, total(dx1))
    dx1b = dx1.astype(B)
    put_product(lin, top_ref, out, turned(a_ref[...]), dx1b)
    loads[0].wait()
    da = mm(dx1b, wo[...], NT).astype(B)
    marks = (qm_ref[...], km_ref[...])
    for j in range(HEADS // 2):
        q, k, v, qs, ks = enc_pair(qkv_ref, marks, j)
        low, zero = low_lanes(count), jnp.zeros_like(q)
        dz = halves(low, da[:, j * 128 : (j + 1) * 128], zero)
        scores = [mm(ks[i], qs[i], NT) for i in range(2)]
        dps = [mm(v, d, NT) for d in dz]
        ps, dss, dq = [], [], jnp.zeros((128, count), F)
        for i, keys in enumerate(halves(low, k, zero)):
            p = softmax_keys(scores[i])[0]
            ps.append(p.astype(B))
            dss.append((p * (dps[i] - jnp.sum(p * dps[i], axis=0, keepdims=True))).astype(B))
            dq += mm(keys, dss[i], TN)
        dk = mm(jnp.concatenate(dss, axis=1), jnp.concatenate(halves(low, q, zero), axis=0))
        dv = mm(jnp.concatenate(ps, axis=1), jnp.concatenate(dz, axis=0))
        for i, value in enumerate((dq.T * 0.125, dk, dv)):
            dp_ref[:, i * D + j * 128 : i * D + (j + 1) * 128] = value.astype(B)
    dp = dp_ref[...]
    sums = total(dp.astype(F))
    put_vector(lin, top_ref, qbias, sums[:, :D])
    put_vector(lin, top_ref, vbias, sums[:, 2 * D :])
    hat, inverse = norm_rows(e0_ref[...])
    put_product(lin, top_ref, qkv, turned(hat * vec_ref[1:2, :D] + vec_ref[2:3, :D]), dp)
    loads[1].wait()
    dn = mm(dp, wq[...], NT)
    put_vector(lin, top_ref, g1, total(dn * hat))
    put_vector(lin, top_ref, b1, total(dn))
    de0 = dx1 + norm_back(dn * vec_ref[1:2, :D], hat, inverse)
    put_vector(lin, top_ref, eb, total(de0))
    flush_start(lin, 0, cuts[0], core_ref[0], kept, away, sems.at[2])
    put_product(lin, top_ref, embed, turned(pix_ref[...]), de0.astype(B))
    c = g_qkv_ref.shape[1] // 128
    start = early_of[3]
    most = top_ref[...]
    for i in range(c):
        piece = g_qkv_ref[:, i * 128 : (i + 1) * 128]
        lin[pl.ds(start + i, g_qkv_ref.shape[0], stride=c), :] = piece
        most = jnp.maximum(most, jnp.max(jnp.abs(piece).reshape(-1, 8, 128), axis=0))
    top_ref[...] = most
    one = g_one_ref
    for row, value in zip(
        early_of[:3] + early_of[4:6],
        (one[3:4, :DD], one[0:1, :DD], one[1:2, :DD], one[2:3, :DD], one[2:3, 2 * DD :]),
    ):
        put_vector(lin, top_ref, row, value)
    end = early_of[6]
    lin[pl.ds(end, lin.shape[0] - end), :] = jnp.zeros((lin.shape[0] - end, 128), F)
    flush_start(lin, 0, cuts[1], core_ref[0], kept, away, sems.at[3])
    flush_start(lin, base_early, cuts[2], core_ref[0], kept, away, sems.at[4])
    for i in range(3):
        flush_wait(lin, cuts[i], sems.at[2 + i])


class Flat:
    def __init__(self, sections, wide, narrow, chunks):
        self.wide, self.narrow, self.sections = wide, narrow, sections
        self.spans = [-(-(rows + (0 if rows % 8 == 0 else 7)) // 8) * 8 for unused, rows in sections]
        self.parts = [-(-span // (narrow * 16)) * 16 for span in self.spans]
        self.starts = [sum(self.parts[:i]) for i in range(len(sections))]
        rows = sum(self.parts)
        step = -(-rows // (chunks * 16)) * 16
        self.chunks = [min(step, rows - i * step) for i in range(chunks)]
        self.shapes = [jax.ShapeDtypeStruct((wide, narrow // 2, count, 128), F) for count in self.chunks]

    def segments(self, section, low, high):
        first, rows = self.sections[section]
        part, span, at = self.parts[section], self.spans[section], self.starts[section]
        out = []
        for s in range(self.wide):
            start = first + s * rows // 8 * 8
            for p in range(self.narrow):
                begin = 0
                for k, count in enumerate(self.chunks):
                    lead = start + p * part - at + begin
                    a = max(low, start + p * part, lead)
                    b = min(high, start + span, start + (p + 1) * part, lead + count)
                    if a < b:
                        out.append((a, b - a, s, p // 2, k, p % 2, a - lead))
                    begin += count
        return out

    def reach(self, section):
        first, rows = self.sections[section]
        return first + (self.wide - 1) * rows // 8 * 8 + self.spans[section]

    def offset(self, section, index):
        return lax.rem(index * self.sections[section][1], 8)

    def of(self, piece, section):
        return piece[self.starts[section] : self.starts[section] + self.parts[section]]

    def squares(self, piece, section, index, part):
        value = self.of(piece, section)
        row = part * self.parts[section] + jnp.arange(value.shape[0], dtype=jnp.int32)[:, None]
        at = self.offset(section, index)
        inside = (row >= at) & (row < at + self.sections[section][1])
        return jnp.sum(jnp.where(inside, value * value, 0.0))

    def take(self, window, section, index):
        return lax.dynamic_slice_in_dim(window, self.offset(section, index), self.sections[section][1])


def enc_back_one(core, visible, live, dx0, saved, vec, mats, flat):
    x1, h, x2 = saved[3:]
    wu, wd, wp = mats[3:]
    rows = x1.shape[0]
    pieces = [p[0] for p in table(ENC_SHAPES)]
    end = pieces[-1] + DD // 128 * D
    total_rows = flat.sections[0][1] * flat.wide
    reach = max(flat.reach(0), total_rows)
    rows_of = tuple(pieces[11:]) + (end, reach)
    base, split = pieces[11], pieces[13]
    smem, vmem, hbm = (
        pl.BlockSpec(memory_space=space) for space in (pltpu.SMEM, pltpu.VMEM, pl.ANY)
    )
    top = jax.ShapeDtypeStruct((8, 128), F)
    cuts = (flat.segments(0, split, reach), flat.segments(0, base, split))
    room = max([reach - base] + [sum(seg[1] for seg in cut) for cut in cuts])
    chunks = len(flat.chunks)
    dx1, top, *out = pl.pallas_call(
        functools.partial(enc_back_one_kernel, base, rows_of, cuts),
        in_specs=[smem] * 3 + [vmem] * 5 + [hbm] * 3,
        out_specs=[vmem] * 2 + [hbm] * (2 * chunks),
        out_shape=[jax.ShapeDtypeStruct((rows + 8, D), F), top] + flat.shapes * 2,
        scratch_shapes=[
            pltpu.VMEM((room, 128), F), pltpu.VMEM(wu.shape, B), pltpu.VMEM(wd.shape, B),
            pltpu.VMEM(wp.shape, B), pltpu.VMEM((rows, DD), F),
            pltpu.VMEM((rows, FF), B), pltpu.SemaphoreType.DMA((5,)),
        ],
        compiler_params=pltpu.CompilerParams(vmem_limit_bytes=VMEM_LIMIT),
        cost_estimate=pl.CostEstimate(flops=20 * 10**9, bytes_accessed=30 << 20, transcendentals=0),
        name="enc_back_one",
    )(core, visible, live, dx0, x1, h, x2, vec, wu, wd, wp)
    return dx1, top, out


def enc_back_two(core, dx1, top, out, saved, pixels, marks, vec, mats, g_qkv, g_one, flat):
    e0, qkv, a = saved[:3]
    wq, wo = mats[1:3]
    rows = pixels.shape[0]
    pieces = [p[0] for p in table(ENC_SHAPES)]
    base = pieces[11]
    early_rows = table(DEC_SHAPES[:6])
    first = flat.sections[1][0]
    last = early_rows[-1][0] + early_rows[-1][2]
    early_of = tuple(base + p[0] for p in early_rows) + (base + last,)
    reach = max(flat.reach(1) - first, last)
    cuts = (
        flat.segments(0, pieces[1] // 8 * 8, base), flat.segments(0, 0, pieces[1] // 8 * 8),
        flat.segments(1, first, first + reach),
    )
    room = max([base + reach] + [sum(seg[1] for seg in cut) for cut in cuts])
    smem, vmem, hbm = (
        pl.BlockSpec(memory_space=space) for space in (pltpu.SMEM, pltpu.VMEM, pl.ANY)
    )
    chunks = len(flat.chunks)
    top, *out = pl.pallas_call(
        functools.partial(enc_back_two_kernel, tuple(pieces[:11]), early_of, first - base, cuts),
        in_specs=[smem] + [vmem] * 10 + [hbm] * 2 + [vmem] + [hbm] * (2 * chunks),
        out_specs=[vmem] + [hbm] * (2 * chunks),
        out_shape=[jax.ShapeDtypeStruct((8, 128), F)] + flat.shapes * 2,
        input_output_aliases={14 + i: 1 + i for i in range(2 * chunks)},
        scratch_shapes=[
            pltpu.VMEM((room, 128), F), pltpu.VMEM(wq.shape, B), pltpu.VMEM(wo.shape, B),
            pltpu.VMEM((rows, 3 * D), B), pltpu.SemaphoreType.DMA((5,)),
        ],
        compiler_params=pltpu.CompilerParams(vmem_limit_bytes=VMEM_LIMIT),
        cost_estimate=pl.CostEstimate(flops=15 * 10**9, bytes_accessed=30 << 20, transcendentals=0),
        name="enc_back_two",
    )(core, dx1, pixels, e0, qkv, a, *marks, vec, g_qkv, g_one, wq, wo, top, *out)
    return out[:chunks], out[chunks:], jnp.max(top)


def table(shapes, row=0):
    out = []
    for s in shapes:
        m, c = (s[0], s[1] // 128) if len(s) == 2 else (1, s[0] // 128)
        out.append((row, m, c))
        row += m * c
    return out


def job_rows(m, c, most):
    return max(n for n in range(16, m + 1, 16) if m % n == 0 and n * c <= most)


def split_rows(shard, shares, note):
    out, place, first = [], 0, 0
    for i, share in enumerate(shares):
        rows = -(-shard * share // (100 * 16)) * 16
        used = rows - 1 if note and i == 0 else rows
        out.append((place, first, 4, rows, used))
        place, first = place + 4 * rows, first + 4 * used
    if first < shard:
        rows = -(-(shard - first) // 32) * 16
        out.append((place, first, 2, rows, rows))
    return out


def unpack_kernel(pieces, groups, shard, wide, core_ref, *refs):
    mats = [p for p in pieces if p[1] > 1]
    count = len(groups)
    own, other, refs = refs[:count], refs[count : 2 * count], refs[2 * count :]
    outs, vec_ref = refs[: len(mats)], refs[len(mats)]
    buf, lin, in_sem, out_sem = refs[len(mats) + 1 : len(mats) + 5]
    stages = refs[len(mats) + 5 :]
    core = core_ref[0]
    plan, size = [], 0
    for g, (place, first, parts, rows, used) in enumerate(groups):
        for i in range(parts):
            a, b = first + i * used, min(first + (i + 1) * used, shard)
            if a < b:
                plan.append((g, i, rows, size, a, b - a))
                size += rows

    def fetch(sources, s, entry):
        g, i, rows, to, at, used = entry
        at_source = (i % 2) * rows if groups[g][2] == 4 else 0
        return pltpu.make_async_copy(
            sources[g].at[s, pl.ds(at_source, rows)], buf.at[s, pl.ds(to, rows)], in_sem.at[s]
        )

    for s in range(wide):
        for c in range(2):

            @pl.when(core == c)
            def _():
                for entry in plan:
                    of = entry[1] // 2 if groups[entry[0]][2] == 4 else entry[1]
                    fetch(own if of == c else other, s, entry).start()

    for s in range(wide):
        pltpu.make_async_copy(buf.at[s, pl.ds(0, size)], buf.at[s, pl.ds(0, size)], in_sem.at[s]).wait()
        for g, i, rows, to, at, used in plan:
            lin[pl.ds(s * shard + at, used), :] = buf[s, pl.ds(to, rows), :].astype(F)[:used]

    vec_ref[...] = jnp.zeros_like(vec_ref)
    v = 0
    for row, m, c in pieces:
        if m == 1:
            for j in range(c):
                vec_ref[v : v + 1, j * 128 : (j + 1) * 128] = lin[pl.ds(row + j, 1), :]
            v += 1
    for k, (row, m, c) in enumerate(mats):
        stage, out = stages[k], outs[k]
        n = stage.shape[1]
        jobs = m // n

        def store(j, slot):
            return pltpu.make_async_copy(
                stage.at[slot], out.at[pl.ds(pl.multiple_of(j * n, 16), n)], out_sem.at[slot]
            )

        def job(j, carry):
            slot = lax.rem(j, 2)

            @pl.when(j >= 2)
            def _():
                store(j - 2, slot).wait()

            for i in range(c):
                rows = pl.ds(row + i + j * (n * c), n, stride=c)
                stage[slot, :, i * 128 : (i + 1) * 128] = lin[rows, :].astype(B)
            store(j, slot).start()
            return carry

        lax.fori_loop(0, jobs, job, 0)
        for j in range(max(jobs - 2, 0), jobs):
            store(j, j % 2).wait()


def unpack_flat(own, other, groups, shard, wide, core, shapes, name):
    pieces = table(shapes)
    mats = [s for s in shapes if len(s) == 2]
    vectors = [s for s in shapes if len(s) == 1]
    width = max(s[0] for s in vectors)
    count = -(-len(vectors) // 8) * 8
    hbm = pl.BlockSpec(memory_space=pl.ANY)
    stages = [pltpu.VMEM((2, job_rows(s[0], s[1] // 128, 1152), s[1]), B) for s in mats]
    room = groups[-1][0] + groups[-1][2] * groups[-1][3]
    return pl.pallas_call(
        functools.partial(unpack_kernel, pieces, groups, shard, wide),
        in_specs=[pl.BlockSpec(memory_space=pltpu.SMEM)] + [hbm] * (2 * len(groups)),
        out_specs=[hbm] * len(mats) + [pl.BlockSpec(memory_space=pltpu.VMEM)],
        out_shape=[jax.ShapeDtypeStruct(s, B) for s in mats] + [jax.ShapeDtypeStruct((count, width), F)],
        scratch_shapes=[
            pltpu.VMEM((wide, room, 128), B), pltpu.VMEM((wide * shard, 128), F),
            pltpu.SemaphoreType.DMA((wide,)), pltpu.SemaphoreType.DMA((2,)),
        ] + stages,
        compiler_params=pltpu.CompilerParams(vmem_limit_bytes=VMEM_LIMIT),
        cost_estimate=pl.CostEstimate(flops=0, bytes_accessed=wide * shard * 1536, transcendentals=0),
        name=name,
    )(core, *own, *other)


def pack_kernel(pieces, segments, core_ref, *refs):
    mats = [p for p in pieces if p[1] > 1]
    ins, vec_ref = refs[: len(mats)], refs[len(mats)]
    top_ref, *out = refs[len(mats) + 1 : -2]
    kept, away = out[: len(out) // 2], out[len(out) // 2 :]
    lin, sem = refs[-2:]
    first, end = pieces[0][0], pieces[-1][0] + pieces[-1][1] * pieces[-1][2]
    lin[pl.ds(0, first), :] = jnp.zeros((first, 128), F)
    lin[pl.ds(end, lin.shape[0] - end), :] = jnp.zeros((lin.shape[0] - end, 128), F)
    top_ref[...] = jnp.zeros_like(top_ref)
    k, v = 0, 0
    for row, m, c in pieces:
        if m == 1:
            put_vector(lin, top_ref, row, vec_ref[v : v + 1, : c * 128])
            v += 1
            continue
        most = top_ref[...]
        for i in range(c):
            piece = ins[k][:, i * 128 : (i + 1) * 128]
            lin[pl.ds(row + i, m, stride=c), :] = piece
            most = jnp.maximum(most, jnp.max(jnp.abs(piece).reshape(-1, 8, 128), axis=0))
        top_ref[...] = most
        k += 1
    flush_start(lin, 0, segments, core_ref[0], kept, away, sem)
    flush_wait(lin, segments, sem)


def pack_late(mats, vectors, pieces, flat, core, name):
    hbm, vmem = pl.BlockSpec(memory_space=pl.ANY), pl.BlockSpec(memory_space=pltpu.VMEM)
    segments = flat.segments(0, 0, flat.reach(0))
    room = max(flat.reach(0), flat.wide * flat.sections[0][1], sum(seg[1] for seg in segments))
    chunks = len(flat.chunks)
    unused, *out = pl.pallas_call(
        functools.partial(pack_kernel, pieces, segments),
        in_specs=[pl.BlockSpec(memory_space=pltpu.SMEM)] + [vmem] * (len(mats) + 1),
        out_specs=[vmem] + [hbm] * (2 * chunks),
        out_shape=[jax.ShapeDtypeStruct((8, 128), F)] + flat.shapes * 2,
        scratch_shapes=[pltpu.VMEM((room, 128), F), pltpu.SemaphoreType.DMA],
        compiler_params=pltpu.CompilerParams(vmem_limit_bytes=VMEM_LIMIT),
        cost_estimate=pl.CostEstimate(flops=0, bytes_accessed=30 << 20, transcendentals=0),
        name=name,
    )(core, *mats, vectors)
    return out[:chunks], out[chunks:]


class Links:
    def __init__(self, mesh):
        self.narrow, self.wide = mesh.shape["narrow"], mesh.shape["wide"]
        self.wide_bits = [("wide", b) for b in reversed(range(self.wide.bit_length() - 1))]
        self.x, self.upper = self.wide_bits[-1], self.wide_bits[:-1]
        self.y, self.core = ("narrow", 1), ("narrow", 0)

    def mine(self, bit):
        return (lax.axis_index(bit[0]) >> bit[1]) & 1

    def swap(self, value, bit):
        mask = 1 << bit[1] if bit[0] == "wide" else self.wide << bit[1]
        pairs = [(i, i ^ mask) for i in range(self.narrow * self.wide)]
        return lax.ppermute(value, AXES, pairs)

    def everyone(self, value, how):
        for bit in [self.core, self.x, self.y] + self.upper:
            value = how(value, self.swap(value, bit))
        return value

    def scale(self, top):
        count = self.narrow * self.wide
        return 32768.0 / (count * jnp.maximum(self.everyone(top, jnp.maximum), 1e-30))

    def gather(self, value, axes, order):
        group = Group(self, value, axes, order)
        while group.order:
            group.step()
        return group.value

    def scatter_parts(self, kept, other, scale):
        axes = self.wide_bits + [self.y]
        parts = []
        for i, (one, two) in enumerate(zip(kept, other)):
            first = [self.x, self.y] if i % 2 == 0 else [self.y, self.x]
            shape = (2,) * len(axes) + one.shape[2:]
            parts.append(Part(self, one.reshape(shape), two.reshape(shape), axes, first + self.upper, scale))
        return parts


class Group:
    def __init__(self, links, value, axes, order):
        self.links, self.value, self.axes, self.order, self.have = links, value, axes, list(order), []

    def step(self):
        bit = self.order.pop(0)
        other = self.links.swap(self.value, bit)
        low = self.links.mine(bit) == 0
        self.have.append(bit)
        place = [b for b in self.axes if b in self.have].index(bit)
        pair = [jnp.where(low, self.value, other), jnp.where(low, other, self.value)]
        self.value = jnp.stack(pair, axis=place)


class Part:
    def __init__(self, links, kept, other, axes, order, scale):
        self.links, self.kept, self.other, self.axes, self.order = links, kept, other, list(axes), list(order)
        self.scale = scale

    def away(self):
        bit = self.order[0]
        self.place, self.index = self.axes.index(bit), self.links.mine(bit)
        value = self.take(1 - self.index)
        return value if len(self.order) == 1 or self.scale is None else (value * self.scale).astype(jnp.float16)

    def take(self, index):
        cut = lambda value: lax.dynamic_index_in_dim(value, index, self.place, keepdims=False)
        return cut(self.kept) + cut(self.other)

    def exchange(self, away):
        bit = self.order.pop(0)
        received = self.links.swap(away, bit)
        if received.dtype == jnp.float16:
            received = received.astype(F) * (1.0 / self.scale)
        self.kept, self.other = self.take(self.index), received
        self.axes.pop(self.place)

    def finish(self):
        while self.order:
            self.exchange(self.away())
        return self.kept + self.other


def after(value, *others):
    return lax.optimization_barrier((value,) + others)[0]


def gather_groups(shard, groups, orders, note, links):
    unused, first, parts, rows, used = groups[-1]
    shard = jnp.pad(shard, ((0, first + parts * used - shard.shape[0]), (0, 0)))
    out = []
    for (unused, first, parts, rows, used), order in zip(groups, orders):
        part = links.mine(links.core) if parts == 2 else links.mine(links.core) * 2 + links.mine(links.y)
        value = lax.dynamic_slice_in_dim(shard, first + part * used, used)
        if used < rows:
            value = jnp.concatenate([value, note])
        out.append(Group(links, value, links.wide_bits + ([links.y] if parts == 4 else []), order))
    return out


def gathered(groups, links):
    own = [g.value.reshape(links.wide, -1, 128) for g in groups]
    return own, [links.swap(v, links.core) for v in own]


def gather_params(enc, dec, note, links):
    y_last, x_last = links.upper + [links.x, links.y], links.upper + [links.y, links.x]
    enc_rows, dec_rows = split_rows(enc.shape[0], (8, 8), False), split_rows(dec.shape[0], (13, 13), True)
    enc_groups = gather_groups(
        enc, enc_rows, (y_last, x_last, links.upper[:-1] + [links.x] + links.upper[-1:]), note, links
    )
    one, two, three = enc_groups
    dec_groups = gather_groups(dec, dec_rows, (x_last, y_last), note, links)
    for g in (one, two):
        g.step()
    three.value = after(three.value, one.value, two.value)
    while one.order:
        for g in dec_groups:
            g.value = after(g.value, one.value, two.value)
        for g in (one, two, three):
            if g.order:
                g.step()
        for g in dec_groups:
            g.step()
    return (*gathered(enc_groups, links), enc_rows), dec_groups, dec_rows


def join_shard(piece, links):
    axes = [links.core, links.y]
    return links.gather(piece, axes, [links.y, links.core]).reshape(-1, 128)


def adamw_update(master, gradient, moment_one, moment_two, clip_scale):
    gradient = gradient * clip_scale
    moment_one = BETA_ONE * moment_one + (1.0 - BETA_ONE) * gradient
    moment_two = BETA_TWO * moment_two + (1.0 - BETA_TWO) * gradient * gradient
    first_hat = moment_one / (1.0 - BETA_ONE**STEP)
    second_hat = moment_two / (1.0 - BETA_TWO**STEP)
    updated = master - learn_rate * (
        first_hat / (jnp.sqrt(second_hat) + EPSILON) + weight_decay * master
    )
    return (moment_one, moment_two, updated)


def body(
    links, vis_pixels, target, clip_lens, vis_index, params_enc, m_enc, v_enc, params_dec, m_dec, v_dec
):
    lengths = clip_lens[0]
    visible = vis_index[0]
    mine, core = lax.axis_index("wide"), links.mine(links.core).astype(jnp.int32).reshape(1)
    enc_shard, dec_shard = (v.shape[0] // 128 for v in (params_enc, params_dec))
    segment, clip_place, slot_live, shown_flag, counted = layout(lengths, visible, target.shape[0])

    here = jnp.sum(counted).astype(jnp.int32)
    note = jnp.pad(jnp.stack([here // 64, here % 64]), (0, 126))[None, :].astype(B)
    enc_parts, dec_groups, dec_rows = gather_params(
        params_enc.astype(B).reshape(-1, 128), params_dec.astype(B).reshape(-1, 128), note, links
    )
    *enc_mats, enc_vec = unpack_flat(*enc_parts, enc_shard, links.wide, core, ENC_SHAPES, "unpack_enc")
    for g in dec_groups:
        g.value = after(g.value, enc_vec)
        while g.order:
            g.step()
    dec_own, dec_other = gathered(dec_groups, links)
    last = dec_rows[0][3] - 1
    notes = jnp.stack([v[0].reshape(links.wide, 2, -1, 128)[:, :, last, :2] for v in (dec_own, dec_other)])
    notes = notes.astype(F)
    masked_count = jnp.sum(notes[..., 0]) * 64.0 + jnp.sum(notes[..., 1])
    cotangent = 1.0 / masked_count

    segment, clip_place, shown_flag, counted = (
        v[:ROWS] for v in (segment, clip_place, shown_flag, counted)
    )
    rows = jnp.stack([counted, counted * (cotangent * (2.0 / PIX)), 1.0 - shown_flag], axis=1)
    rows = jnp.pad(rows, ((0, 0), (0, 125)))
    lane = jnp.arange(128, dtype=jnp.int32)[None, :] % 64

    def marks_of(labels):
        mark = lane == labels[:, None]
        return mark.astype(B), jnp.where(mark | (lane > 3), 0.0, -1e30).astype(B)

    q_marks, k_marks = marks_of(segment)
    slot_segment, slot_place = slot_layout(lengths, visible)
    slot_marks = marks_of(slot_segment)

    latent, *saved = enc_forward(vis_pixels, sinusoid(slot_place, D), *slot_marks, enc_vec, enc_mats)
    dec_own = [after(v, latent) for v in dec_own]
    *dec_mats, dec_vec = unpack_flat(
        dec_own, dec_other, dec_rows, dec_shard, links.wide, core, DEC_SHAPES, "unpack_dec"
    )
    w_qkv, w_out, w_up, w_down, w_head = dec_mats
    bias = jnp.concatenate([dec_vec[3, :DD], jnp.zeros((DD,), F), dec_vec[4, :DD]])
    vec_one = stack_rows([dec_vec[1, :DD], dec_vec[2, :DD], bias], 3 * DD)
    vec_two = jnp.concatenate([dec_vec[5:13], jnp.zeros((8, DFF), F)])
    x0, qkv = qkv_forward(
        visible, slot_live, latent, sinusoid(clip_place, DD), rows, w_qkv, vec_one, dec_vec
    )
    a, lse = attend_forward(qkv, q_marks, k_marks)
    da, dx1, dd, g_out, g_up, g_down, g_head, g_two = mlp_both(
        x0, a, target, rows, w_out, w_up, w_down, w_head, vec_two
    )

    late_flat = Flat([(0, dec_shard)], links.wide, links.narrow, 2)
    kept, away = pack_late(
        [g_out, g_up, g_down, g_head], g_two, table(DEC_SHAPES)[6:], late_flat, core, "pack_dec"
    )
    back = lambda da, h: attend_back(qkv, q_marks, k_marks, da, lse, dd, h)
    da, away = lax.optimization_barrier((da, away))
    late = links.scatter_parts(kept, [links.swap(v, links.core) for v in away], None)
    dqkv = [back(da, 0)]
    for h in (1, 2):
        sent = [part.away() for part in late]
        da, sent, dqkv = lax.optimization_barrier((da, sent, dqkv))
        dqkv = dqkv + [back(da, h)]
        for part, value in zip(late, sent):
            part.exchange(value)
    sent = [part.away() for part in late]
    dx1, sent, dqkv = lax.optimization_barrier((dx1, sent, dqkv))
    dx0, g_qkv, g_one = qkv_back(x0, dx1, dqkv, rows, w_qkv, vec_one)
    for part, value in zip(late, sent):
        part.exchange(value)

    early = table(DEC_SHAPES[:6])
    early_count = early[-1][0] + early[-1][2]
    flat = Flat(
        [(0, enc_shard), (enc_shard * links.wide, -(-early_count // links.wide))], links.wide, links.narrow, 4
    )
    dx1, top, out = enc_back_one(core, visible, slot_live, dx0, saved, enc_vec, enc_mats, flat)
    sent = [part.away() for part in late]
    dx1, sent = lax.optimization_barrier((dx1, sent))
    kept, away, top = enc_back_two(
        core, dx1, top, out, saved, vis_pixels, slot_marks, enc_vec, enc_mats, g_qkv, g_one, flat
    )
    for part, value in zip(late, sent):
        part.exchange(value)
    piece_dec = jnp.concatenate([part.finish() for part in late])
    first = [links.swap(v, links.core) for v in away[:2]]
    second = [links.swap(after(v, *first), links.core) for v in away[2:]]
    parts = links.scatter_parts(kept, first + second, links.scale(top))
    piece = jnp.concatenate([part.finish() for part in parts])

    part = links.mine(links.core) * 2 + links.mine(links.y)
    squares = flat.squares(piece, 0, mine, part) + flat.squares(piece, 1, mine, part)
    squares += late_flat.squares(piece_dec, 0, mine, part)
    squares, loss_sum = links.everyone(jnp.stack([squares, jnp.sum(g_two[8]) / PIX]), jnp.add)
    grad_norm = jnp.sqrt(squares)
    clip_scale = jnp.minimum(1.0, clip_norm / (grad_norm + 1e-06))
    narrow_bits = [links.core, links.y]
    joined, joined_late = join_shard(flat.of(piece, 0), links), join_shard(piece_dec, links)
    everywhere = links.gather(
        flat.of(piece, 1), links.wide_bits + narrow_bits, links.upper + [links.x, links.y, links.core]
    ).reshape(links.wide, -1, 128)
    count = flat.sections[1][1]
    early_sum = jnp.concatenate(
        [everywhere[s, s * count % 8 : s * count % 8 + count] for s in range(links.wide)]
    )
    early_sum = jnp.pad(early_sum, ((0, links.wide * dec_shard - links.wide * count), (0, 0)))
    grad_enc = flat.take(joined, 0, mine).reshape(-1)
    grad_dec = late_flat.take(joined_late, 0, mine) + lax.dynamic_slice_in_dim(early_sum, mine * dec_shard, dec_shard)
    enc_one, enc_two, enc_new = adamw_update(params_enc, grad_enc, m_enc, v_enc, clip_scale)
    dec_one, dec_two, dec_new = adamw_update(
        params_dec, grad_dec.reshape(-1), m_dec, v_dec, clip_scale
    )
    return (loss_sum, masked_count, grad_norm, enc_one, enc_two, enc_new, dec_one, dec_two, dec_new)


def solution(mesh):
    placed = (P(AXES, None),) * 4 + (P("wide"),) * 6
    return jax.shard_map(
        functools.partial(body, Links(mesh)),
        mesh=mesh,
        in_specs=placed,
        out_specs=(P(), P(), P()) + (P("wide"),) * 6,
        check_vma=False,
    )
```

```python
import functools
import math

import jax
import jax.numpy as jnp
from jax import lax
from jax.experimental import pallas as pl
from jax.experimental.pallas import tpu as pltpu
from jax.sharding import PartitionSpec as P

D = 768
HEADS = 12
FF = 3072
DD = 384
DHEADS = 6
DFF = 1536
PIX = 1536
STEP = 10
ROWS = 2592

learn_rate = 0.05
BETA_ONE = 0.9
BETA_TWO = 0.95
EPSILON = 1e-08
weight_decay = 0.05
clip_norm = 0.05

F = jnp.float32
B = jnp.bfloat16
AXES = ("narrow", "wide")
NT = (((1,), (1,)), ((), ()))
NN = (((1,), (0,)), ((), ()))
TN = (((0,), (0,)), ((), ()))
VMEM_LIMIT = 60 << 20


def mm(left, right, dims=NN):
    return lax.dot_general(left, right, dims, preferred_element_type=F)


ENC_SHAPES = [
    (PIX, D), (D,), (D,), (D,), (D, 3 * D), (D,), (D,), (D, D), (D,), (D,), (D,),
    (D, FF), (FF,), (FF, D), (D,), (D,), (D,), (D, DD),
]
DEC_SHAPES = [
    (DD,), (DD,), (DD,), (DD, 3 * DD), (DD,), (DD,), (DD, DD), (DD,), (DD,), (DD,),
    (DD, DFF), (DFF,), (DFF, DD), (DD,), (DD,), (DD,), (DD, PIX), (PIX,),
]


def sinusoid(places, columns):
    half_width = columns // 2
    frequency = jnp.exp(jnp.arange(half_width, dtype=F) * (-math.log(10000.0) / half_width))
    angles = places[:, None] * frequency[None, :]
    return jnp.concatenate([jnp.sin(angles), jnp.cos(angles)], axis=1)


def layout(lengths, visible, row_count):
    positions = jnp.arange(row_count, dtype=jnp.int32)
    clip_ends = jnp.cumsum(lengths)
    starts = clip_ends - lengths
    segment = jnp.sum((positions[:, None] >= clip_ends[None, :]).astype(jnp.int32), axis=1)
    member = segment[:, None] == jnp.arange(3, dtype=jnp.int32)[None, :]
    clip_begin = jnp.sum(jnp.where(member, starts[None, :], 0), axis=1)
    clip_place = (positions - clip_begin).astype(F)
    pack_total = clip_ends[2]
    slot_live = (visible < pack_total).astype(F)
    shown_flag = jnp.zeros((row_count,), F).at[visible].add(slot_live)
    counted = jnp.where(positions < pack_total, 1.0 - shown_flag, 0.0)
    return (segment, clip_place, slot_live, shown_flag, counted)


def slot_layout(lengths, visible):
    clip_ends = jnp.cumsum(lengths)
    starts = clip_ends - lengths
    segment = jnp.sum((visible[:, None] >= clip_ends[None, :]).astype(jnp.int32), axis=1)
    member = segment[:, None] == jnp.arange(3, dtype=jnp.int32)[None, :]
    clip_begin = jnp.sum(jnp.where(member, starts[None, :], 0), axis=1)
    return segment, (visible - clip_begin).astype(F)


def norm_rows(x):
    center = x - jnp.mean(x, axis=1, keepdims=True)
    inverse = lax.rsqrt(jnp.mean(center * center, axis=1, keepdims=True) + 1e-06)
    return center * inverse, inverse


def norm_back(grad, hat, inverse):
    return inverse * (
        grad
        - jnp.mean(grad, axis=1, keepdims=True)
        - hat * jnp.mean(grad * hat, axis=1, keepdims=True)
    )


def total(x):
    return jnp.sum(x, axis=0, keepdims=True)


def low_lanes(rows):
    return lax.broadcasted_iota(jnp.int32, (rows, 128), 1) < 64


def low_rows(columns):
    return lax.broadcasted_iota(jnp.int32, (128, columns), 0) < 64


def halves(low, value, other):
    return jnp.where(low, value, other), jnp.where(low, other, value)


def softmax_keys(s):
    m = jnp.max(s, axis=0, keepdims=True)
    e = jnp.exp(s - m)
    l = jnp.sum(e, axis=0, keepdims=True)
    return e * (1.0 / l), m + jnp.log(l)


def qkv_kernel(vis_ref, live_ref, latent_ref, place_ref, row_ref, w_ref, vec_ref, mask_ref, x_ref, o_ref):
    x_ref[...] = place_ref[...] + row_ref[:, 2:3] * mask_ref[0:1, :DD]

    def add_slot(i, carry):
        at = pl.ds(jnp.minimum(vis_ref[i], ROWS - 1), 1)
        x_ref[at, :] += latent_ref[pl.ds(i, 1), :] * live_ref[i]
        return carry

    lax.fori_loop(0, latent_ref.shape[0], add_slot, 0, unroll=8)
    bm = 432

    def block(i, carry):
        part = pl.ds(pl.multiple_of(i * bm, 16), bm)
        hat, inverse = norm_rows(x_ref[part, :])
        normed = (hat * vec_ref[0:1, :DD] + vec_ref[1:2, :DD]).astype(B)
        o_ref[part, :] = (mm(normed, w_ref[...]) + vec_ref[2:3, :]).astype(B)
        return carry

    lax.fori_loop(0, ROWS // bm, block, 0)


def qkv_forward(visible, live, latent, places, rows, w, vec, mask):
    smem, vmem = pl.BlockSpec(memory_space=pltpu.SMEM), pl.BlockSpec(memory_space=pltpu.VMEM)
    return pl.pallas_call(
        qkv_kernel,
        in_specs=[smem] * 2 + [vmem] * 6,
        out_specs=[vmem] * 2,
        out_shape=[jax.ShapeDtypeStruct((ROWS, DD), F), jax.ShapeDtypeStruct((ROWS, 3 * DD), B)],
        compiler_params=pltpu.CompilerParams(vmem_limit_bytes=VMEM_LIMIT),
        cost_estimate=pl.CostEstimate(flops=10 * 10**9, bytes_accessed=16 << 20, transcendentals=0),
        name="dec_qkv",
    )(visible, live, latent, places, rows, w, vec, mask)


def attend_kernel(q_ref, k_ref, v_ref, qf_ref, kf_ref, o_ref, lse_ref, k0, k1):
    rows, bq = k_ref.shape[0], q_ref.shape[0]

    @pl.when(pl.program_id(1) == 0)
    def _():
        k0[...], k1[...] = halves(low_lanes(rows), k_ref[...], kf_ref[...])

    qs = halves(low_lanes(bq), q_ref[...] * jnp.asarray(0.125, B), qf_ref[...])
    scores = [mm(keys[...], q, NT) for keys, q in zip((k0, k1), qs)]
    outs, logs = [], []
    for s in scores:
        p, log = softmax_keys(s)
        outs.append(mm(v_ref[...], p.astype(B), TN))
        logs.append(log)
    o_ref[...] = jnp.where(low_rows(bq), outs[0], outs[1]).T.astype(B)
    lse_ref[0] = jnp.concatenate(logs + [jnp.zeros((6, bq), F)], axis=0)


def attend_forward(qkv, qf, kf, bq=864):
    nq = ROWS // bq
    return pl.pallas_call(
        attend_kernel,
        grid=(3, nq),
        in_specs=[
            pl.BlockSpec((bq, 128), lambda h, i: (i, h)),
            pl.BlockSpec((ROWS, 128), lambda h, i: (0, 3 + h)),
            pl.BlockSpec((ROWS, 128), lambda h, i: (0, 6 + h)),
            pl.BlockSpec((bq, 128), lambda h, i: (i, 0)),
            pl.BlockSpec((ROWS, 128), lambda h, i: (0, 0)),
        ],
        out_specs=[
            pl.BlockSpec((bq, 128), lambda h, i: (i, h)),
            pl.BlockSpec((1, 8, bq), lambda h, i: (h * nq + i, 0, 0)),
        ],
        out_shape=[
            jax.ShapeDtypeStruct((ROWS, DD), B),
            jax.ShapeDtypeStruct((3 * nq, 8, bq), F),
        ],
        scratch_shapes=[pltpu.VMEM((ROWS, 128), B)] * 2,
        compiler_params=pltpu.CompilerParams(vmem_limit_bytes=VMEM_LIMIT),
        cost_estimate=pl.CostEstimate(flops=60 * 10**9, bytes_accessed=16 << 20, transcendentals=0),
        name="dec_attend",
    )(qkv, qkv, qkv, qf, kf)


def attend_back_kernel(
    h, kc, q_ref, k_ref, v_ref, qf_ref, kf_ref, da_ref, lse_ref, dd_ref, dq_ref, dk_ref, dv_ref,
    k0, k1, z0, z1, dk_sum, dv_sum,
):
    rows, bq = k_ref.shape[0], q_ref.shape[0]
    step = pl.program_id(0)

    @pl.when(step == 0)
    def _():
        low, keys = low_lanes(rows), k_ref[...]
        k0[...], k1[...] = halves(low, keys, kf_ref[...])
        z0[...], z1[...] = halves(low, keys, jnp.zeros_like(keys))
        dk_sum[...] = jnp.zeros_like(dk_sum)
        dv_sum[...] = jnp.zeros_like(dv_sum)

    low = low_lanes(bq)
    q, da = q_ref[...] * jnp.asarray(0.125, B), da_ref[...]
    zero = jnp.zeros_like(q)
    qs = halves(low, q, qf_ref[...])
    dz = halves(low, da, zero)
    q_both, d_both = jnp.concatenate(halves(low, q, zero), axis=0), jnp.concatenate(dz, axis=0)
    mean = jnp.concatenate([dd_ref[i] for i in range(dd_ref.shape[0])], axis=1)
    dq = jnp.zeros((128, bq), F)
    for c in range(rows // kc):
        part = slice(c * kc, (c + 1) * kc)
        scores = [mm(keys[part, :], q, NT) for keys, q in zip((k0, k1), qs)]
        dps = [mm(v_ref[part, :], d, NT) for d in dz]
        ps, dss = [], []
        for i in range(2):
            p = jnp.exp(scores[i] - lse_ref[0, i : i + 1, :])
            ps.append(p.astype(B))
            dss.append((p * (dps[i] - mean[2 * h + i : 2 * h + i + 1, :])).astype(B))
        dv_sum[part, :] += mm(jnp.concatenate(ps, axis=1), d_both)
        dk_sum[part, :] += mm(jnp.concatenate(dss, axis=1), q_both)
        for z, ds in zip((z0, z1), dss):
            dq += mm(z[part, :], ds, TN)
    dq_ref[...] = (dq.T * 0.125).astype(B)

    @pl.when(step == pl.num_programs(0) - 1)
    def _():
        dk_ref[...] = dk_sum[...].astype(B)
        dv_ref[...] = dv_sum[...].astype(B)


def attend_back(qkv, qf, kf, da, lse, dd, h, bq=864, kc=864):
    nq = ROWS // bq
    many = bq // dd.shape[2]
    return pl.pallas_call(
        functools.partial(attend_back_kernel, h, kc),
        grid=(nq,),
        in_specs=[
            pl.BlockSpec((bq, 128), lambda i: (i, h)),
            pl.BlockSpec((ROWS, 128), lambda i: (0, 3 + h)),
            pl.BlockSpec((ROWS, 128), lambda i: (0, 6 + h)),
            pl.BlockSpec((bq, 128), lambda i: (i, 0)),
            pl.BlockSpec((ROWS, 128), lambda i: (0, 0)),
            pl.BlockSpec((bq, 128), lambda i: (i, h)),
            pl.BlockSpec((1, 8, bq), lambda i: (h * nq + i, 0, 0)),
            pl.BlockSpec((many, 8, bq // many), lambda i: (i, 0, 0)),
        ],
        out_specs=[
            pl.BlockSpec((bq, 128), lambda i: (i, 0)),
            pl.BlockSpec((ROWS, 128), lambda i: (0, 0)),
            pl.BlockSpec((ROWS, 128), lambda i: (0, 0)),
        ],
        out_shape=[jax.ShapeDtypeStruct((ROWS, 128), B)] * 3,
        scratch_shapes=[pltpu.VMEM((ROWS, 128), B)] * 4 + [pltpu.VMEM((ROWS, 128), F)] * 2,
        compiler_params=pltpu.CompilerParams(vmem_limit_bytes=VMEM_LIMIT),
        cost_estimate=pl.CostEstimate(flops=40 * 10**9, bytes_accessed=8 << 20, transcendentals=0),
        name="dec_attend_back",
    )(qkv, qkv, qkv, qf, kf, da, lse, dd)


def mlp_kernel(
    x_ref, a_ref, t_ref, row_ref, wo_ref, wu_ref, wd_ref, wh_ref, vec_ref,
    da_ref, dx_ref, dd_ref, go_ref, gu_ref, gd_ref, gh_ref, gv_ref,
):
    @pl.when(pl.program_id(0) == 0)
    def _():
        for ref in (go_ref, gu_ref, gd_ref, gh_ref, gv_ref):
            ref[...] = jnp.zeros_like(ref)

    a = a_ref[...]
    x1 = x_ref[...] + mm(a, wo_ref[...]) + vec_ref[0:1, :DD]
    hat2, inv2 = norm_rows(x1)
    n2 = (hat2 * vec_ref[1:2, :DD] + vec_ref[2:3, :DD]).astype(B)
    h = mm(n2, wu_ref[...]) + vec_ref[3:4, :]
    cdf = 0.5 * (1.0 + lax.erf(h * (1.0 / math.sqrt(2.0))))
    u = (h * cdf).astype(B)
    slope = cdf + h * jnp.exp(-0.5 * h * h) * (1.0 / math.sqrt(2.0 * math.pi))
    x2 = x1 + mm(u, wd_ref[...]) + vec_ref[4:5, :DD]
    hatf, invf = norm_rows(x2)
    nf = (hatf * vec_ref[5:6, :DD] + vec_ref[6:7, :DD]).astype(B)
    pred = mm(nf, wh_ref[...]) + vec_ref[7:8, :]
    goal, unused = norm_rows(t_ref[...].astype(F))
    err = pred - goal
    gv_ref[8:9, :] += total(err * err * row_ref[:, 0:1])
    dpred = err * row_ref[:, 1:2]
    gv_ref[7:8, :] += total(dpred)
    dpred = dpred.astype(B)
    gh_ref[...] += mm(nf, dpred, TN)
    dnf = mm(dpred, wh_ref[...], NT)
    gv_ref[5:6, :DD] += total(dnf * hatf)
    gv_ref[6:7, :DD] += total(dnf)
    dx2 = norm_back(dnf * vec_ref[5:6, :DD], hatf, invf)
    gv_ref[4:5, :DD] += total(dx2)
    dx2b = dx2.astype(B)
    gd_ref[...] += mm(u, dx2b, TN)
    dh = mm(dx2b, wd_ref[...], NT) * slope
    gv_ref[3:4, :] += total(dh)
    dh = dh.astype(B)
    gu_ref[...] += mm(n2, dh, TN)
    dn2 = mm(dh, wu_ref[...], NT)
    gv_ref[1:2, :DD] += total(dn2 * hat2)
    gv_ref[2:3, :DD] += total(dn2)
    dx1 = dx2 + norm_back(dn2 * vec_ref[1:2, :DD], hat2, inv2)
    gv_ref[0:1, :DD] += total(dx1)
    dx_ref[...] = dx1
    dx1 = dx1.astype(B)
    go_ref[...] += mm(a, dx1, TN)
    da = mm(dx1, wo_ref[...], NT).astype(B)
    da_ref[...] = da
    head_of = lax.broadcasted_iota(jnp.int32, (8, DD), 1) // 64
    pick = (head_of == lax.broadcasted_iota(jnp.int32, (8, DD), 0)).astype(F)
    dd_ref[0] = lax.dot_general(
        pick, da.astype(F) * a.astype(F), NT, precision=lax.Precision.HIGHEST, preferred_element_type=F
    )


def mlp_both(x, a, target, rows, wo, wu, wd, wh, vec, bm=432):
    full = lambda shape: pl.BlockSpec(shape, lambda i: (0, 0))
    part = lambda width: pl.BlockSpec((bm, width), lambda i: (i, 0))
    sums = [wo.shape, wu.shape, wd.shape, wh.shape, vec.shape]
    return pl.pallas_call(
        mlp_kernel,
        grid=(ROWS // bm,),
        in_specs=[part(DD), part(DD), part(PIX), part(128)]
        + [full(w.shape) for w in (wo, wu, wd, wh, vec)],
        out_specs=[part(DD), part(DD), pl.BlockSpec((1, 8, bm), lambda i: (i, 0, 0))] + [full(s) for s in sums],
        out_shape=[
            jax.ShapeDtypeStruct((ROWS, DD), B),
            jax.ShapeDtypeStruct((ROWS, DD), F),
            jax.ShapeDtypeStruct((ROWS // bm, 8, bm), F),
        ]
        + [jax.ShapeDtypeStruct(s, F) for s in sums],
        compiler_params=pltpu.CompilerParams(vmem_limit_bytes=VMEM_LIMIT),
        name="dec_mlp",
    )(x, a, target, rows, wo, wu, wd, wh, vec)


def qkv_back_kernel(x_ref, dx_ref, *refs):
    parts, (row_ref, w_ref, vec_ref, o_ref, g_ref, gv_ref) = refs[:9], refs[9:]

    @pl.when(pl.program_id(0) == 0)
    def _():
        for ref in (g_ref, gv_ref):
            ref[...] = jnp.zeros_like(ref)

    hat, inverse = norm_rows(x_ref[...])
    normed = (hat * vec_ref[0:1, :DD] + vec_ref[1:2, :DD]).astype(B)
    dp = jnp.concatenate([parts[3 * h + i][...] for i in range(3) for h in range(3)], axis=1)
    g_ref[...] += mm(normed, dp, TN)
    dn = mm(dp, w_ref[...], NT)
    gv_ref[2:3, :] += total(dp.astype(F))
    gv_ref[0:1, :DD] += total(dn * hat)
    gv_ref[1:2, :DD] += total(dn)
    dx = dx_ref[...] + norm_back(dn * vec_ref[0:1, :DD], hat, inverse)
    o_ref[...] = dx
    gv_ref[3:4, :DD] += total(dx * row_ref[:, 2:3])


def qkv_back(x, dx, dqkv, rows, w, vec, bm=432):
    full = lambda shape: pl.BlockSpec(shape, lambda i: (0, 0))
    part = lambda width: pl.BlockSpec((bm, width), lambda i: (i, 0))
    return pl.pallas_call(
        qkv_back_kernel,
        grid=(ROWS // bm,),
        in_specs=[part(DD)] * 2 + [part(128)] * 10 + [full(w.shape), full(vec.shape)],
        out_specs=[part(DD), full(w.shape), full(vec.shape)],
        out_shape=[
            jax.ShapeDtypeStruct((ROWS, DD), F),
            jax.ShapeDtypeStruct(w.shape, F),
            jax.ShapeDtypeStruct(vec.shape, F),
        ],
        compiler_params=pltpu.CompilerParams(vmem_limit_bytes=VMEM_LIMIT),
        cost_estimate=pl.CostEstimate(flops=15 * 10**9, bytes_accessed=8 << 20, transcendentals=0),
        name="dec_qkv_back",
    )(x, dx, *[part for head in dqkv for part in head], rows, w, vec)


def stack_rows(pieces, width, count=8):
    rows = [jnp.pad(p.astype(F), (0, width - p.shape[0])) for p in pieces]
    rows += [jnp.zeros((width,), F)] * (count - len(rows))
    return jnp.stack(rows)


def gelu_parts(h):
    cdf = 0.5 * (1.0 + lax.erf(h * (1.0 / math.sqrt(2.0))))
    return cdf, cdf + h * jnp.exp(-0.5 * h * h) * (1.0 / math.sqrt(2.0 * math.pi))


def enc_pair(qkv_ref, marks, j):
    q, k, v = (qkv_ref[:, i * D + j * 128 : i * D + (j + 1) * 128] for i in range(3))
    q = q * jnp.asarray(0.125, B)
    low = low_lanes(q.shape[0])
    return q, k, v, halves(low, q, marks[0]), halves(low, k, marks[1])


def enc_forward_kernel(
    pix_ref, place_ref, qm_ref, km_ref, vec_ref, we_hbm, wq_hbm, wo_hbm, wu_hbm, wd_hbm, wp_hbm,
    latent_ref, e0_ref, qkv_ref, a_ref, x1_ref, h_ref, x2_ref,
    we, wq, wo, wu, wd, wp, sems,
):
    loads = [
        pltpu.make_async_copy(source, target, sems.at[i])
        for i, (source, target) in enumerate(
            zip((we_hbm, wq_hbm, wo_hbm, wu_hbm, wd_hbm, wp_hbm), (we, wq, wo, wu, wd, wp))
        )
    ]
    for load in loads:
        load.start()
    loads[0].wait()
    e0 = mm(pix_ref[...], we[...]) + vec_ref[0:1, :D] + place_ref[...]
    e0_ref[...] = e0
    hat, unused = norm_rows(e0)
    n1 = (hat * vec_ref[1:2, :D] + vec_ref[2:3, :D]).astype(B)
    loads[1].wait()
    for i, bias in enumerate((vec_ref[3:4, :D], 0.0, vec_ref[4:5, :D])):
        part = slice(i * D, (i + 1) * D)
        qkv_ref[:, part] = (mm(n1, wq[:, part]) + bias).astype(B)
    marks = (qm_ref[...], km_ref[...])
    for j in range(HEADS // 2):
        unused, unused, v, qs, ks = enc_pair(qkv_ref, marks, j)
        scores = [mm(ks[i], qs[i], NT) for i in range(2)]
        outs = [mm(v, softmax_keys(s)[0].astype(B), TN) for s in scores]
        a_ref[:, j * 128 : (j + 1) * 128] = jnp.where(low_rows(v.shape[0]), outs[0], outs[1]).T.astype(B)
    loads[2].wait()
    x1 = e0 + mm(a_ref[...], wo[...]) + vec_ref[5:6, :D]
    x1_ref[...] = x1
    hat, unused = norm_rows(x1)
    n2 = (hat * vec_ref[6:7, :D] + vec_ref[7:8, :D]).astype(B)
    loads[3].wait()
    loads[4].wait()
    x2 = x1 + vec_ref[9:10, :D]
    for i in range(4):
        part = slice(i * D, (i + 1) * D)
        h = mm(n2, wu[:, part]) + vec_ref[8:9, part]
        h_ref[:, part] = h
        x2 += mm((h * gelu_parts(h)[0]).astype(B), wd[part, :])
    x2_ref[...] = x2
    hat, unused = norm_rows(x2)
    loads[5].wait()
    latent_ref[...] = mm((hat * vec_ref[10:11, :D] + vec_ref[11:12, :D]).astype(B), wp[...])


def enc_forward(pixels, places, q_marks, k_marks, vec, mats):
    rows = pixels.shape[0]
    hbm, vmem = pl.BlockSpec(memory_space=pl.ANY), pl.BlockSpec(memory_space=pltpu.VMEM)
    outs = [(DD, F), (D, F), (3 * D, B), (D, B), (D, F), (FF, F), (D, F)]
    return pl.pallas_call(
        enc_forward_kernel,
        in_specs=[vmem] * 5 + [hbm] * 6,
        out_specs=[vmem] * 7,
        out_shape=[jax.ShapeDtypeStruct((rows, width), kind) for width, kind in outs],
        scratch_shapes=[pltpu.VMEM(m.shape, B) for m in mats] + [pltpu.SemaphoreType.DMA((6,))],
        compiler_params=pltpu.CompilerParams(vmem_limit_bytes=VMEM_LIMIT),
        cost_estimate=pl.CostEstimate(flops=15 * 10**9, bytes_accessed=20 << 20, transcendentals=0),
        name="enc_forward",
    )(pixels, places, q_marks, k_marks, vec, *mats)


def put_product(lin, top, row, left, right):
    m, c = left.shape[0], right.shape[1] // 128
    step = min(m, 768)
    most = top[...]
    for r in range(0, m, step):
        for first in range(0, c, 2):
            last = min(first + 2, c)
            value = mm(left[r : r + step, :], right[:, first * 128 : last * 128])
            for i in range(first, last):
                piece = value[:, (i - first) * 128 : (i - first + 1) * 128]
                lin[pl.ds(row + r * c + i, step, stride=c), :] = piece
                most = jnp.maximum(most, jnp.max(jnp.abs(piece).reshape(-1, 8, 128), axis=0))
    top[...] = most


def put_vector(lin, top, row, value):
    for i in range(value.shape[1] // 128):
        piece = value[:, i * 128 : (i + 1) * 128]
        lin[pl.ds(row + i, 1), :] = piece
        top[0:1, :] = jnp.maximum(top[0:1, :], jnp.abs(piece))


def turned(value):
    return value.astype(F).T.astype(B)


def flush_start(lin, base, segments, core, kept, away, sem):
    for c in range(2):

        @pl.when(core == c)
        def _():
            for source, count, s, h, k, y, to in segments:
                target = (kept if h == c else away)[k]
                pltpu.make_async_copy(
                    lin.at[pl.ds(source - base, count)], target.at[s, y, pl.ds(to, count)], sem
                ).start()


def flush_wait(lin, segments, sem):
    count = sum(segment[1] for segment in segments)
    pltpu.make_async_copy(lin.at[pl.ds(0, count)], lin.at[pl.ds(0, count)], sem).wait()


def enc_back_one_kernel(
    base, rows_of, cuts, core_ref, vis_ref, live_ref, dx0_ref, x1_ref, h_ref, x2_ref, vec_ref, wu_hbm, wd_hbm, wp_hbm,
    dx1_ref, top_ref, *refs,
):
    chunks = (len(refs) - 7) // 2
    kept, away = refs[:chunks], refs[chunks : 2 * chunks]
    lin, wu, wd, wp, dl_ref, dh_ref, sems = refs[-7:]
    loads = [
        pltpu.make_async_copy(source, target, sems.at[i])
        for i, (source, target) in enumerate(zip((wp_hbm, wd_hbm, wu_hbm), (wp, wd, wu)))
    ]
    for load in loads:
        load.start()
    top_ref[...] = jnp.zeros_like(top_ref)
    upb, down, db, fg, fb, proj, end, last = (r - base for r in rows_of[1:])

    def take_slot(i, carry):
        at = pl.ds(jnp.minimum(vis_ref[i], ROWS - 1), 1)
        dl_ref[pl.ds(i, 1), :] = dx0_ref[at, :] * live_ref[i]
        return carry

    lax.fori_loop(0, dl_ref.shape[0], take_slot, 0, unroll=8)
    dl = dl_ref[...].astype(B)
    hatf, invf = norm_rows(x2_ref[...])
    put_product(lin, top_ref, proj, turned(hatf * vec_ref[10:11, :D] + vec_ref[11:12, :D]), dl)
    lin[pl.ds(end, lin.shape[0] - end), :] = jnp.zeros((lin.shape[0] - end, 128), F)
    loads[0].wait()
    dnf = mm(dl, wp[...], NT)
    put_vector(lin, top_ref, fg, total(dnf * hatf))
    put_vector(lin, top_ref, fb, total(dnf))
    dx2 = norm_back(dnf * vec_ref[10:11, :D], hatf, invf)
    put_vector(lin, top_ref, db, total(dx2))
    dx2b = dx2.astype(B)
    loads[1].wait()
    for i in range(4):
        part = slice(i * D, (i + 1) * D)
        h = h_ref[:, part]
        kept_share, slope = gelu_parts(h)
        put_product(lin, top_ref, down + i * D * (D // 128), turned(h * kept_share), dx2b)
        dh = mm(dx2b, wd[part, :], NT) * slope
        put_vector(lin, top_ref, upb + i * (D // 128), total(dh))
        dh_ref[:, part] = dh.astype(B)
    flush_start(lin, base, cuts[0], core_ref[0], kept, away, sems.at[3])
    loads[2].wait()
    hat2, inv2 = norm_rows(x1_ref[...])
    put_product(lin, top_ref, 0, turned(hat2 * vec_ref[6:7, :D] + vec_ref[7:8, :D]), dh_ref[...])
    flush_start(lin, base, cuts[1], core_ref[0], kept, away, sems.at[4])
    dn2 = mm(dh_ref[...], wu[...], NT)
    dx1_ref[0:1, :] = jnp.zeros((1, D), F)
    dx1 = dx2 + norm_back(dn2 * vec_ref[6:7, :D], hat2, inv2)
    count = dx1.shape[0]
    dx1_ref[0:count, :] = dx1
    dx1_ref[count : count + 1, :] = total(dn2 * hat2)
    dx1_ref[count + 1 : count + 2, :] = total(dn2)
    flush_wait(lin, cuts[0], sems.at[3])
    flush_wait(lin, cuts[1], sems.at[4])


def enc_back_two_kernel(
    rows_of, early_of, base_early, cuts, core_ref, dx1_ref, pix_ref, e0_ref, qkv_ref, a_ref, qm_ref, km_ref, vec_ref,
    g_qkv_ref, g_one_ref, wq_hbm, wo_hbm, top_in, *refs,
):
    chunks = (len(refs) - 6) // 4
    top_ref = refs[2 * chunks]
    kept, away = refs[2 * chunks + 1 : 3 * chunks + 1], refs[3 * chunks + 1 : 4 * chunks + 1]
    lin, wq, wo, dp_ref, sems = refs[-5:]
    loads = [
        pltpu.make_async_copy(source, target, sems.at[i])
        for i, (source, target) in enumerate(zip((wo_hbm, wq_hbm), (wo, wq)))
    ]
    for load in loads:
        load.start()
    top_ref[...] = top_in[...]
    embed, eb, g1, b1, qkv, qbias, vbias, out, ob, g2, b2 = rows_of
    count = pix_ref.shape[0]
    dx1 = dx1_ref[0:count, :]
    put_vector(lin, top_ref, g2, dx1_ref[count : count + 1, :])
    put_vector(lin, top_ref, b2, dx1_ref[count + 1 : count + 2, :])
    put_vector(lin, top_ref, ob, total(dx1))
    dx1b = dx1.astype(B)
    put_product(lin, top_ref, out, turned(a_ref[...]), dx1b)
    loads[0].wait()
    da = mm(dx1b, wo[...], NT).astype(B)
    marks = (qm_ref[...], km_ref[...])
    for j in range(HEADS // 2):
        q, k, v, qs, ks = enc_pair(qkv_ref, marks, j)
        low, zero = low_lanes(count), jnp.zeros_like(q)
        dz = halves(low, da[:, j * 128 : (j + 1) * 128], zero)
        scores = [mm(ks[i], qs[i], NT) for i in range(2)]
        dps = [mm(v, d, NT) for d in dz]
        ps, dss, dq = [], [], jnp.zeros((128, count), F)
        for i, keys in enumerate(halves(low, k, zero)):
            p = softmax_keys(scores[i])[0]
            ps.append(p.astype(B))
            dss.append((p * (dps[i] - jnp.sum(p * dps[i], axis=0, keepdims=True))).astype(B))
            dq += mm(keys, dss[i], TN)
        dk = mm(jnp.concatenate(dss, axis=1), jnp.concatenate(halves(low, q, zero), axis=0))
        dv = mm(jnp.concatenate(ps, axis=1), jnp.concatenate(dz, axis=0))
        for i, value in enumerate((dq.T * 0.125, dk, dv)):
            dp_ref[:, i * D + j * 128 : i * D + (j + 1) * 128] = value.astype(B)
    dp = dp_ref[...]
    sums = total(dp.astype(F))
    put_vector(lin, top_ref, qbias, sums[:, :D])
    put_vector(lin, top_ref, vbias, sums[:, 2 * D :])
    hat, inverse = norm_rows(e0_ref[...])
    put_product(lin, top_ref, qkv, turned(hat * vec_ref[1:2, :D] + vec_ref[2:3, :D]), dp)
    loads[1].wait()
    dn = mm(dp, wq[...], NT)
    put_vector(lin, top_ref, g1, total(dn * hat))
    put_vector(lin, top_ref, b1, total(dn))
    de0 = dx1 + norm_back(dn * vec_ref[1:2, :D], hat, inverse)
    put_vector(lin, top_ref, eb, total(de0))
    flush_start(lin, 0, cuts[0], core_ref[0], kept, away, sems.at[2])
    put_product(lin, top_ref, embed, turned(pix_ref[...]), de0.astype(B))
    c = g_qkv_ref.shape[1] // 128
    start = early_of[3]
    most = top_ref[...]
    for i in range(c):
        piece = g_qkv_ref[:, i * 128 : (i + 1) * 128]
        lin[pl.ds(start + i, g_qkv_ref.shape[0], stride=c), :] = piece
        most = jnp.maximum(most, jnp.max(jnp.abs(piece).reshape(-1, 8, 128), axis=0))
    top_ref[...] = most
    one = g_one_ref
    for row, value in zip(
        early_of[:3] + early_of[4:6],
        (one[3:4, :DD], one[0:1, :DD], one[1:2, :DD], one[2:3, :DD], one[2:3, 2 * DD :]),
    ):
        put_vector(lin, top_ref, row, value)
    end = early_of[6]
    lin[pl.ds(end, lin.shape[0] - end), :] = jnp.zeros((lin.shape[0] - end, 128), F)
    flush_start(lin, 0, cuts[1], core_ref[0], kept, away, sems.at[3])
    flush_start(lin, base_early, cuts[2], core_ref[0], kept, away, sems.at[4])
    for i in range(3):
        flush_wait(lin, cuts[i], sems.at[2 + i])


class Flat:
    def __init__(self, sections, wide, narrow, chunks):
        self.wide, self.narrow, self.sections = wide, narrow, sections
        self.spans = [-(-(rows + (0 if rows % 8 == 0 else 7)) // 8) * 8 for unused, rows in sections]
        self.parts = [-(-span // (narrow * 16)) * 16 for span in self.spans]
        self.starts = [sum(self.parts[i + 1 :]) for i in range(len(sections))]
        rows = sum(self.parts)
        step = -(-rows // (chunks * 16)) * 16
        self.chunks = [min(step, rows - i * step) for i in range(chunks)]
        self.shapes = [jax.ShapeDtypeStruct((wide, narrow // 2, count, 128), F) for count in self.chunks]

    def segments(self, section, low, high):
        first, rows = self.sections[section]
        part, span, at = self.parts[section], self.spans[section], self.starts[section]
        out = []
        for s in range(self.wide):
            start = first + s * rows // 8 * 8
            for p in range(self.narrow):
                begin = 0
                for k, count in enumerate(self.chunks):
                    lead = start + p * part - at + begin
                    a = max(low, start + p * part, lead)
                    b = min(high, start + span, start + (p + 1) * part, lead + count)
                    if a < b:
                        out.append((a, b - a, s, p // 2, k, p % 2, a - lead))
                    begin += count
        return out

    def reach(self, section):
        first, rows = self.sections[section]
        return first + (self.wide - 1) * rows // 8 * 8 + self.spans[section]

    def offset(self, section, index):
        return lax.rem(index * self.sections[section][1], 8)

    def of(self, piece, section):
        return piece[self.starts[section] : self.starts[section] + self.parts[section]]

    def squares(self, piece, section, index, part):
        value = self.of(piece, section)
        row = part * self.parts[section] + jnp.arange(value.shape[0], dtype=jnp.int32)[:, None]
        at = self.offset(section, index)
        inside = (row >= at) & (row < at + self.sections[section][1])
        return jnp.sum(jnp.where(inside, value * value, 0.0))

    def take(self, window, section, index):
        return lax.dynamic_slice_in_dim(window, self.offset(section, index), self.sections[section][1])


def enc_back_one(core, visible, live, dx0, saved, vec, mats, flat):
    x1, h, x2 = saved[3:]
    wu, wd, wp = mats[3:]
    rows = x1.shape[0]
    pieces = [p[0] for p in table(ENC_SHAPES)]
    end = pieces[-1] + DD // 128 * D
    total_rows = flat.sections[0][1] * flat.wide
    reach = max(flat.reach(0), total_rows)
    rows_of = tuple(pieces[11:]) + (end, reach)
    base, split = pieces[11], pieces[13]
    smem, vmem, hbm = (
        pl.BlockSpec(memory_space=space) for space in (pltpu.SMEM, pltpu.VMEM, pl.ANY)
    )
    top = jax.ShapeDtypeStruct((8, 128), F)
    cuts = (flat.segments(0, split, reach), flat.segments(0, base, split))
    room = max([reach - base] + [sum(seg[1] for seg in cut) for cut in cuts])
    chunks = len(flat.chunks)
    dx1, top, *out = pl.pallas_call(
        functools.partial(enc_back_one_kernel, base, rows_of, cuts),
        in_specs=[smem] * 3 + [vmem] * 5 + [hbm] * 3,
        out_specs=[vmem] * 2 + [hbm] * (2 * chunks),
        out_shape=[jax.ShapeDtypeStruct((rows + 8, D), F), top] + flat.shapes * 2,
        scratch_shapes=[
            pltpu.VMEM((room, 128), F), pltpu.VMEM(wu.shape, B), pltpu.VMEM(wd.shape, B),
            pltpu.VMEM(wp.shape, B), pltpu.VMEM((rows, DD), F),
            pltpu.VMEM((rows, FF), B), pltpu.SemaphoreType.DMA((5,)),
        ],
        compiler_params=pltpu.CompilerParams(vmem_limit_bytes=VMEM_LIMIT),
        cost_estimate=pl.CostEstimate(flops=20 * 10**9, bytes_accessed=30 << 20, transcendentals=0),
        name="enc_back_one",
    )(core, visible, live, dx0, x1, h, x2, vec, wu, wd, wp)
    return dx1, top, out


def enc_back_two(core, dx1, top, out, saved, pixels, marks, vec, mats, g_qkv, g_one, flat):
    e0, qkv, a = saved[:3]
    wq, wo = mats[1:3]
    rows = pixels.shape[0]
    pieces = [p[0] for p in table(ENC_SHAPES)]
    base = pieces[11]
    early_rows = table(DEC_SHAPES[:6])
    first = flat.sections[1][0]
    last = early_rows[-1][0] + early_rows[-1][2]
    early_of = tuple(base + p[0] for p in early_rows) + (base + last,)
    reach = max(flat.reach(1) - first, last)
    cuts = (
        flat.segments(0, pieces[1] // 8 * 8, base), flat.segments(0, 0, pieces[1] // 8 * 8),
        flat.segments(1, first, first + reach),
    )
    room = max([base + reach] + [sum(seg[1] for seg in cut) for cut in cuts])
    smem, vmem, hbm = (
        pl.BlockSpec(memory_space=space) for space in (pltpu.SMEM, pltpu.VMEM, pl.ANY)
    )
    chunks = len(flat.chunks)
    top, *out = pl.pallas_call(
        functools.partial(enc_back_two_kernel, tuple(pieces[:11]), early_of, first - base, cuts),
        in_specs=[smem] + [vmem] * 10 + [hbm] * 2 + [vmem] + [hbm] * (2 * chunks),
        out_specs=[vmem] + [hbm] * (2 * chunks),
        out_shape=[jax.ShapeDtypeStruct((8, 128), F)] + flat.shapes * 2,
        input_output_aliases={14 + i: 1 + i for i in range(2 * chunks)},
        scratch_shapes=[
            pltpu.VMEM((room, 128), F), pltpu.VMEM(wq.shape, B), pltpu.VMEM(wo.shape, B),
            pltpu.VMEM((rows, 3 * D), B), pltpu.SemaphoreType.DMA((5,)),
        ],
        compiler_params=pltpu.CompilerParams(vmem_limit_bytes=VMEM_LIMIT),
        cost_estimate=pl.CostEstimate(flops=15 * 10**9, bytes_accessed=30 << 20, transcendentals=0),
        name="enc_back_two",
    )(core, dx1, pixels, e0, qkv, a, *marks, vec, g_qkv, g_one, wq, wo, top, *out)
    return out[:chunks], out[chunks:], top


def table(shapes, row=0):
    out = []
    for s in shapes:
        m, c = (s[0], s[1] // 128) if len(s) == 2 else (1, s[0] // 128)
        out.append((row, m, c))
        row += m * c
    return out


def job_rows(m, c, most):
    return max(n for n in range(16, m + 1, 16) if m % n == 0 and n * c <= most)


def split_rows(shard, shares, note):
    out, place, first = [], 0, 0
    for i in range(len(shares) + 1):
        rows = shard * shares[i] / 100 if i < len(shares) else (shard - first) / 4
        rows = math.ceil(rows / 16) * 16
        used = rows - 1 if note and i == 0 else rows
        out.append((place, first, 4, rows, used))
        place, first = place + 4 * rows, first + 4 * used
    return out


def unpack_kernel(pieces, groups, leads, ways, span, wide, mine_ref, *refs):
    mats = [p for p in pieces if p[1] > 1]
    sources = [refs[4 * g : 4 * g + 4] for g in range(len(groups))]
    refs = refs[4 * len(groups) :]
    outs, vec_ref = refs[: len(mats)], refs[len(mats)]
    buf, lin, in_sem, out_sem = refs[len(mats) + 1 : len(mats) + 5]
    stages = refs[len(mats) + 5 :]
    bits = wide.bit_length()
    plans, size = [], 0
    for (place, first, parts, rows, used), lead in zip(groups, leads):
        plan = []
        for i in range(parts):
            a, b = first + i * used, min(first + (i + 1) * used, span)
            if a < b:
                plan.append((i // 2, i % 2, lead, rows, size, a, b - a))
                size += rows
        plans.append(plan)

    for g, (plan, (last, way)) in enumerate(zip(plans, ways)):
        for core in range(2):
            for side in range(2):

                @pl.when((mine_ref[0] == core) & (mine_ref[1 + g] == side))
                def _():
                    for s in range(wide):
                        for c, y, low, rows, to, at, count in plan:
                            index = [s >> (bits - 2 - j) & 1 for j in range(bits - 1)] + [y]
                            source = sources[g][2 * (c != core) + (index[last] != side)]
                            index = sum(index[j] << (len(way) - 1 - i) for i, j in enumerate(way))
                            pltpu.make_async_copy(
                                source.at[index, pl.ds(low, rows)], buf.at[s, pl.ds(to, rows)], in_sem.at[s]
                            ).start()

    for s in range(wide):
        pltpu.make_async_copy(buf.at[s, pl.ds(0, size)], buf.at[s, pl.ds(0, size)], in_sem.at[s]).wait()
        for plan in plans:
            for c, y, low, rows, to, at, count in plan:
                lin[pl.ds(s * span + at, count), :] = buf[s, pl.ds(to, rows), :].astype(F)[:count]

    vec_ref[...] = jnp.zeros_like(vec_ref)
    v = 0
    for row, m, c in pieces:
        if m == 1:
            for j in range(c):
                vec_ref[v : v + 1, j * 128 : (j + 1) * 128] = lin[pl.ds(row + j, 1), :]
            v += 1
    for k, (row, m, c) in enumerate(mats):
        stage, out = stages[k], outs[k]
        n = stage.shape[1]
        jobs = m // n

        def store(j, slot):
            return pltpu.make_async_copy(
                stage.at[slot], out.at[pl.ds(pl.multiple_of(j * n, 16), n)], out_sem.at[slot]
            )

        def job(j, carry):
            slot = lax.rem(j, 2)

            @pl.when(j >= 2)
            def _():
                store(j - 2, slot).wait()

            for i in range(c):
                rows = pl.ds(row + i + j * (n * c), n, stride=c)
                stage[slot, :, i * 128 : (i + 1) * 128] = lin[rows, :].astype(B)
            store(j, slot).start()
            return carry

        lax.fori_loop(0, jobs, job, 0)
        for j in range(max(jobs - 2, 0), jobs):
            store(j, j % 2).wait()


def unpack_flat(arrays, groups, leads, ways, mine, span, wide, shapes, name):
    pieces = table(shapes)
    mats = [s for s in shapes if len(s) == 2]
    vectors = [s for s in shapes if len(s) == 1]
    width = max(s[0] for s in vectors)
    count = -(-len(vectors) // 8) * 8
    hbm = pl.BlockSpec(memory_space=pl.ANY)
    stages = [pltpu.VMEM((2, job_rows(s[0], s[1] // 128, 1152), s[1]), B) for s in mats]
    room = groups[-1][0] + groups[-1][2] * groups[-1][3]
    return pl.pallas_call(
        functools.partial(unpack_kernel, pieces, groups, leads, ways, span, wide),
        in_specs=[pl.BlockSpec(memory_space=pltpu.SMEM)] + [hbm] * len(arrays),
        out_specs=[hbm] * len(mats) + [pl.BlockSpec(memory_space=pltpu.VMEM)],
        out_shape=[jax.ShapeDtypeStruct(s, B) for s in mats] + [jax.ShapeDtypeStruct((count, width), F)],
        scratch_shapes=[
            pltpu.VMEM((wide, room, 128), B), pltpu.VMEM((wide * span, 128), F),
            pltpu.SemaphoreType.DMA((wide,)), pltpu.SemaphoreType.DMA((2,)),
        ] + stages,
        compiler_params=pltpu.CompilerParams(vmem_limit_bytes=VMEM_LIMIT),
        cost_estimate=pl.CostEstimate(flops=0, bytes_accessed=wide * span * 1536, transcendentals=0),
        name=name,
    )(mine, *arrays)


def pack_kernel(pieces, segments, core_ref, *refs):
    mats = [p for p in pieces if p[1] > 1]
    ins, vec_ref = refs[: len(mats)], refs[len(mats)]
    top_ref, *out = refs[len(mats) + 1 : -2]
    kept, away = out[: len(out) // 2], out[len(out) // 2 :]
    lin, sem = refs[-2:]
    first, end = pieces[0][0], pieces[-1][0] + pieces[-1][1] * pieces[-1][2]
    lin[pl.ds(0, first), :] = jnp.zeros((first, 128), F)
    lin[pl.ds(end, lin.shape[0] - end), :] = jnp.zeros((lin.shape[0] - end, 128), F)
    top_ref[...] = jnp.zeros_like(top_ref)
    k, v = 0, 0
    for row, m, c in pieces:
        if m == 1:
            put_vector(lin, top_ref, row, vec_ref[v : v + 1, : c * 128])
            v += 1
            continue
        most = top_ref[...]
        for i in range(c):
            piece = ins[k][:, i * 128 : (i + 1) * 128]
            lin[pl.ds(row + i, m, stride=c), :] = piece
            most = jnp.maximum(most, jnp.max(jnp.abs(piece).reshape(-1, 8, 128), axis=0))
        top_ref[...] = most
        k += 1
    flush_start(lin, 0, segments, core_ref[0], kept, away, sem)
    flush_wait(lin, segments, sem)


def pack_late(mats, vectors, pieces, flat, core, name):
    hbm, vmem = pl.BlockSpec(memory_space=pl.ANY), pl.BlockSpec(memory_space=pltpu.VMEM)
    segments = flat.segments(0, 0, flat.reach(0))
    room = max(flat.reach(0), flat.wide * flat.sections[0][1], sum(seg[1] for seg in segments))
    chunks = len(flat.chunks)
    unused, *out = pl.pallas_call(
        functools.partial(pack_kernel, pieces, segments),
        in_specs=[pl.BlockSpec(memory_space=pltpu.SMEM)] + [vmem] * (len(mats) + 1),
        out_specs=[vmem] + [hbm] * (2 * chunks),
        out_shape=[jax.ShapeDtypeStruct((8, 128), F)] + flat.shapes * 2,
        scratch_shapes=[pltpu.VMEM((room, 128), F), pltpu.SemaphoreType.DMA],
        compiler_params=pltpu.CompilerParams(vmem_limit_bytes=VMEM_LIMIT),
        cost_estimate=pl.CostEstimate(flops=0, bytes_accessed=30 << 20, transcendentals=0),
        name=name,
    )(core, *mats, vectors)
    return out[:chunks], out[chunks:]


class Links:
    def __init__(self, mesh):
        self.narrow, self.wide = mesh.shape["narrow"], mesh.shape["wide"]
        self.wide_bits = [("wide", b) for b in reversed(range(self.wide.bit_length() - 1))]
        self.x, self.upper = self.wide_bits[-1], self.wide_bits[:-1]
        self.y, self.core = ("narrow", 1), ("narrow", 0)

    def mine(self, bit):
        return (lax.axis_index(bit[0]) >> bit[1]) & 1

    def swap(self, value, bit):
        mask = 1 << bit[1] if bit[0] == "wide" else self.wide << bit[1]
        pairs = [(i, i ^ mask) for i in range(self.narrow * self.wide)]
        return lax.ppermute(value, AXES, pairs)

    def everyone(self, value, bits):
        for bit in bits:
            value = value + self.swap(value, bit)
        return value

    def gather(self, value, order):
        group = Group(self, value, order)
        while group.order:
            group.step()
        return group.value

    def scatter_parts(self, kept, other, bound=None):
        axes = self.wide_bits + [self.y]
        parts, orders = [], [[self.x, self.y] + self.upper, [self.y, self.x] + self.upper]
        for i, (one, two) in enumerate(zip(kept, other)):
            one, two = (v.reshape((2,) * len(axes) + v.shape[2:]) for v in (one, two))
            parts.append(Part(self, one, two, axes, orders[i % 2], bound))
        return parts


class Group:
    def __init__(self, links, value, order):
        self.links, self.value, self.order, self.have = links, value, list(order), []

    def step(self):
        bit = self.order.pop(0)
        other = self.links.swap(self.value, bit)
        low = self.links.mine(bit) == 0
        self.have.insert(0, bit)
        self.value = jnp.stack([jnp.where(low, self.value, other), jnp.where(low, other, self.value)])


class Part:
    def __init__(self, links, kept, other, axes, order, bound):
        self.links, self.kept, self.other, self.axes, self.order = links, kept, other, list(axes), list(order)
        self.bound, self.rows, self.received = bound, kept.shape[-2], None

    def away(self):
        self.arrive()
        bit = self.order[0]
        self.place, self.index = self.axes.index(bit), self.links.mine(bit)
        value = self.take(1 - self.index)
        if self.bound is None or len(self.order) == 1:
            return value
        power = jnp.clip(jnp.floor(14.0 - jnp.log2(jnp.maximum(self.bound, 1e-30))), -100.0, 100.0)
        note = jnp.broadcast_to(power, value.shape[:-2] + (8, 128))
        return jnp.concatenate([value * jnp.exp2(power), note], axis=-2).astype(jnp.float16)

    def take(self, index):
        cut = lambda value: lax.dynamic_index_in_dim(value, index, self.place, keepdims=False)[..., : self.rows, :]
        return cut(self.kept) + cut(self.other)

    def exchange(self, away):
        bit = self.order.pop(0)
        self.kept, self.received = self.take(self.index), self.links.swap(away, bit)
        self.axes.pop(self.place)

    def arrive(self, token=()):
        if self.received is None:
            return
        received, self.received = after(self.received, *token), None
        if received.dtype == jnp.float16:
            power = received[(0,) * (received.ndim - 2) + (self.rows, 0)].astype(F)
            received = received[..., : self.rows, :].astype(F) * jnp.exp2(-power)
            self.bound = self.bound + jnp.exp2(15.0 - power)
        self.other = received

    def finish(self):
        while self.order:
            self.exchange(self.away())
        self.arrive()
        return self.kept + self.other


def after(value, *others):
    return lax.optimization_barrier((value,) + others)[0]


def gather_params(enc, dec, note, links):
    orders = (
        links.upper[:-1] + [links.x, links.y] + links.upper[-1:],
        links.upper + [links.x, links.y], links.upper + [links.y, links.x],
    )
    tables = split_rows(enc.shape[0], (8.5, 8), False), split_rows(dec.shape[0], (8.5, 8), True)
    part = links.mine(links.core) * 2 + links.mine(links.y)
    padded = [
        jnp.pad(v, ((0, t[-1][1] + 4 * t[-1][4] - v.shape[0]), (0, 0))) for v, t in zip((enc, dec), tables)
    ]
    arrays, ways, mine = [], [], [links.mine(links.core)]
    for g, order in enumerate(orders):
        pieces = []
        for v, t in zip(padded, tables):
            unused, first, parts, rows, used = t[g]
            pieces.append(lax.dynamic_slice_in_dim(v, first + part * used, used))
            if used < rows:
                pieces.append(note)
        group = Group(links, jnp.concatenate(pieces), order)
        while len(group.order) > 1:
            group.step()
        last = group.order[0]
        both = [group.value, links.swap(group.value, last)]
        both += [links.swap(v, links.core) for v in both]
        arrays += [v.reshape((-1,) + v.shape[-2:]) for v in both]
        bits = links.wide_bits + [links.y]
        ways.append((bits.index(last), tuple(bits.index(b) for b in group.have)))
        mine.append(links.mine(last))
    at = tables[0][0][3] + tables[1][0][4]
    notes = sum(jnp.sum(v[:, at, :2].astype(F), axis=0) for v in arrays[:4])
    return arrays, tables, tuple(ways), jnp.stack(mine).astype(jnp.int32), notes


def join_shard(piece, links):
    return links.gather(piece, [links.y, links.core])


def adamw_update(master, gradient, moment_one, moment_two, clip_scale):
    gradient = gradient * clip_scale
    moment_one = BETA_ONE * moment_one + (1.0 - BETA_ONE) * gradient
    moment_two = BETA_TWO * moment_two + (1.0 - BETA_TWO) * gradient * gradient
    first_hat = moment_one / (1.0 - BETA_ONE**STEP)
    second_hat = moment_two / (1.0 - BETA_TWO**STEP)
    updated = master - learn_rate * (
        first_hat / (jnp.sqrt(second_hat) + EPSILON) + weight_decay * master
    )
    return (moment_one, moment_two, updated)


def body(
    links, vis_pixels, target, clip_lens, vis_index, params_enc, m_enc, v_enc, params_dec, m_dec, v_dec
):
    lengths = clip_lens[0]
    visible = vis_index[0]
    mine, core = lax.axis_index("wide"), links.mine(links.core).astype(jnp.int32).reshape(1)
    enc_shard, dec_shard = (v.shape[0] // 128 for v in (params_enc, params_dec))
    segment, clip_place, slot_live, shown_flag, counted = layout(lengths, visible, target.shape[0])

    here = jnp.sum(counted).astype(jnp.int32)
    note = jnp.pad(jnp.stack([here // 64, here % 64]), (0, 126))[None, :].astype(B)
    arrays, tables, ways, sides, notes = gather_params(
        params_enc.astype(B).reshape(-1, 128), params_dec.astype(B).reshape(-1, 128), note, links
    )
    *enc_mats, enc_vec = unpack_flat(
        arrays, tables[0], (0, 0, 0), ways, sides, enc_shard, links.wide, ENC_SHAPES, "unpack_enc"
    )
    masked_count = notes[0] * 64.0 + notes[1]
    cotangent = 1.0 / masked_count

    segment, clip_place, shown_flag, counted = (
        v[:ROWS] for v in (segment, clip_place, shown_flag, counted)
    )
    rows = jnp.stack([counted, counted * (cotangent * (2.0 / PIX)), 1.0 - shown_flag], axis=1)
    rows = jnp.pad(rows, ((0, 0), (0, 125)))
    lane = jnp.arange(128, dtype=jnp.int32)[None, :] % 64

    def marks_of(labels):
        mark = lane == labels[:, None]
        return mark.astype(B), jnp.where(mark | (lane > 3), 0.0, -1e30).astype(B)

    q_marks, k_marks = marks_of(segment)
    slot_segment, slot_place = slot_layout(lengths, visible)
    slot_marks = marks_of(slot_segment)

    latent, *saved = enc_forward(vis_pixels, sinusoid(slot_place, D), *slot_marks, enc_vec, enc_mats)
    arrays[0] = after(arrays[0], latent)
    *dec_mats, dec_vec = unpack_flat(
        arrays, tables[1], tuple(t[3] for t in tables[0]), ways, sides, dec_shard, links.wide, DEC_SHAPES, "unpack_dec"
    )
    w_qkv, w_out, w_up, w_down, w_head = dec_mats
    bias = jnp.concatenate([dec_vec[3, :DD], jnp.zeros((DD,), F), dec_vec[4, :DD]])
    vec_one = stack_rows([dec_vec[1, :DD], dec_vec[2, :DD], bias], 3 * DD)
    vec_two = jnp.concatenate([dec_vec[5:13], jnp.zeros((8, DFF), F)])
    x0, qkv = qkv_forward(
        visible, slot_live, latent, sinusoid(clip_place, DD), rows, w_qkv, vec_one, dec_vec
    )
    a, lse = attend_forward(qkv, q_marks, k_marks)
    da, dx1, dd, g_out, g_up, g_down, g_head, g_two = mlp_both(
        x0, a, target, rows, w_out, w_up, w_down, w_head, vec_two
    )

    late_flat = Flat([(0, dec_shard)], links.wide, links.narrow, 2)
    kept, away = pack_late(
        [g_out, g_up, g_down, g_head], g_two, table(DEC_SHAPES)[6:], late_flat, core, "pack_dec"
    )
    back = lambda da, h: attend_back(qkv, q_marks, k_marks, da, lse, dd, h)
    da, away = lax.optimization_barrier((da, away))
    late = links.scatter_parts(kept, [links.swap(v, links.core) for v in away])
    dqkv = [back(da, 0)]
    for h in (1, 2):
        sent = [part.away() for part in late]
        da, sent, dqkv = lax.optimization_barrier((da, sent, dqkv))
        dqkv = dqkv + [back(da, h)]
        for part, value in zip(late, sent):
            part.exchange(value)
    sent = [part.away() for part in late]
    dx1, sent, dqkv = lax.optimization_barrier((dx1, sent, dqkv))
    dx0, g_qkv, g_one = qkv_back(x0, dx1, dqkv, rows, w_qkv, vec_one)
    for part, value in zip(late, sent):
        part.exchange(value)

    early = table(DEC_SHAPES[:6])
    early_count = early[-1][0] + early[-1][2]
    flat = Flat(
        [(0, enc_shard), (enc_shard * links.wide, -(-early_count // (8 * links.wide)) * 8)], links.wide, links.narrow, 2
    )
    dx1, top, out = enc_back_one(core, visible, slot_live, dx0, saved, enc_vec, enc_mats, flat)
    sent = [part.away() for part in late]
    dx1, sent = lax.optimization_barrier((dx1, sent))
    kept, away, top = enc_back_two(
        core, dx1, top, out, saved, vis_pixels, slot_marks, enc_vec, enc_mats, g_qkv, g_one, flat
    )
    for part, value in zip(late, sent):
        part.exchange(value)
    beside = links.swap(top, links.core)
    first = [links.swap(after(v, beside), links.core) for v in away[:1]]
    second = [links.swap(after(v, *first), links.core) for v in away[1:]]
    parts = links.scatter_parts(kept, first + second, jnp.max(top + beside))
    for unused in range(len(parts[0].order)):
        for part in parts:
            part.exchange(part.away())
    piece_dec = jnp.concatenate([part.finish() for part in late])
    chunks = [part.finish() for part in parts]
    piece = jnp.concatenate(chunks)

    part = links.mine(links.core) * 2 + links.mine(links.y)
    squares = flat.squares(piece, 0, mine, part) + flat.squares(piece, 1, mine, part)
    squares += late_flat.squares(piece_dec, 0, mine, part)
    sums = links.everyone(jnp.stack([squares, jnp.sum(g_two[8]) / PIX]), [links.y])
    chunks[-1] = after(chunks[-1], sums)
    sides = [links.swap(chunk, links.y) for chunk in chunks]
    sums = links.everyone(sums, [links.core] + links.wide_bits[:-1])
    sides[-1] = after(sides[-1], sums)
    squares, loss_sum = links.everyone(sums, links.wide_bits[-1:])
    low = links.mine(links.y) == 0
    joined = [
        jnp.stack([jnp.where(low, one, two), jnp.where(low, two, one)]) for one, two in zip(chunks, sides)
    ]
    joined = jnp.concatenate([links.gather(v, [links.core]) for v in joined], axis=2)
    joined = joined[:, :, flat.starts[0] :].reshape(-1, 128)
    joined_late = join_shard(piece_dec, links).reshape(-1, 128)
    grad_norm = jnp.sqrt(squares)
    clip_scale = jnp.minimum(1.0, clip_norm / (grad_norm + 1e-06))
    order = links.upper + [links.x, links.y, links.core]
    everywhere = links.gather(chunks[0][: flat.parts[1]], order)
    places = [order[::-1].index(bit) for bit in links.wide_bits + [links.core, links.y]]
    everywhere = everywhere.transpose(places + [len(places), len(places) + 1]).reshape(links.wide, -1, 128)
    early_sum = everywhere[:, : flat.sections[1][1]].reshape(-1, 128)
    early_sum = jnp.pad(early_sum, ((0, dec_shard), (0, 0)))
    start = jnp.minimum(mine * dec_shard, early_sum.shape[0] - dec_shard)
    grad_enc = flat.take(joined, 0, mine).reshape(-1)
    grad_dec = late_flat.take(joined_late, 0, mine) + lax.dynamic_slice_in_dim(early_sum, start, dec_shard)
    enc_one, enc_two, enc_new = adamw_update(params_enc, grad_enc, m_enc, v_enc, clip_scale)
    dec_one, dec_two, dec_new = adamw_update(
        params_dec, grad_dec.reshape(-1), m_dec, v_dec, clip_scale
    )
    return (loss_sum, masked_count, grad_norm, enc_one, enc_two, enc_new, dec_one, dec_two, dec_new)


def solution(mesh):
    placed = (P(AXES, None),) * 4 + (P("wide"),) * 6
    return jax.shard_map(
        functools.partial(body, Links(mesh)),
        mesh=mesh,
        in_specs=placed,
        out_specs=(P(), P(), P()) + (P("wide"),) * 6,
        check_vma=False,
    )
```

```python
import functools
import math

import jax
import jax.numpy as jnp
from jax import lax
from jax.experimental import pallas as pl
from jax.experimental.pallas import tpu as pltpu
from jax.sharding import PartitionSpec as P

D = 768
HEADS = 12
FF = 3072
DD = 384
DHEADS = 6
DFF = 1536
PIX = 1536
STEP = 10
ROWS = 2592

learn_rate = 0.05
BETA_ONE = 0.9
BETA_TWO = 0.95
EPSILON = 1e-08
weight_decay = 0.05
clip_norm = 0.05

F = jnp.float32
B = jnp.bfloat16
AXES = ("narrow", "wide")
NT = (((1,), (1,)), ((), ()))
NN = (((1,), (0,)), ((), ()))
TN = (((0,), (0,)), ((), ()))
VMEM_LIMIT = 60 << 20
SLOTS = 4


def mm(left, right, dims=NN):
    return lax.dot_general(left, right, dims, preferred_element_type=F)


ENC_SHAPES = [
    (PIX, D), (D,), (D,), (D,), (D, 3 * D), (D,), (D,), (D, D), (D,), (D,), (D,),
    (D, FF), (FF,), (FF, D), (D,), (D,), (D,), (D, DD),
]
DEC_SHAPES = [
    (DD,), (DD,), (DD,), (DD, 3 * DD), (DD,), (DD,), (DD, DD), (DD,), (DD,), (DD,),
    (DD, DFF), (DFF,), (DFF, DD), (DD,), (DD,), (DD,), (DD, PIX), (PIX,),
]


def sinusoid(places, columns):
    half_width = columns // 2
    frequency = jnp.exp(jnp.arange(half_width, dtype=F) * (-math.log(10000.0) / half_width))
    angles = places[:, None] * frequency[None, :]
    return jnp.concatenate([jnp.sin(angles), jnp.cos(angles)], axis=1)


def layout(lengths, visible, row_count):
    positions = jnp.arange(row_count, dtype=jnp.int32)
    clip_ends = jnp.cumsum(lengths)
    starts = clip_ends - lengths
    segment = jnp.sum((positions[:, None] >= clip_ends[None, :]).astype(jnp.int32), axis=1)
    member = segment[:, None] == jnp.arange(3, dtype=jnp.int32)[None, :]
    clip_begin = jnp.sum(jnp.where(member, starts[None, :], 0), axis=1)
    clip_place = (positions - clip_begin).astype(F)
    pack_total = clip_ends[2]
    slot_live = (visible < pack_total).astype(F)
    shown_flag = jnp.zeros((row_count,), F).at[visible].add(slot_live)
    counted = jnp.where(positions < pack_total, 1.0 - shown_flag, 0.0)
    return (segment, clip_place, slot_live, shown_flag, counted)


def slot_layout(lengths, visible):
    clip_ends = jnp.cumsum(lengths)
    starts = clip_ends - lengths
    segment = jnp.sum((visible[:, None] >= clip_ends[None, :]).astype(jnp.int32), axis=1)
    member = segment[:, None] == jnp.arange(3, dtype=jnp.int32)[None, :]
    clip_begin = jnp.sum(jnp.where(member, starts[None, :], 0), axis=1)
    return segment, (visible - clip_begin).astype(F)


def norm_rows(x):
    center = x - jnp.mean(x, axis=1, keepdims=True)
    inverse = lax.rsqrt(jnp.mean(center * center, axis=1, keepdims=True) + 1e-06)
    return center * inverse, inverse


def norm_back(grad, hat, inverse):
    return inverse * (
        grad
        - jnp.mean(grad, axis=1, keepdims=True)
        - hat * jnp.mean(grad * hat, axis=1, keepdims=True)
    )


def total(x):
    return jnp.sum(x, axis=0, keepdims=True)


def low_lanes(rows):
    return lax.broadcasted_iota(jnp.int32, (rows, 128), 1) < 64


def low_rows(columns):
    return lax.broadcasted_iota(jnp.int32, (128, columns), 0) < 64


def halves(low, value, other):
    return jnp.where(low, value, other), jnp.where(low, other, value)


def softmax_keys(s):
    m = jnp.max(s, axis=0, keepdims=True)
    e = jnp.exp(s - m)
    l = jnp.sum(e, axis=0, keepdims=True)
    return e * (1.0 / l), m + jnp.log(l)


def qkv_kernel(vis_ref, live_ref, latent_ref, place_ref, row_ref, w_ref, vec_ref, mask_ref, x_ref, o_ref):
    x_ref[...] = place_ref[...] + row_ref[:, 2:3] * mask_ref[0:1, :DD]

    def add_slot(i, carry):
        at = pl.ds(jnp.minimum(vis_ref[i], ROWS - 1), 1)
        x_ref[at, :] += latent_ref[pl.ds(i, 1), :] * live_ref[i]
        return carry

    lax.fori_loop(0, latent_ref.shape[0], add_slot, 0, unroll=8)
    bm = 432

    def block(i, carry):
        part = pl.ds(pl.multiple_of(i * bm, 16), bm)
        hat, inverse = norm_rows(x_ref[part, :])
        normed = (hat * vec_ref[0:1, :DD] + vec_ref[1:2, :DD]).astype(B)
        o_ref[part, :] = (mm(normed, w_ref[...]) + vec_ref[2:3, :]).astype(B)
        return carry

    lax.fori_loop(0, ROWS // bm, block, 0)


def qkv_forward(visible, live, latent, places, rows, w, vec, mask):
    smem, vmem = pl.BlockSpec(memory_space=pltpu.SMEM), pl.BlockSpec(memory_space=pltpu.VMEM)
    return pl.pallas_call(
        qkv_kernel,
        in_specs=[smem] * 2 + [vmem] * 6,
        out_specs=[vmem] * 2,
        out_shape=[jax.ShapeDtypeStruct((ROWS, DD), F), jax.ShapeDtypeStruct((ROWS, 3 * DD), B)],
        compiler_params=pltpu.CompilerParams(vmem_limit_bytes=VMEM_LIMIT),
        cost_estimate=pl.CostEstimate(flops=10 * 10**9, bytes_accessed=16 << 20, transcendentals=0),
        name="dec_qkv",
    )(visible, live, latent, places, rows, w, vec, mask)


def attend_kernel(q_ref, k_ref, v_ref, qf_ref, kf_ref, o_ref, lse_ref, k0, k1):
    rows, bq = k_ref.shape[0], q_ref.shape[0]

    @pl.when(pl.program_id(1) == 0)
    def _():
        k0[...], k1[...] = halves(low_lanes(rows), k_ref[...], kf_ref[...])

    qs = halves(low_lanes(bq), q_ref[...] * jnp.asarray(0.125, B), qf_ref[...])
    scores = [mm(keys[...], q, NT) for keys, q in zip((k0, k1), qs)]
    outs, logs = [], []
    for s in scores:
        p, log = softmax_keys(s)
        outs.append(mm(v_ref[...], p.astype(B), TN))
        logs.append(log)
    o_ref[...] = jnp.where(low_rows(bq), outs[0], outs[1]).T.astype(B)
    lse_ref[0] = jnp.concatenate(logs + [jnp.zeros((6, bq), F)], axis=0)


def attend_forward(qkv, qf, kf, bq=864):
    nq = ROWS // bq
    return pl.pallas_call(
        attend_kernel,
        grid=(3, nq),
        in_specs=[
            pl.BlockSpec((bq, 128), lambda h, i: (i, h)),
            pl.BlockSpec((ROWS, 128), lambda h, i: (0, 3 + h)),
            pl.BlockSpec((ROWS, 128), lambda h, i: (0, 6 + h)),
            pl.BlockSpec((bq, 128), lambda h, i: (i, 0)),
            pl.BlockSpec((ROWS, 128), lambda h, i: (0, 0)),
        ],
        out_specs=[
            pl.BlockSpec((bq, 128), lambda h, i: (i, h)),
            pl.BlockSpec((1, 8, bq), lambda h, i: (h * nq + i, 0, 0)),
        ],
        out_shape=[
            jax.ShapeDtypeStruct((ROWS, DD), B),
            jax.ShapeDtypeStruct((3 * nq, 8, bq), F),
        ],
        scratch_shapes=[pltpu.VMEM((ROWS, 128), B)] * 2,
        compiler_params=pltpu.CompilerParams(vmem_limit_bytes=VMEM_LIMIT),
        cost_estimate=pl.CostEstimate(flops=60 * 10**9, bytes_accessed=16 << 20, transcendentals=0),
        name="dec_attend",
    )(qkv, qkv, qkv, qf, kf)


def attend_back_kernel(
    h, kc, q_ref, k_ref, v_ref, qf_ref, kf_ref, da_ref, lse_ref, dd_ref, dq_ref, dk_ref, dv_ref,
    k0, k1, z0, z1, dk_sum, dv_sum,
):
    rows, bq = k_ref.shape[0], q_ref.shape[0]
    step = pl.program_id(0)

    @pl.when(step == 0)
    def _():
        low, keys = low_lanes(rows), k_ref[...]
        k0[...], k1[...] = halves(low, keys, kf_ref[...])
        z0[...], z1[...] = halves(low, keys, jnp.zeros_like(keys))
        dk_sum[...] = jnp.zeros_like(dk_sum)
        dv_sum[...] = jnp.zeros_like(dv_sum)

    low = low_lanes(bq)
    q, da = q_ref[...] * jnp.asarray(0.125, B), da_ref[...]
    zero = jnp.zeros_like(q)
    qs = halves(low, q, qf_ref[...])
    dz = halves(low, da, zero)
    q_both, d_both = jnp.concatenate(halves(low, q, zero), axis=0), jnp.concatenate(dz, axis=0)
    mean = jnp.concatenate([dd_ref[i] for i in range(dd_ref.shape[0])], axis=1)
    dq = jnp.zeros((128, bq), F)
    for c in range(rows // kc):
        part = slice(c * kc, (c + 1) * kc)
        scores = [mm(keys[part, :], q, NT) for keys, q in zip((k0, k1), qs)]
        dps = [mm(v_ref[part, :], d, NT) for d in dz]
        ps, dss = [], []
        for i in range(2):
            p = jnp.exp(scores[i] - lse_ref[0, i : i + 1, :])
            ps.append(p.astype(B))
            dss.append((p * (dps[i] - mean[2 * h + i : 2 * h + i + 1, :])).astype(B))
        dv_sum[part, :] += mm(jnp.concatenate(ps, axis=1), d_both)
        dk_sum[part, :] += mm(jnp.concatenate(dss, axis=1), q_both)
        for z, ds in zip((z0, z1), dss):
            dq += mm(z[part, :], ds, TN)
    dq_ref[...] = (dq.T * 0.125).astype(B)

    @pl.when(step == pl.num_programs(0) - 1)
    def _():
        dk_ref[...] = dk_sum[...].astype(B)
        dv_ref[...] = dv_sum[...].astype(B)


def attend_back(qkv, qf, kf, da, lse, dd, h, bq=864, kc=864):
    nq = ROWS // bq
    many = bq // dd.shape[2]
    return pl.pallas_call(
        functools.partial(attend_back_kernel, h, kc),
        grid=(nq,),
        in_specs=[
            pl.BlockSpec((bq, 128), lambda i: (i, h)),
            pl.BlockSpec((ROWS, 128), lambda i: (0, 3 + h)),
            pl.BlockSpec((ROWS, 128), lambda i: (0, 6 + h)),
            pl.BlockSpec((bq, 128), lambda i: (i, 0)),
            pl.BlockSpec((ROWS, 128), lambda i: (0, 0)),
            pl.BlockSpec((bq, 128), lambda i: (i, h)),
            pl.BlockSpec((1, 8, bq), lambda i: (h * nq + i, 0, 0)),
            pl.BlockSpec((many, 8, bq // many), lambda i: (i, 0, 0)),
        ],
        out_specs=[
            pl.BlockSpec((bq, 128), lambda i: (i, 0)),
            pl.BlockSpec((ROWS, 128), lambda i: (0, 0)),
            pl.BlockSpec((ROWS, 128), lambda i: (0, 0)),
        ],
        out_shape=[jax.ShapeDtypeStruct((ROWS, 128), B)] * 3,
        scratch_shapes=[pltpu.VMEM((ROWS, 128), B)] * 4 + [pltpu.VMEM((ROWS, 128), F)] * 2,
        compiler_params=pltpu.CompilerParams(vmem_limit_bytes=VMEM_LIMIT),
        cost_estimate=pl.CostEstimate(flops=40 * 10**9, bytes_accessed=8 << 20, transcendentals=0),
        name="dec_attend_back",
    )(qkv, qkv, qkv, qf, kf, da, lse, dd)


def mlp_kernel(
    x_ref, a_ref, t_ref, row_ref, wo_ref, wu_ref, wd_ref, wh_ref, vec_ref,
    da_ref, dx_ref, dd_ref, go_ref, gu_ref, gd_ref, gh_ref, gv_ref,
):
    @pl.when(pl.program_id(0) == 0)
    def _():
        for ref in (go_ref, gu_ref, gd_ref, gh_ref, gv_ref):
            ref[...] = jnp.zeros_like(ref)

    a = a_ref[...]
    x1 = x_ref[...] + mm(a, wo_ref[...]) + vec_ref[0:1, :DD]
    hat2, inv2 = norm_rows(x1)
    n2 = (hat2 * vec_ref[1:2, :DD] + vec_ref[2:3, :DD]).astype(B)
    h = mm(n2, wu_ref[...]) + vec_ref[3:4, :]
    cdf = 0.5 * (1.0 + lax.erf(h * (1.0 / math.sqrt(2.0))))
    u = (h * cdf).astype(B)
    slope = cdf + h * jnp.exp(-0.5 * h * h) * (1.0 / math.sqrt(2.0 * math.pi))
    x2 = x1 + mm(u, wd_ref[...]) + vec_ref[4:5, :DD]
    hatf, invf = norm_rows(x2)
    nf = (hatf * vec_ref[5:6, :DD] + vec_ref[6:7, :DD]).astype(B)
    pred = mm(nf, wh_ref[...]) + vec_ref[7:8, :]
    goal, unused = norm_rows(t_ref[...].astype(F))
    err = pred - goal
    gv_ref[8:9, :] += total(err * err * row_ref[:, 0:1])
    dpred = err * row_ref[:, 1:2]
    gv_ref[7:8, :] += total(dpred)
    dpred = dpred.astype(B)
    gh_ref[...] += mm(nf, dpred, TN)
    dnf = mm(dpred, wh_ref[...], NT)
    gv_ref[5:6, :DD] += total(dnf * hatf)
    gv_ref[6:7, :DD] += total(dnf)
    dx2 = norm_back(dnf * vec_ref[5:6, :DD], hatf, invf)
    gv_ref[4:5, :DD] += total(dx2)
    dx2b = dx2.astype(B)
    gd_ref[...] += mm(u, dx2b, TN)
    dh = mm(dx2b, wd_ref[...], NT) * slope
    gv_ref[3:4, :] += total(dh)
    dh = dh.astype(B)
    gu_ref[...] += mm(n2, dh, TN)
    dn2 = mm(dh, wu_ref[...], NT)
    gv_ref[1:2, :DD] += total(dn2 * hat2)
    gv_ref[2:3, :DD] += total(dn2)
    dx1 = dx2 + norm_back(dn2 * vec_ref[1:2, :DD], hat2, inv2)
    gv_ref[0:1, :DD] += total(dx1)
    dx_ref[...] = dx1
    dx1 = dx1.astype(B)
    go_ref[...] += mm(a, dx1, TN)
    da = mm(dx1, wo_ref[...], NT).astype(B)
    da_ref[...] = da
    head_of = lax.broadcasted_iota(jnp.int32, (8, DD), 1) // 64
    pick = (head_of == lax.broadcasted_iota(jnp.int32, (8, DD), 0)).astype(F)
    dd_ref[0] = lax.dot_general(
        pick, da.astype(F) * a.astype(F), NT, precision=lax.Precision.HIGHEST, preferred_element_type=F
    )


def mlp_both(x, a, target, rows, wo, wu, wd, wh, vec, bm=864):
    full = lambda shape: pl.BlockSpec(shape, lambda i: (0, 0))
    part = lambda width: pl.BlockSpec((bm, width), lambda i: (i, 0))
    sums = [wo.shape, wu.shape, wd.shape, wh.shape, vec.shape]
    return pl.pallas_call(
        mlp_kernel,
        grid=(ROWS // bm,),
        in_specs=[part(DD), part(DD), part(PIX), part(128)]
        + [full(w.shape) for w in (wo, wu, wd, wh, vec)],
        out_specs=[part(DD), part(DD), pl.BlockSpec((1, 8, bm), lambda i: (i, 0, 0))] + [full(s) for s in sums],
        out_shape=[
            jax.ShapeDtypeStruct((ROWS, DD), B),
            jax.ShapeDtypeStruct((ROWS, DD), F),
            jax.ShapeDtypeStruct((ROWS // bm, 8, bm), F),
        ]
        + [jax.ShapeDtypeStruct(s, F) for s in sums],
        compiler_params=pltpu.CompilerParams(vmem_limit_bytes=VMEM_LIMIT),
        name="dec_mlp",
    )(x, a, target, rows, wo, wu, wd, wh, vec)


def qkv_back_kernel(x_ref, dx_ref, *refs):
    parts, (row_ref, w_ref, vec_ref, o_ref, g_ref, gv_ref) = refs[:9], refs[9:]

    @pl.when(pl.program_id(0) == 0)
    def _():
        for ref in (g_ref, gv_ref):
            ref[...] = jnp.zeros_like(ref)

    hat, inverse = norm_rows(x_ref[...])
    normed = (hat * vec_ref[0:1, :DD] + vec_ref[1:2, :DD]).astype(B)
    dp = jnp.concatenate([parts[3 * h + i][...] for i in range(3) for h in range(3)], axis=1)
    g_ref[...] += mm(normed, dp, TN)
    dn = mm(dp, w_ref[...], NT)
    gv_ref[2:3, :] += total(dp.astype(F))
    gv_ref[0:1, :DD] += total(dn * hat)
    gv_ref[1:2, :DD] += total(dn)
    dx = dx_ref[...] + norm_back(dn * vec_ref[0:1, :DD], hat, inverse)
    o_ref[...] = dx
    gv_ref[3:4, :DD] += total(dx * row_ref[:, 2:3])


def qkv_back(x, dx, dqkv, rows, w, vec, bm=432):
    full = lambda shape: pl.BlockSpec(shape, lambda i: (0, 0))
    part = lambda width: pl.BlockSpec((bm, width), lambda i: (i, 0))
    return pl.pallas_call(
        qkv_back_kernel,
        grid=(ROWS // bm,),
        in_specs=[part(DD)] * 2 + [part(128)] * 10 + [full(w.shape), full(vec.shape)],
        out_specs=[part(DD), full(w.shape), full(vec.shape)],
        out_shape=[
            jax.ShapeDtypeStruct((ROWS, DD), F),
            jax.ShapeDtypeStruct(w.shape, F),
            jax.ShapeDtypeStruct(vec.shape, F),
        ],
        compiler_params=pltpu.CompilerParams(vmem_limit_bytes=VMEM_LIMIT),
        cost_estimate=pl.CostEstimate(flops=15 * 10**9, bytes_accessed=8 << 20, transcendentals=0),
        name="dec_qkv_back",
    )(x, dx, *[part for head in dqkv for part in head], rows, w, vec)


def stack_rows(pieces, width, count=8):
    rows = [jnp.pad(p.astype(F), (0, width - p.shape[0])) for p in pieces]
    rows += [jnp.zeros((width,), F)] * (count - len(rows))
    return jnp.stack(rows)


def gelu_parts(h):
    cdf = 0.5 * (1.0 + lax.erf(h * (1.0 / math.sqrt(2.0))))
    return cdf, cdf + h * jnp.exp(-0.5 * h * h) * (1.0 / math.sqrt(2.0 * math.pi))


def enc_pair(qkv_ref, marks, j):
    q, k, v = (qkv_ref[:, i * D + j * 128 : i * D + (j + 1) * 128] for i in range(3))
    q = q * jnp.asarray(0.125, B)
    low = low_lanes(q.shape[0])
    return q, k, v, halves(low, q, marks[0]), halves(low, k, marks[1])


def enc_forward_kernel(
    pix_ref, place_ref, qm_ref, km_ref, vec_ref, we_hbm, wq_hbm, wo_hbm, wu_hbm, wd_hbm, wp_hbm,
    latent_ref, e0_ref, qkv_ref, a_ref, x1_ref, h_ref, x2_ref,
    we, wq, wo, wu, wd, wp, sems,
):
    loads = [
        pltpu.make_async_copy(source, target, sems.at[i])
        for i, (source, target) in enumerate(
            zip((we_hbm, wq_hbm, wo_hbm, wu_hbm, wd_hbm, wp_hbm), (we, wq, wo, wu, wd, wp))
        )
    ]
    for load in loads:
        load.start()
    loads[0].wait()
    e0 = mm(pix_ref[...], we[...]) + vec_ref[0:1, :D] + place_ref[...]
    e0_ref[...] = e0
    hat, unused = norm_rows(e0)
    n1 = (hat * vec_ref[1:2, :D] + vec_ref[2:3, :D]).astype(B)
    loads[1].wait()
    for i, bias in enumerate((vec_ref[3:4, :D], 0.0, vec_ref[4:5, :D])):
        part = slice(i * D, (i + 1) * D)
        qkv_ref[:, part] = (mm(n1, wq[:, part]) + bias).astype(B)
    marks = (qm_ref[...], km_ref[...])
    for j in range(HEADS // 2):
        unused, unused, v, qs, ks = enc_pair(qkv_ref, marks, j)
        scores = [mm(ks[i], qs[i], NT) for i in range(2)]
        outs = [mm(v, softmax_keys(s)[0].astype(B), TN) for s in scores]
        a_ref[:, j * 128 : (j + 1) * 128] = jnp.where(low_rows(v.shape[0]), outs[0], outs[1]).T.astype(B)
    loads[2].wait()
    x1 = e0 + mm(a_ref[...], wo[...]) + vec_ref[5:6, :D]
    x1_ref[...] = x1
    hat, unused = norm_rows(x1)
    n2 = (hat * vec_ref[6:7, :D] + vec_ref[7:8, :D]).astype(B)
    loads[3].wait()
    loads[4].wait()
    x2 = x1 + vec_ref[9:10, :D]
    for i in range(4):
        part = slice(i * D, (i + 1) * D)
        h = mm(n2, wu[:, part]) + vec_ref[8:9, part]
        h_ref[:, part] = h
        x2 += mm((h * gelu_parts(h)[0]).astype(B), wd[part, :])
    x2_ref[...] = x2
    hat, unused = norm_rows(x2)
    loads[5].wait()
    latent_ref[...] = mm((hat * vec_ref[10:11, :D] + vec_ref[11:12, :D]).astype(B), wp[...])


def enc_forward(pixels, places, q_marks, k_marks, vec, mats):
    rows = pixels.shape[0]
    hbm, vmem = pl.BlockSpec(memory_space=pl.ANY), pl.BlockSpec(memory_space=pltpu.VMEM)
    outs = [(DD, F), (D, F), (3 * D, B), (D, B), (D, F), (FF, F), (D, F)]
    return pl.pallas_call(
        enc_forward_kernel,
        in_specs=[vmem] * 5 + [hbm] * 6,
        out_specs=[vmem] * 7,
        out_shape=[jax.ShapeDtypeStruct((rows, width), kind) for width, kind in outs],
        scratch_shapes=[pltpu.VMEM(m.shape, B) for m in mats] + [pltpu.SemaphoreType.DMA((6,))],
        compiler_params=pltpu.CompilerParams(vmem_limit_bytes=VMEM_LIMIT),
        cost_estimate=pl.CostEstimate(flops=15 * 10**9, bytes_accessed=20 << 20, transcendentals=0),
        name="enc_forward",
    )(pixels, places, q_marks, k_marks, vec, *mats)


def put_product(lin, top, row, left, right):
    m, c = left.shape[0], right.shape[1] // 128
    step = min(m, 768)
    most = top[...]
    for r in range(0, m, step):
        for first in range(0, c, 2):
            last = min(first + 2, c)
            value = mm(left[r : r + step, :], right[:, first * 128 : last * 128])
            for i in range(first, last):
                piece = value[:, (i - first) * 128 : (i - first + 1) * 128]
                lin[pl.ds(row + r * c + i, step, stride=c), :] = piece
                most = jnp.maximum(most, jnp.max(jnp.abs(piece).reshape(-1, 8, 128), axis=0))
    top[...] = most


def put_vector(lin, top, row, value):
    for i in range(value.shape[1] // 128):
        piece = value[:, i * 128 : (i + 1) * 128]
        lin[pl.ds(row + i, 1), :] = piece
        top[0:1, :] = jnp.maximum(top[0:1, :], jnp.abs(piece))


def turned(value):
    return value.astype(F).T.astype(B)


def flush_start(lin, base, segments, core, kept, away, sem):
    for c in range(2):

        @pl.when(core == c)
        def _():
            for source, count, s, h, k, y, to in segments:
                target = (kept if h == c else away)[k]
                pltpu.make_async_copy(
                    lin.at[pl.ds(source - base, count)], target.at[s, y, pl.ds(to, count)], sem
                ).start()


def flush_wait(lin, segments, sem):
    count = sum(segment[1] for segment in segments)
    pltpu.make_async_copy(lin.at[pl.ds(0, count)], lin.at[pl.ds(0, count)], sem).wait()


def enc_back_one_kernel(
    base, rows_of, cuts, core_ref, vis_ref, live_ref, dx0_ref, x1_ref, h_ref, x2_ref, vec_ref, wu_hbm, wd_hbm, wp_hbm,
    dx1_ref, top_ref, *refs,
):
    chunks = (len(refs) - 7) // 2
    kept, away = refs[:chunks], refs[chunks : 2 * chunks]
    lin, wu, wd, wp, dl_ref, dh_ref, sems = refs[-7:]
    loads = [
        pltpu.make_async_copy(source, target, sems.at[i])
        for i, (source, target) in enumerate(zip((wp_hbm, wd_hbm, wu_hbm), (wp, wd, wu)))
    ]
    for load in loads:
        load.start()
    top_ref[...] = jnp.zeros_like(top_ref)
    upb, down, db, fg, fb, proj, end, last = (r - base for r in rows_of[1:])

    def take_slot(i, carry):
        at = pl.ds(jnp.minimum(vis_ref[i], ROWS - 1), 1)
        dl_ref[pl.ds(i, 1), :] = dx0_ref[at, :] * live_ref[i]
        return carry

    lax.fori_loop(0, dl_ref.shape[0], take_slot, 0, unroll=8)
    dl = dl_ref[...].astype(B)
    hatf, invf = norm_rows(x2_ref[...])
    put_product(lin, top_ref, proj, turned(hatf * vec_ref[10:11, :D] + vec_ref[11:12, :D]), dl)
    lin[pl.ds(end, lin.shape[0] - end), :] = jnp.zeros((lin.shape[0] - end, 128), F)
    loads[0].wait()
    dnf = mm(dl, wp[...], NT)
    put_vector(lin, top_ref, fg, total(dnf * hatf))
    put_vector(lin, top_ref, fb, total(dnf))
    dx2 = norm_back(dnf * vec_ref[10:11, :D], hatf, invf)
    put_vector(lin, top_ref, db, total(dx2))
    dx2b = dx2.astype(B)
    loads[1].wait()
    for i in range(4):
        part = slice(i * D, (i + 1) * D)
        h = h_ref[:, part]
        kept_share, slope = gelu_parts(h)
        put_product(lin, top_ref, down + i * D * (D // 128), turned(h * kept_share), dx2b)
        dh = mm(dx2b, wd[part, :], NT) * slope
        put_vector(lin, top_ref, upb + i * (D // 128), total(dh))
        dh_ref[:, part] = dh.astype(B)
    flush_start(lin, base, cuts[0], core_ref[0], kept, away, sems.at[3])
    loads[2].wait()
    hat2, inv2 = norm_rows(x1_ref[...])
    put_product(lin, top_ref, 0, turned(hat2 * vec_ref[6:7, :D] + vec_ref[7:8, :D]), dh_ref[...])
    flush_start(lin, base, cuts[1], core_ref[0], kept, away, sems.at[4])
    dn2 = mm(dh_ref[...], wu[...], NT)
    dx1_ref[0:1, :] = jnp.zeros((1, D), F)
    dx1 = dx2 + norm_back(dn2 * vec_ref[6:7, :D], hat2, inv2)
    count = dx1.shape[0]
    dx1_ref[0:count, :] = dx1
    dx1_ref[count : count + 1, :] = total(dn2 * hat2)
    dx1_ref[count + 1 : count + 2, :] = total(dn2)
    flush_wait(lin, cuts[0], sems.at[3])
    flush_wait(lin, cuts[1], sems.at[4])


def enc_back_two_kernel(
    rows_of, early_of, base_early, cuts, core_ref, dx1_ref, pix_ref, e0_ref, qkv_ref, a_ref, qm_ref, km_ref, vec_ref,
    g_qkv_ref, g_one_ref, wq_hbm, wo_hbm, top_in, *refs,
):
    chunks = (len(refs) - 6) // 4
    top_ref = refs[2 * chunks]
    kept, away = refs[2 * chunks + 1 : 3 * chunks + 1], refs[3 * chunks + 1 : 4 * chunks + 1]
    lin, wq, wo, dp_ref, sems = refs[-5:]
    loads = [
        pltpu.make_async_copy(source, target, sems.at[i])
        for i, (source, target) in enumerate(zip((wo_hbm, wq_hbm), (wo, wq)))
    ]
    for load in loads:
        load.start()
    top_ref[...] = top_in[...]
    embed, eb, g1, b1, qkv, qbias, vbias, out, ob, g2, b2 = rows_of
    count = pix_ref.shape[0]
    dx1 = dx1_ref[0:count, :]
    put_vector(lin, top_ref, g2, dx1_ref[count : count + 1, :])
    put_vector(lin, top_ref, b2, dx1_ref[count + 1 : count + 2, :])
    put_vector(lin, top_ref, ob, total(dx1))
    dx1b = dx1.astype(B)
    put_product(lin, top_ref, out, turned(a_ref[...]), dx1b)
    loads[0].wait()
    da = mm(dx1b, wo[...], NT).astype(B)
    marks = (qm_ref[...], km_ref[...])
    for j in range(HEADS // 2):
        q, k, v, qs, ks = enc_pair(qkv_ref, marks, j)
        low, zero = low_lanes(count), jnp.zeros_like(q)
        dz = halves(low, da[:, j * 128 : (j + 1) * 128], zero)
        scores = [mm(ks[i], qs[i], NT) for i in range(2)]
        dps = [mm(v, d, NT) for d in dz]
        ps, dss, dq = [], [], jnp.zeros((128, count), F)
        for i, keys in enumerate(halves(low, k, zero)):
            p = softmax_keys(scores[i])[0]
            ps.append(p.astype(B))
            dss.append((p * (dps[i] - jnp.sum(p * dps[i], axis=0, keepdims=True))).astype(B))
            dq += mm(keys, dss[i], TN)
        dk = mm(jnp.concatenate(dss, axis=1), jnp.concatenate(halves(low, q, zero), axis=0))
        dv = mm(jnp.concatenate(ps, axis=1), jnp.concatenate(dz, axis=0))
        for i, value in enumerate((dq.T * 0.125, dk, dv)):
            dp_ref[:, i * D + j * 128 : i * D + (j + 1) * 128] = value.astype(B)
    dp = dp_ref[...]
    sums = total(dp.astype(F))
    put_vector(lin, top_ref, qbias, sums[:, :D])
    put_vector(lin, top_ref, vbias, sums[:, 2 * D :])
    hat, inverse = norm_rows(e0_ref[...])
    put_product(lin, top_ref, qkv, turned(hat * vec_ref[1:2, :D] + vec_ref[2:3, :D]), dp)
    loads[1].wait()
    dn = mm(dp, wq[...], NT)
    put_vector(lin, top_ref, g1, total(dn * hat))
    put_vector(lin, top_ref, b1, total(dn))
    de0 = dx1 + norm_back(dn * vec_ref[1:2, :D], hat, inverse)
    put_vector(lin, top_ref, eb, total(de0))
    flush_start(lin, 0, cuts[0], core_ref[0], kept, away, sems.at[2])
    put_product(lin, top_ref, embed, turned(pix_ref[...]), de0.astype(B))
    c = g_qkv_ref.shape[1] // 128
    start = early_of[3]
    most = top_ref[...]
    for i in range(c):
        piece = g_qkv_ref[:, i * 128 : (i + 1) * 128]
        lin[pl.ds(start + i, g_qkv_ref.shape[0], stride=c), :] = piece
        most = jnp.maximum(most, jnp.max(jnp.abs(piece).reshape(-1, 8, 128), axis=0))
    top_ref[...] = most
    one = g_one_ref
    for row, value in zip(
        early_of[:3] + early_of[4:6],
        (one[3:4, :DD], one[0:1, :DD], one[1:2, :DD], one[2:3, :DD], one[2:3, 2 * DD :]),
    ):
        put_vector(lin, top_ref, row, value)
    end = early_of[6]
    lin[pl.ds(end, lin.shape[0] - end), :] = jnp.zeros((lin.shape[0] - end, 128), F)
    flush_start(lin, 0, cuts[1], core_ref[0], kept, away, sems.at[3])
    flush_start(lin, base_early, cuts[2], core_ref[0], kept, away, sems.at[4])
    for i in range(3):
        flush_wait(lin, cuts[i], sems.at[2 + i])


class Flat:
    def __init__(self, sections, wide, narrow, chunks):
        self.wide, self.narrow, self.sections = wide, narrow, sections
        self.spans = [-(-(rows + (0 if rows % 8 == 0 else 7)) // 8) * 8 for unused, rows in sections]
        self.parts = [-(-span // (narrow * 16)) * 16 for span in self.spans]
        self.starts = [sum(self.parts[i + 1 :]) for i in range(len(sections))]
        rows = sum(self.parts)
        step = -(-rows // (chunks * 16)) * 16
        self.chunks = [min(step, rows - i * step) for i in range(chunks)]
        self.shapes = [jax.ShapeDtypeStruct((wide, narrow // 2, count, 128), F) for count in self.chunks]

    def segments(self, section, low, high):
        first, rows = self.sections[section]
        part, span, at = self.parts[section], self.spans[section], self.starts[section]
        out = []
        for s in range(self.wide):
            start = first + s * rows // 8 * 8
            for p in range(self.narrow):
                begin = 0
                for k, count in enumerate(self.chunks):
                    lead = start + p * part - at + begin
                    a = max(low, start + p * part, lead)
                    b = min(high, start + span, start + (p + 1) * part, lead + count)
                    if a < b:
                        out.append((a, b - a, s, p // 2, k, p % 2, a - lead))
                    begin += count
        return out

    def reach(self, section):
        first, rows = self.sections[section]
        return first + (self.wide - 1) * rows // 8 * 8 + self.spans[section]

    def offset(self, section, index):
        return lax.rem(index * self.sections[section][1], 8)

    def of(self, piece, section):
        return piece[self.starts[section] : self.starts[section] + self.parts[section]]

    def squares(self, piece, section, index, part):
        value = self.of(piece, section)
        row = part * self.parts[section] + jnp.arange(value.shape[0], dtype=jnp.int32)[:, None]
        at = self.offset(section, index)
        inside = (row >= at) & (row < at + self.sections[section][1])
        return jnp.sum(jnp.where(inside, value * value, 0.0))

    def take(self, window, section, index):
        return lax.dynamic_slice_in_dim(window, self.offset(section, index), self.sections[section][1])


def enc_back_one(core, visible, live, dx0, saved, vec, mats, flat):
    x1, h, x2 = saved[3:]
    wu, wd, wp = mats[3:]
    rows = x1.shape[0]
    pieces = [p[0] for p in table(ENC_SHAPES)]
    end = pieces[-1] + DD // 128 * D
    total_rows = flat.sections[0][1] * flat.wide
    reach = max(flat.reach(0), total_rows)
    rows_of = tuple(pieces[11:]) + (end, reach)
    base, split = pieces[11], pieces[13]
    smem, vmem, hbm = (
        pl.BlockSpec(memory_space=space) for space in (pltpu.SMEM, pltpu.VMEM, pl.ANY)
    )
    top = jax.ShapeDtypeStruct((8, 128), F)
    cuts = (flat.segments(0, split, reach), flat.segments(0, base, split))
    room = max([reach - base] + [sum(seg[1] for seg in cut) for cut in cuts])
    chunks = len(flat.chunks)
    dx1, top, *out = pl.pallas_call(
        functools.partial(enc_back_one_kernel, base, rows_of, cuts),
        in_specs=[smem] * 3 + [vmem] * 5 + [hbm] * 3,
        out_specs=[vmem] * 2 + [hbm] * (2 * chunks),
        out_shape=[jax.ShapeDtypeStruct((rows + 8, D), F), top] + flat.shapes * 2,
        scratch_shapes=[
            pltpu.VMEM((room, 128), F), pltpu.VMEM(wu.shape, B), pltpu.VMEM(wd.shape, B),
            pltpu.VMEM(wp.shape, B), pltpu.VMEM((rows, DD), F),
            pltpu.VMEM((rows, FF), B), pltpu.SemaphoreType.DMA((5,)),
        ],
        compiler_params=pltpu.CompilerParams(vmem_limit_bytes=VMEM_LIMIT),
        cost_estimate=pl.CostEstimate(flops=20 * 10**9, bytes_accessed=30 << 20, transcendentals=0),
        name="enc_back_one",
    )(core, visible, live, dx0, x1, h, x2, vec, wu, wd, wp)
    return dx1, top, out


def enc_back_two(core, dx1, top, out, saved, pixels, marks, vec, mats, g_qkv, g_one, flat):
    e0, qkv, a = saved[:3]
    wq, wo = mats[1:3]
    rows = pixels.shape[0]
    pieces = [p[0] for p in table(ENC_SHAPES)]
    base = pieces[11]
    early_rows = table(DEC_SHAPES[:6])
    first = flat.sections[1][0]
    last = early_rows[-1][0] + early_rows[-1][2]
    early_of = tuple(base + p[0] for p in early_rows) + (base + last,)
    reach = max(flat.reach(1) - first, last)
    cuts = (
        flat.segments(0, pieces[1] // 8 * 8, base), flat.segments(0, 0, pieces[1] // 8 * 8),
        flat.segments(1, first, first + reach),
    )
    room = max([base + reach] + [sum(seg[1] for seg in cut) for cut in cuts])
    smem, vmem, hbm = (
        pl.BlockSpec(memory_space=space) for space in (pltpu.SMEM, pltpu.VMEM, pl.ANY)
    )
    chunks = len(flat.chunks)
    top, *out = pl.pallas_call(
        functools.partial(enc_back_two_kernel, tuple(pieces[:11]), early_of, first - base, cuts),
        in_specs=[smem] + [vmem] * 10 + [hbm] * 2 + [vmem] + [hbm] * (2 * chunks),
        out_specs=[vmem] + [hbm] * (2 * chunks),
        out_shape=[jax.ShapeDtypeStruct((8, 128), F)] + flat.shapes * 2,
        input_output_aliases={14 + i: 1 + i for i in range(2 * chunks)},
        scratch_shapes=[
            pltpu.VMEM((room, 128), F), pltpu.VMEM(wq.shape, B), pltpu.VMEM(wo.shape, B),
            pltpu.VMEM((rows, 3 * D), B), pltpu.SemaphoreType.DMA((5,)),
        ],
        compiler_params=pltpu.CompilerParams(vmem_limit_bytes=VMEM_LIMIT),
        cost_estimate=pl.CostEstimate(flops=15 * 10**9, bytes_accessed=30 << 20, transcendentals=0),
        name="enc_back_two",
    )(core, dx1, pixels, e0, qkv, a, *marks, vec, g_qkv, g_one, wq, wo, top, *out)
    return out[:chunks], out[chunks:], top


def table(shapes, row=0):
    out = []
    for s in shapes:
        m, c = (s[0], s[1] // 128) if len(s) == 2 else (1, s[0] // 128)
        out.append((row, m, c))
        row += m * c
    return out


def job_rows(m, c, most):
    return max(n for n in range(16, m + 1, 16) if m % n == 0 and n * c <= most)


def split_rows(shard, shares, note):
    out, place, first = [], 0, 0
    for i in range(len(shares) + 1):
        rows = shard * shares[i] / 100 if i < len(shares) else (shard - first) / 4
        rows = math.ceil(rows / 16) * 16
        used = rows - 1 if note and i == 0 else rows
        out.append((place, first, 4, rows, used))
        place, first = place + 4 * rows, first + 4 * used
    return out


def unpack_kernel(pieces, groups, leads, ways, span, wide, mine_ref, *refs):
    mats = [p for p in pieces if p[1] > 1]
    sources = [refs[4 * g : 4 * g + 4] for g in range(len(groups))]
    refs = refs[4 * len(groups) :]
    outs, vec_ref = refs[: len(mats)], refs[len(mats)]
    buf, lin, in_sem, out_sem = refs[len(mats) + 1 : len(mats) + 5]
    stages = refs[len(mats) + 5 :]
    bits = wide.bit_length()
    plans, size = [], 0
    for (place, first, parts, rows, used), lead in zip(groups, leads):
        plan = []
        for i in range(parts):
            a, b = first + i * used, min(first + (i + 1) * used, span)
            if a < b:
                plan.append((i // 2, i % 2, lead, rows, size, a, b - a))
                size += rows
        plans.append(plan)

    for g, (plan, (last, way)) in enumerate(zip(plans, ways)):
        for core in range(2):
            for side in range(2):

                @pl.when((mine_ref[0] == core) & (mine_ref[1 + g] == side))
                def _():
                    for s in range(wide):
                        for c, y, low, rows, to, at, count in plan:
                            index = [s >> (bits - 2 - j) & 1 for j in range(bits - 1)] + [y]
                            source = sources[g][2 * (c != core) + (index[last] != side)]
                            index = sum(index[j] << (len(way) - 1 - i) for i, j in enumerate(way))
                            pltpu.make_async_copy(
                                source.at[index, pl.ds(low, rows)], buf.at[s, pl.ds(to, rows)], in_sem.at[s]
                            ).start()

    for s in range(wide):
        pltpu.make_async_copy(buf.at[s, pl.ds(0, size)], buf.at[s, pl.ds(0, size)], in_sem.at[s]).wait()
        for plan in plans:
            for c, y, low, rows, to, at, count in plan:
                lin[pl.ds(s * span + at, count), :] = buf[s, pl.ds(to, rows), :].astype(F)[:count]

    vec_ref[...] = jnp.zeros_like(vec_ref)
    v = 0
    for row, m, c in pieces:
        if m == 1:
            for j in range(c):
                vec_ref[v : v + 1, j * 128 : (j + 1) * 128] = lin[pl.ds(row + j, 1), :]
            v += 1
    open_stores = []
    for k, (row, m, c) in enumerate(mats):
        stage, out = stages[k], outs[k]
        n = stage.shape[1]
        jobs = m // n

        def store(j, slot, k=k, stage=stage, out=out, n=n):
            return pltpu.make_async_copy(
                stage.at[slot], out.at[pl.ds(pl.multiple_of(j * n, 16), n)], out_sem.at[k, slot]
            )

        def job(j, carry):
            slot = lax.rem(j, SLOTS)

            @pl.when(j >= SLOTS)
            def _():
                store(j - SLOTS, slot).wait()

            for i in range(c):
                rows = pl.ds(row + i + j * (n * c), n, stride=c)
                stage[slot, :, i * 128 : (i + 1) * 128] = lin[rows, :].astype(B)
            store(j, slot).start()
            return carry

        lax.fori_loop(0, jobs, job, 0)
        open_stores += [(store, j) for j in range(max(jobs - SLOTS, 0), jobs)]
    for store, j in open_stores:
        store(j, j % SLOTS).wait()


def unpack_flat(arrays, groups, leads, ways, mine, span, wide, shapes, name):
    pieces = table(shapes)
    mats = [s for s in shapes if len(s) == 2]
    vectors = [s for s in shapes if len(s) == 1]
    width = max(s[0] for s in vectors)
    count = -(-len(vectors) // 8) * 8
    hbm = pl.BlockSpec(memory_space=pl.ANY)
    stages = [pltpu.VMEM((SLOTS, job_rows(s[0], s[1] // 128, 1152), s[1]), B) for s in mats]
    room = groups[-1][0] + groups[-1][2] * groups[-1][3]
    return pl.pallas_call(
        functools.partial(unpack_kernel, pieces, groups, leads, ways, span, wide),
        in_specs=[pl.BlockSpec(memory_space=pltpu.SMEM)] + [hbm] * len(arrays),
        out_specs=[hbm] * len(mats) + [pl.BlockSpec(memory_space=pltpu.VMEM)],
        out_shape=[jax.ShapeDtypeStruct(s, B) for s in mats] + [jax.ShapeDtypeStruct((count, width), F)],
        scratch_shapes=[
            pltpu.VMEM((wide, room, 128), B), pltpu.VMEM((wide * span, 128), F),
            pltpu.SemaphoreType.DMA((wide,)), pltpu.SemaphoreType.DMA((len(mats), SLOTS)),
        ] + stages,
        compiler_params=pltpu.CompilerParams(vmem_limit_bytes=VMEM_LIMIT),
        cost_estimate=pl.CostEstimate(flops=0, bytes_accessed=wide * span * 1536, transcendentals=0),
        name=name,
    )(mine, *arrays)


def pack_kernel(pieces, segments, core_ref, *refs):
    mats = [p for p in pieces if p[1] > 1]
    ins, vec_ref = refs[: len(mats)], refs[len(mats)]
    top_ref, *out = refs[len(mats) + 1 : -2]
    kept, away = out[: len(out) // 2], out[len(out) // 2 :]
    lin, sem = refs[-2:]
    first, end = pieces[0][0], pieces[-1][0] + pieces[-1][1] * pieces[-1][2]
    lin[pl.ds(0, first), :] = jnp.zeros((first, 128), F)
    lin[pl.ds(end, lin.shape[0] - end), :] = jnp.zeros((lin.shape[0] - end, 128), F)
    top_ref[...] = jnp.zeros_like(top_ref)
    k, v = 0, 0
    for row, m, c in pieces:
        if m == 1:
            put_vector(lin, top_ref, row, vec_ref[v : v + 1, : c * 128])
            v += 1
            continue
        most = top_ref[...]
        for i in range(c):
            piece = ins[k][:, i * 128 : (i + 1) * 128]
            lin[pl.ds(row + i, m, stride=c), :] = piece
            most = jnp.maximum(most, jnp.max(jnp.abs(piece).reshape(-1, 8, 128), axis=0))
        top_ref[...] = most
        k += 1
    flush_start(lin, 0, segments, core_ref[0], kept, away, sem)
    flush_wait(lin, segments, sem)


def pack_late(mats, vectors, pieces, flat, core, name):
    hbm, vmem = pl.BlockSpec(memory_space=pl.ANY), pl.BlockSpec(memory_space=pltpu.VMEM)
    segments = flat.segments(0, 0, flat.reach(0))
    room = max(flat.reach(0), flat.wide * flat.sections[0][1], sum(seg[1] for seg in segments))
    chunks = len(flat.chunks)
    unused, *out = pl.pallas_call(
        functools.partial(pack_kernel, pieces, segments),
        in_specs=[pl.BlockSpec(memory_space=pltpu.SMEM)] + [vmem] * (len(mats) + 1),
        out_specs=[vmem] + [hbm] * (2 * chunks),
        out_shape=[jax.ShapeDtypeStruct((8, 128), F)] + flat.shapes * 2,
        scratch_shapes=[pltpu.VMEM((room, 128), F), pltpu.SemaphoreType.DMA],
        compiler_params=pltpu.CompilerParams(vmem_limit_bytes=VMEM_LIMIT),
        cost_estimate=pl.CostEstimate(flops=0, bytes_accessed=30 << 20, transcendentals=0),
        name=name,
    )(core, *mats, vectors)
    return out[:chunks], out[chunks:]


class Links:
    def __init__(self, mesh):
        self.narrow, self.wide = mesh.shape["narrow"], mesh.shape["wide"]
        self.wide_bits = [("wide", b) for b in reversed(range(self.wide.bit_length() - 1))]
        self.x, self.upper = self.wide_bits[-1], self.wide_bits[:-1]
        self.y, self.core = ("narrow", 1), ("narrow", 0)

    def mine(self, bit):
        return (lax.axis_index(bit[0]) >> bit[1]) & 1

    def swap(self, value, bit):
        mask = 1 << bit[1] if bit[0] == "wide" else self.wide << bit[1]
        pairs = [(i, i ^ mask) for i in range(self.narrow * self.wide)]
        return lax.ppermute(value, AXES, pairs)

    def everyone(self, value, bits):
        for bit in bits:
            value = value + self.swap(value, bit)
        return value

    def gather(self, value, order):
        group = Group(self, value, order)
        while group.order:
            group.step()
        return group.value

    def scatter_parts(self, kept, other, bound=None):
        axes = self.wide_bits + [self.y]
        parts, orders = [], [[self.x, self.y] + self.upper, [self.y, self.x] + self.upper]
        for i, (one, two) in enumerate(zip(kept, other)):
            one, two = (v.reshape((2,) * len(axes) + v.shape[2:]) for v in (one, two))
            parts.append(Part(self, one, two, axes, orders[i % 2], bound))
        return parts


class Group:
    def __init__(self, links, value, order):
        self.links, self.value, self.order, self.have = links, value, list(order), []

    def step(self):
        bit = self.order.pop(0)
        other = self.links.swap(self.value, bit)
        low = self.links.mine(bit) == 0
        self.have.insert(0, bit)
        self.value = jnp.stack([jnp.where(low, self.value, other), jnp.where(low, other, self.value)])


class Part:
    def __init__(self, links, kept, other, axes, order, bound):
        self.links, self.kept, self.other, self.axes, self.order = links, kept, other, list(axes), list(order)
        self.bound, self.rows, self.received = bound, kept.shape[-2], None

    def away(self):
        self.arrive()
        bit = self.order[0]
        self.place, self.index = self.axes.index(bit), self.links.mine(bit)
        value = self.take(1 - self.index)
        if self.bound is None or len(self.order) == 1:
            return value
        power = jnp.clip(jnp.floor(14.0 - jnp.log2(jnp.maximum(self.bound, 1e-30))), -100.0, 100.0)
        note = jnp.broadcast_to(power, value.shape[:-2] + (8, 128))
        return jnp.concatenate([value * jnp.exp2(power), note], axis=-2).astype(jnp.float16)

    def take(self, index):
        cut = lambda value: lax.dynamic_index_in_dim(value, index, self.place, keepdims=False)[..., : self.rows, :]
        return cut(self.kept) + cut(self.other)

    def exchange(self, away):
        bit = self.order.pop(0)
        self.kept, self.received = self.take(self.index), self.links.swap(away, bit)
        self.axes.pop(self.place)

    def arrive(self, token=()):
        if self.received is None:
            return
        received, self.received = after(self.received, *token), None
        if received.dtype == jnp.float16:
            power = received[(0,) * (received.ndim - 2) + (self.rows, 0)].astype(F)
            received = received[..., : self.rows, :].astype(F) * jnp.exp2(-power)
            self.bound = self.bound + jnp.exp2(15.0 - power)
        self.other = received

    def finish(self):
        while self.order:
            self.exchange(self.away())
        self.arrive()
        return self.kept + self.other


def after(value, *others):
    return lax.optimization_barrier((value,) + others)[0]


def gather_params(enc, dec, note, links):
    orders = (
        links.upper[:-1] + [links.x, links.y] + links.upper[-1:],
        links.upper + [links.x, links.y], links.upper + [links.y, links.x],
    )
    tables = split_rows(enc.shape[0], (8.5, 8), False), split_rows(dec.shape[0], (8.5, 8), True)
    part = links.mine(links.core) * 2 + links.mine(links.y)
    padded = [
        jnp.pad(v, ((0, t[-1][1] + 4 * t[-1][4] - v.shape[0]), (0, 0))) for v, t in zip((enc, dec), tables)
    ]
    arrays, ways, mine = [], [], [links.mine(links.core)]
    for g, order in enumerate(orders):
        pieces = []
        for v, t in zip(padded, tables):
            unused, first, parts, rows, used = t[g]
            pieces.append(lax.dynamic_slice_in_dim(v, first + part * used, used))
            if used < rows:
                pieces.append(note)
        group = Group(links, jnp.concatenate(pieces), order)
        while len(group.order) > 1:
            group.step()
        last = group.order[0]
        both = [group.value, links.swap(group.value, last)]
        both += [links.swap(v, links.core) for v in both]
        arrays += [v.reshape((-1,) + v.shape[-2:]) for v in both]
        bits = links.wide_bits + [links.y]
        ways.append((bits.index(last), tuple(bits.index(b) for b in group.have)))
        mine.append(links.mine(last))
    at = tables[0][0][3] + tables[1][0][4]
    notes = sum(jnp.sum(v[:, at, :2].astype(F), axis=0) for v in arrays[:4])
    return arrays, tables, tuple(ways), jnp.stack(mine).astype(jnp.int32), notes


def join_shard(piece, links):
    return links.gather(piece, [links.y, links.core])


def adamw_update(master, gradient, moment_one, moment_two, clip_scale):
    gradient = gradient * clip_scale
    moment_one = BETA_ONE * moment_one + (1.0 - BETA_ONE) * gradient
    moment_two = BETA_TWO * moment_two + (1.0 - BETA_TWO) * gradient * gradient
    first_hat = moment_one / (1.0 - BETA_ONE**STEP)
    second_hat = moment_two / (1.0 - BETA_TWO**STEP)
    updated = master - learn_rate * (
        first_hat / (jnp.sqrt(second_hat) + EPSILON) + weight_decay * master
    )
    return (moment_one, moment_two, updated)


def body(
    links, vis_pixels, target, clip_lens, vis_index, params_enc, m_enc, v_enc, params_dec, m_dec, v_dec
):
    lengths = clip_lens[0]
    visible = vis_index[0]
    mine, core = lax.axis_index("wide"), links.mine(links.core).astype(jnp.int32).reshape(1)
    enc_shard, dec_shard = (v.shape[0] // 128 for v in (params_enc, params_dec))
    segment, clip_place, slot_live, shown_flag, counted = layout(lengths, visible, target.shape[0])

    here = jnp.sum(counted).astype(jnp.int32)
    note = jnp.pad(jnp.stack([here // 64, here % 64]), (0, 126))[None, :].astype(B)
    arrays, tables, ways, sides, notes = gather_params(
        params_enc.astype(B).reshape(-1, 128), params_dec.astype(B).reshape(-1, 128), note, links
    )
    *enc_mats, enc_vec = unpack_flat(
        arrays, tables[0], (0, 0, 0), ways, sides, enc_shard, links.wide, ENC_SHAPES, "unpack_enc"
    )
    masked_count = notes[0] * 64.0 + notes[1]
    cotangent = 1.0 / masked_count

    segment, clip_place, shown_flag, counted = (
        v[:ROWS] for v in (segment, clip_place, shown_flag, counted)
    )
    rows = jnp.stack([counted, counted * (cotangent * (2.0 / PIX)), 1.0 - shown_flag], axis=1)
    rows = jnp.pad(rows, ((0, 0), (0, 125)))
    lane = jnp.arange(128, dtype=jnp.int32)[None, :] % 64

    def marks_of(labels):
        mark = lane == labels[:, None]
        return mark.astype(B), jnp.where(mark | (lane > 3), 0.0, -1e30).astype(B)

    q_marks, k_marks = marks_of(segment)
    slot_segment, slot_place = slot_layout(lengths, visible)
    slot_marks = marks_of(slot_segment)

    latent, *saved = enc_forward(vis_pixels, sinusoid(slot_place, D), *slot_marks, enc_vec, enc_mats)
    arrays[0] = after(arrays[0], latent)
    *dec_mats, dec_vec = unpack_flat(
        arrays, tables[1], tuple(t[3] for t in tables[0]), ways, sides, dec_shard, links.wide, DEC_SHAPES, "unpack_dec"
    )
    w_qkv, w_out, w_up, w_down, w_head = dec_mats
    bias = jnp.concatenate([dec_vec[3, :DD], jnp.zeros((DD,), F), dec_vec[4, :DD]])
    vec_one = stack_rows([dec_vec[1, :DD], dec_vec[2, :DD], bias], 3 * DD)
    vec_two = jnp.concatenate([dec_vec[5:13], jnp.zeros((8, DFF), F)])
    x0, qkv = qkv_forward(
        visible, slot_live, latent, sinusoid(clip_place, DD), rows, w_qkv, vec_one, dec_vec
    )
    a, lse = attend_forward(qkv, q_marks, k_marks)
    da, dx1, dd, g_out, g_up, g_down, g_head, g_two = mlp_both(
        x0, a, target, rows, w_out, w_up, w_down, w_head, vec_two
    )

    late_flat = Flat([(0, dec_shard)], links.wide, links.narrow, 2)
    kept, away = pack_late(
        [g_out, g_up, g_down, g_head], g_two, table(DEC_SHAPES)[6:], late_flat, core, "pack_dec"
    )
    back = lambda da, h: attend_back(qkv, q_marks, k_marks, da, lse, dd, h)
    da, away = lax.optimization_barrier((da, away))
    late = links.scatter_parts(kept, [links.swap(v, links.core) for v in away])
    dqkv = [back(da, 0)]
    for h in (1, 2):
        sent = [part.away() for part in late]
        da, sent, dqkv = lax.optimization_barrier((da, sent, dqkv))
        dqkv = dqkv + [back(da, h)]
        for part, value in zip(late, sent):
            part.exchange(value)
    sent = [part.away() for part in late]
    dx1, sent, dqkv = lax.optimization_barrier((dx1, sent, dqkv))
    dx0, g_qkv, g_one = qkv_back(x0, dx1, dqkv, rows, w_qkv, vec_one)
    for part, value in zip(late, sent):
        part.exchange(value)

    early = table(DEC_SHAPES[:6])
    early_count = early[-1][0] + early[-1][2]
    flat = Flat(
        [(0, enc_shard), (enc_shard * links.wide, -(-early_count // (8 * links.wide)) * 8)], links.wide, links.narrow, 2
    )
    dx1, top, out = enc_back_one(core, visible, slot_live, dx0, saved, enc_vec, enc_mats, flat)
    sent = [part.away() for part in late]
    dx1, sent = lax.optimization_barrier((dx1, sent))
    kept, away, top = enc_back_two(
        core, dx1, top, out, saved, vis_pixels, slot_marks, enc_vec, enc_mats, g_qkv, g_one, flat
    )
    for part, value in zip(late, sent):
        part.exchange(value)
    beside = links.swap(top, links.core)
    first = [links.swap(after(v, beside), links.core) for v in away[:1]]
    second = [links.swap(after(v, *first), links.core) for v in away[1:]]
    parts = links.scatter_parts(kept, first + second, jnp.max(top + beside))
    for unused in range(len(parts[0].order)):
        for part in parts:
            part.exchange(part.away())
    piece_dec = jnp.concatenate([part.finish() for part in late])
    chunks = [part.finish() for part in parts]
    piece = jnp.concatenate(chunks)

    part = links.mine(links.core) * 2 + links.mine(links.y)
    squares = flat.squares(piece, 0, mine, part) + flat.squares(piece, 1, mine, part)
    squares += late_flat.squares(piece_dec, 0, mine, part)
    sums = links.everyone(jnp.stack([squares, jnp.sum(g_two[8]) / PIX]), [links.y])
    chunks[-1] = after(chunks[-1], sums)
    sides = [links.swap(chunk, links.y) for chunk in chunks]
    sums = links.everyone(sums, [links.core] + links.wide_bits[:-1])
    sides[-1] = after(sides[-1], sums)
    squares, loss_sum = links.everyone(sums, links.wide_bits[-1:])
    low = links.mine(links.y) == 0
    joined = [
        jnp.stack([jnp.where(low, one, two), jnp.where(low, two, one)]) for one, two in zip(chunks, sides)
    ]
    joined = jnp.concatenate([links.gather(v, [links.core]) for v in joined], axis=2)
    joined = joined[:, :, flat.starts[0] :].reshape(-1, 128)
    joined_late = join_shard(piece_dec, links).reshape(-1, 128)
    grad_norm = jnp.sqrt(squares)
    clip_scale = jnp.minimum(1.0, clip_norm / (grad_norm + 1e-06))
    order = links.upper + [links.x, links.y, links.core]
    everywhere = links.gather(chunks[0][: flat.parts[1]], order)
    places = [order[::-1].index(bit) for bit in links.wide_bits + [links.core, links.y]]
    everywhere = everywhere.transpose(places + [len(places), len(places) + 1]).reshape(links.wide, -1, 128)
    early_sum = everywhere[:, : flat.sections[1][1]].reshape(-1, 128)
    early_sum = jnp.pad(early_sum, ((0, dec_shard), (0, 0)))
    start = jnp.minimum(mine * dec_shard, early_sum.shape[0] - dec_shard)
    grad_enc = flat.take(joined, 0, mine).reshape(-1)
    grad_dec = late_flat.take(joined_late, 0, mine) + lax.dynamic_slice_in_dim(early_sum, start, dec_shard)
    enc_one, enc_two, enc_new = adamw_update(params_enc, grad_enc, m_enc, v_enc, clip_scale)
    dec_one, dec_two, dec_new = adamw_update(
        params_dec, grad_dec.reshape(-1), m_dec, v_dec, clip_scale
    )
    return (loss_sum, masked_count, grad_norm, enc_one, enc_two, enc_new, dec_one, dec_two, dec_new)


def solution(mesh):
    placed = (P(AXES, None),) * 4 + (P("wide"),) * 6
    return jax.shard_map(
        functools.partial(body, Links(mesh)),
        mesh=mesh,
        in_specs=placed,
        out_specs=(P(), P(), P()) + (P("wide"),) * 6,
        check_vma=False,
    )
```

```python
import functools
import math

import jax
import jax.numpy as jnp
from jax import lax
from jax.experimental import pallas as pl
from jax.experimental.pallas import tpu as pltpu
from jax.sharding import PartitionSpec as P

D = 768
HEADS = 12
FF = 3072
DD = 384
DHEADS = 6
DFF = 1536
PIX = 1536
STEP = 10
ROWS = 2592

learn_rate = 0.05
BETA_ONE = 0.9
BETA_TWO = 0.95
EPSILON = 1e-08
weight_decay = 0.05
clip_norm = 0.05

F = jnp.float32
B = jnp.bfloat16
AXES = ("narrow", "wide")
NT = (((1,), (1,)), ((), ()))
NN = (((1,), (0,)), ((), ()))
TN = (((0,), (0,)), ((), ()))
VMEM_LIMIT = 60 << 20
SLOTS = 4


def mm(left, right, dims=NN):
    return lax.dot_general(left, right, dims, preferred_element_type=F)


ENC_SHAPES = [
    (PIX, D), (D,), (D,), (D,), (D, 3 * D), (D,), (D,), (D, D), (D,), (D,), (D,),
    (D, FF), (FF,), (FF, D), (D,), (D,), (D,), (D, DD),
]
DEC_SHAPES = [
    (DD,), (DD,), (DD,), (DD, 3 * DD), (DD,), (DD,), (DD, DD), (DD,), (DD,), (DD,),
    (DD, DFF), (DFF,), (DFF, DD), (DD,), (DD,), (DD,), (DD, PIX), (PIX,),
]


def sinusoid(places, columns):
    half_width = columns // 2
    frequency = jnp.exp(jnp.arange(half_width, dtype=F) * (-math.log(10000.0) / half_width))
    angles = places[:, None] * frequency[None, :]
    return jnp.concatenate([jnp.sin(angles), jnp.cos(angles)], axis=1)


def layout(lengths, visible, row_count):
    positions = jnp.arange(row_count, dtype=jnp.int32)
    clip_ends = jnp.cumsum(lengths)
    starts = clip_ends - lengths
    segment = jnp.sum((positions[:, None] >= clip_ends[None, :]).astype(jnp.int32), axis=1)
    member = segment[:, None] == jnp.arange(3, dtype=jnp.int32)[None, :]
    clip_begin = jnp.sum(jnp.where(member, starts[None, :], 0), axis=1)
    clip_place = (positions - clip_begin).astype(F)
    pack_total = clip_ends[2]
    slot_live = (visible < pack_total).astype(F)
    shown_flag = jnp.zeros((row_count,), F).at[visible].add(slot_live)
    counted = jnp.where(positions < pack_total, 1.0 - shown_flag, 0.0)
    return (segment, clip_place, slot_live, shown_flag, counted)


def slot_layout(lengths, visible):
    clip_ends = jnp.cumsum(lengths)
    starts = clip_ends - lengths
    segment = jnp.sum((visible[:, None] >= clip_ends[None, :]).astype(jnp.int32), axis=1)
    member = segment[:, None] == jnp.arange(3, dtype=jnp.int32)[None, :]
    clip_begin = jnp.sum(jnp.where(member, starts[None, :], 0), axis=1)
    return segment, (visible - clip_begin).astype(F)


def norm_rows(x):
    center = x - jnp.mean(x, axis=1, keepdims=True)
    inverse = lax.rsqrt(jnp.mean(center * center, axis=1, keepdims=True) + 1e-06)
    return center * inverse, inverse


def norm_back(grad, hat, inverse):
    return inverse * (
        grad
        - jnp.mean(grad, axis=1, keepdims=True)
        - hat * jnp.mean(grad * hat, axis=1, keepdims=True)
    )


def total(x):
    return jnp.sum(x, axis=0, keepdims=True)


def low_lanes(rows):
    return lax.broadcasted_iota(jnp.int32, (rows, 128), 1) < 64


def low_rows(columns):
    return lax.broadcasted_iota(jnp.int32, (128, columns), 0) < 64


def halves(low, value, other):
    return jnp.where(low, value, other), jnp.where(low, other, value)


def softmax_keys(s):
    m = jnp.max(s, axis=0, keepdims=True)
    e = jnp.exp(s - m)
    l = jnp.sum(e, axis=0, keepdims=True)
    return e * (1.0 / l), m + jnp.log(l)


def qkv_kernel(vis_ref, live_ref, latent_ref, place_ref, row_ref, w_ref, vec_ref, mask_ref, x_ref, o_ref):
    x_ref[...] = place_ref[...] + row_ref[:, 2:3] * mask_ref[0:1, :DD]

    def add_slot(i, carry):
        at = pl.ds(jnp.minimum(vis_ref[i], ROWS - 1), 1)
        x_ref[at, :] += latent_ref[pl.ds(i, 1), :] * live_ref[i]
        return carry

    lax.fori_loop(0, latent_ref.shape[0], add_slot, 0, unroll=8)
    bm = 864

    def block(i, carry):
        part = pl.ds(pl.multiple_of(i * bm, 16), bm)
        hat, inverse = norm_rows(x_ref[part, :])
        normed = (hat * vec_ref[0:1, :DD] + vec_ref[1:2, :DD]).astype(B)
        o_ref[part, :] = (mm(normed, w_ref[...]) + vec_ref[2:3, :]).astype(B)
        return carry

    lax.fori_loop(0, ROWS // bm, block, 0)


def qkv_forward(visible, live, latent, places, rows, w, vec, mask):
    smem, vmem = pl.BlockSpec(memory_space=pltpu.SMEM), pl.BlockSpec(memory_space=pltpu.VMEM)
    return pl.pallas_call(
        qkv_kernel,
        in_specs=[smem] * 2 + [vmem] * 6,
        out_specs=[vmem] * 2,
        out_shape=[jax.ShapeDtypeStruct((ROWS, DD), F), jax.ShapeDtypeStruct((ROWS, 3 * DD), B)],
        compiler_params=pltpu.CompilerParams(vmem_limit_bytes=VMEM_LIMIT),
        cost_estimate=pl.CostEstimate(flops=10 * 10**9, bytes_accessed=16 << 20, transcendentals=0),
        name="dec_qkv",
    )(visible, live, latent, places, rows, w, vec, mask)


def attend_kernel(q_ref, k_ref, v_ref, qf_ref, kf_ref, o_ref, lse_ref, k0, k1):
    rows, bq = k_ref.shape[0], q_ref.shape[0]

    @pl.when(pl.program_id(1) == 0)
    def _():
        k0[...], k1[...] = halves(low_lanes(rows), k_ref[...], kf_ref[...])

    qs = halves(low_lanes(bq), q_ref[...] * jnp.asarray(0.125, B), qf_ref[...])
    scores = [mm(keys[...], q, NT) for keys, q in zip((k0, k1), qs)]
    outs, logs = [], []
    for s in scores:
        p, log = softmax_keys(s)
        outs.append(mm(v_ref[...], p.astype(B), TN))
        logs.append(log)
    o_ref[...] = jnp.where(low_rows(bq), outs[0], outs[1]).T.astype(B)
    lse_ref[0] = jnp.concatenate(logs + [jnp.zeros((6, bq), F)], axis=0)


def attend_forward(qkv, qf, kf, bq=864):
    nq = ROWS // bq
    return pl.pallas_call(
        attend_kernel,
        grid=(3, nq),
        in_specs=[
            pl.BlockSpec((bq, 128), lambda h, i: (i, h)),
            pl.BlockSpec((ROWS, 128), lambda h, i: (0, 3 + h)),
            pl.BlockSpec((ROWS, 128), lambda h, i: (0, 6 + h)),
            pl.BlockSpec((bq, 128), lambda h, i: (i, 0)),
            pl.BlockSpec((ROWS, 128), lambda h, i: (0, 0)),
        ],
        out_specs=[
            pl.BlockSpec((bq, 128), lambda h, i: (i, h)),
            pl.BlockSpec((1, 8, bq), lambda h, i: (h * nq + i, 0, 0)),
        ],
        out_shape=[
            jax.ShapeDtypeStruct((ROWS, DD), B),
            jax.ShapeDtypeStruct((3 * nq, 8, bq), F),
        ],
        scratch_shapes=[pltpu.VMEM((ROWS, 128), B)] * 2,
        compiler_params=pltpu.CompilerParams(vmem_limit_bytes=VMEM_LIMIT),
        cost_estimate=pl.CostEstimate(flops=60 * 10**9, bytes_accessed=16 << 20, transcendentals=0),
        name="dec_attend",
    )(qkv, qkv, qkv, qf, kf)


def attend_back_kernel(
    h, kc, q_ref, k_ref, v_ref, qf_ref, kf_ref, da_ref, lse_ref, dd_ref, dq_ref, dk_ref, dv_ref,
    k0, k1, z0, z1, dk_sum, dv_sum,
):
    rows, bq = k_ref.shape[0], q_ref.shape[0]
    step = pl.program_id(0)

    @pl.when(step == 0)
    def _():
        low, keys = low_lanes(rows), k_ref[...]
        k0[...], k1[...] = halves(low, keys, kf_ref[...])
        z0[...], z1[...] = halves(low, keys, jnp.zeros_like(keys))
        dk_sum[...] = jnp.zeros_like(dk_sum)
        dv_sum[...] = jnp.zeros_like(dv_sum)

    low = low_lanes(bq)
    q, da = q_ref[...] * jnp.asarray(0.125, B), da_ref[...]
    zero = jnp.zeros_like(q)
    qs = halves(low, q, qf_ref[...])
    dz = halves(low, da, zero)
    q_both, d_both = jnp.concatenate(halves(low, q, zero), axis=0), jnp.concatenate(dz, axis=0)
    mean = jnp.concatenate([dd_ref[i] for i in range(dd_ref.shape[0])], axis=1)
    dq = jnp.zeros((128, bq), F)
    for c in range(rows // kc):
        part = slice(c * kc, (c + 1) * kc)
        scores = [mm(keys[part, :], q, NT) for keys, q in zip((k0, k1), qs)]
        dps = [mm(v_ref[part, :], d, NT) for d in dz]
        ps, dss = [], []
        for i in range(2):
            p = jnp.exp(scores[i] - lse_ref[0, i : i + 1, :])
            ps.append(p.astype(B))
            dss.append((p * (dps[i] - mean[2 * h + i : 2 * h + i + 1, :])).astype(B))
        dv_sum[part, :] += mm(jnp.concatenate(ps, axis=1), d_both)
        dk_sum[part, :] += mm(jnp.concatenate(dss, axis=1), q_both)
        for z, ds in zip((z0, z1), dss):
            dq += mm(z[part, :], ds, TN)
    dq_ref[...] = (dq.T * 0.125).astype(B)

    @pl.when(step == pl.num_programs(0) - 1)
    def _():
        dk_ref[...] = dk_sum[...].astype(B)
        dv_ref[...] = dv_sum[...].astype(B)


def attend_back(qkv, qf, kf, da, lse, dd, h, bq=864, kc=864):
    nq = ROWS // bq
    many = bq // dd.shape[2]
    return pl.pallas_call(
        functools.partial(attend_back_kernel, h, kc),
        grid=(nq,),
        in_specs=[
            pl.BlockSpec((bq, 128), lambda i: (i, h)),
            pl.BlockSpec((ROWS, 128), lambda i: (0, 3 + h)),
            pl.BlockSpec((ROWS, 128), lambda i: (0, 6 + h)),
            pl.BlockSpec((bq, 128), lambda i: (i, 0)),
            pl.BlockSpec((ROWS, 128), lambda i: (0, 0)),
            pl.BlockSpec((bq, 128), lambda i: (i, h)),
            pl.BlockSpec((1, 8, bq), lambda i: (h * nq + i, 0, 0)),
            pl.BlockSpec((many, 8, bq // many), lambda i: (i, 0, 0)),
        ],
        out_specs=[
            pl.BlockSpec((bq, 128), lambda i: (i, 0)),
            pl.BlockSpec((ROWS, 128), lambda i: (0, 0)),
            pl.BlockSpec((ROWS, 128), lambda i: (0, 0)),
        ],
        out_shape=[jax.ShapeDtypeStruct((ROWS, 128), B)] * 3,
        scratch_shapes=[pltpu.VMEM((ROWS, 128), B)] * 4 + [pltpu.VMEM((ROWS, 128), F)] * 2,
        compiler_params=pltpu.CompilerParams(vmem_limit_bytes=VMEM_LIMIT),
        cost_estimate=pl.CostEstimate(flops=40 * 10**9, bytes_accessed=8 << 20, transcendentals=0),
        name="dec_attend_back",
    )(qkv, qkv, qkv, qf, kf, da, lse, dd)


def mlp_kernel(
    x_ref, a_ref, t_ref, row_ref, wo_ref, wu_ref, wd_ref, wh_ref, vec_ref,
    da_ref, dx_ref, dd_ref, go_ref, gu_ref, gd_ref, gh_ref, gv_ref,
):
    @pl.when(pl.program_id(0) == 0)
    def _():
        for ref in (go_ref, gu_ref, gd_ref, gh_ref, gv_ref):
            ref[...] = jnp.zeros_like(ref)

    a = a_ref[...]
    x1 = x_ref[...] + mm(a, wo_ref[...]) + vec_ref[0:1, :DD]
    hat2, inv2 = norm_rows(x1)
    n2 = (hat2 * vec_ref[1:2, :DD] + vec_ref[2:3, :DD]).astype(B)
    h = mm(n2, wu_ref[...]) + vec_ref[3:4, :]
    cdf = 0.5 * (1.0 + lax.erf(h * (1.0 / math.sqrt(2.0))))
    u = (h * cdf).astype(B)
    slope = cdf + h * jnp.exp(-0.5 * h * h) * (1.0 / math.sqrt(2.0 * math.pi))
    x2 = x1 + mm(u, wd_ref[...]) + vec_ref[4:5, :DD]
    hatf, invf = norm_rows(x2)
    nf = (hatf * vec_ref[5:6, :DD] + vec_ref[6:7, :DD]).astype(B)
    pred = mm(nf, wh_ref[...]) + vec_ref[7:8, :]
    goal, unused = norm_rows(t_ref[...].astype(F))
    err = pred - goal
    gv_ref[8:9, :] += total(err * err * row_ref[:, 0:1])
    dpred = err * row_ref[:, 1:2]
    gv_ref[7:8, :] += total(dpred)
    dpred = dpred.astype(B)
    gh_ref[...] += mm(nf, dpred, TN)
    dnf = mm(dpred, wh_ref[...], NT)
    gv_ref[5:6, :DD] += total(dnf * hatf)
    gv_ref[6:7, :DD] += total(dnf)
    dx2 = norm_back(dnf * vec_ref[5:6, :DD], hatf, invf)
    gv_ref[4:5, :DD] += total(dx2)
    dx2b = dx2.astype(B)
    gd_ref[...] += mm(u, dx2b, TN)
    dh = mm(dx2b, wd_ref[...], NT) * slope
    gv_ref[3:4, :] += total(dh)
    dh = dh.astype(B)
    gu_ref[...] += mm(n2, dh, TN)
    dn2 = mm(dh, wu_ref[...], NT)
    gv_ref[1:2, :DD] += total(dn2 * hat2)
    gv_ref[2:3, :DD] += total(dn2)
    dx1 = dx2 + norm_back(dn2 * vec_ref[1:2, :DD], hat2, inv2)
    gv_ref[0:1, :DD] += total(dx1)
    dx_ref[...] = dx1
    dx1 = dx1.astype(B)
    go_ref[...] += mm(a, dx1, TN)
    da = mm(dx1, wo_ref[...], NT).astype(B)
    da_ref[...] = da
    head_of = lax.broadcasted_iota(jnp.int32, (8, DD), 1) // 64
    pick = (head_of == lax.broadcasted_iota(jnp.int32, (8, DD), 0)).astype(F)
    dd_ref[0] = lax.dot_general(
        pick, da.astype(F) * a.astype(F), NT, precision=lax.Precision.HIGHEST, preferred_element_type=F
    )


def mlp_both(x, a, target, rows, wo, wu, wd, wh, vec, bm=864):
    full = lambda shape: pl.BlockSpec(shape, lambda i: (0, 0))
    part = lambda width: pl.BlockSpec((bm, width), lambda i: (i, 0))
    sums = [wo.shape, wu.shape, wd.shape, wh.shape, vec.shape]
    return pl.pallas_call(
        mlp_kernel,
        grid=(ROWS // bm,),
        in_specs=[part(DD), part(DD), part(PIX), part(128)]
        + [full(w.shape) for w in (wo, wu, wd, wh, vec)],
        out_specs=[part(DD), part(DD), pl.BlockSpec((1, 8, bm), lambda i: (i, 0, 0))] + [full(s) for s in sums],
        out_shape=[
            jax.ShapeDtypeStruct((ROWS, DD), B),
            jax.ShapeDtypeStruct((ROWS, DD), F),
            jax.ShapeDtypeStruct((ROWS // bm, 8, bm), F),
        ]
        + [jax.ShapeDtypeStruct(s, F) for s in sums],
        compiler_params=pltpu.CompilerParams(vmem_limit_bytes=VMEM_LIMIT),
        name="dec_mlp",
    )(x, a, target, rows, wo, wu, wd, wh, vec)


def qkv_back_kernel(x_ref, dx_ref, *refs):
    parts, (row_ref, w_ref, vec_ref, o_ref, g_ref, gv_ref) = refs[:9], refs[9:]

    @pl.when(pl.program_id(0) == 0)
    def _():
        for ref in (g_ref, gv_ref):
            ref[...] = jnp.zeros_like(ref)

    hat, inverse = norm_rows(x_ref[...])
    normed = (hat * vec_ref[0:1, :DD] + vec_ref[1:2, :DD]).astype(B)
    dp = jnp.concatenate([parts[3 * h + i][...] for i in range(3) for h in range(3)], axis=1)
    g_ref[...] += mm(normed, dp, TN)
    dn = mm(dp, w_ref[...], NT)
    gv_ref[2:3, :] += total(dp.astype(F))
    gv_ref[0:1, :DD] += total(dn * hat)
    gv_ref[1:2, :DD] += total(dn)
    dx = dx_ref[...] + norm_back(dn * vec_ref[0:1, :DD], hat, inverse)
    o_ref[...] = dx
    gv_ref[3:4, :DD] += total(dx * row_ref[:, 2:3])


def qkv_back(x, dx, dqkv, rows, w, vec, bm=864):
    full = lambda shape: pl.BlockSpec(shape, lambda i: (0, 0))
    part = lambda width: pl.BlockSpec((bm, width), lambda i: (i, 0))
    return pl.pallas_call(
        qkv_back_kernel,
        grid=(ROWS // bm,),
        in_specs=[part(DD)] * 2 + [part(128)] * 10 + [full(w.shape), full(vec.shape)],
        out_specs=[part(DD), full(w.shape), full(vec.shape)],
        out_shape=[
            jax.ShapeDtypeStruct((ROWS, DD), F),
            jax.ShapeDtypeStruct(w.shape, F),
            jax.ShapeDtypeStruct(vec.shape, F),
        ],
        compiler_params=pltpu.CompilerParams(vmem_limit_bytes=VMEM_LIMIT),
        cost_estimate=pl.CostEstimate(flops=15 * 10**9, bytes_accessed=8 << 20, transcendentals=0),
        name="dec_qkv_back",
    )(x, dx, *[part for head in dqkv for part in head], rows, w, vec)


def stack_rows(pieces, width, count=8):
    rows = [jnp.pad(p.astype(F), (0, width - p.shape[0])) for p in pieces]
    rows += [jnp.zeros((width,), F)] * (count - len(rows))
    return jnp.stack(rows)


def gelu_parts(h):
    cdf = 0.5 * (1.0 + lax.erf(h * (1.0 / math.sqrt(2.0))))
    return cdf, cdf + h * jnp.exp(-0.5 * h * h) * (1.0 / math.sqrt(2.0 * math.pi))


def enc_pair(qkv_ref, marks, j):
    q, k, v = (qkv_ref[:, i * D + j * 128 : i * D + (j + 1) * 128] for i in range(3))
    q = q * jnp.asarray(0.125, B)
    low = low_lanes(q.shape[0])
    return q, k, v, halves(low, q, marks[0]), halves(low, k, marks[1])


def enc_forward_kernel(
    pix_ref, place_ref, qm_ref, km_ref, vec_ref, we_hbm, wq_hbm, wo_hbm, wu_hbm, wd_hbm, wp_hbm,
    latent_ref, e0_ref, qkv_ref, a_ref, x1_ref, h_ref, x2_ref,
    we, wq, wo, wu, wd, wp, sems,
):
    loads = [
        pltpu.make_async_copy(source, target, sems.at[i])
        for i, (source, target) in enumerate(
            zip((we_hbm, wq_hbm, wo_hbm, wu_hbm, wd_hbm, wp_hbm), (we, wq, wo, wu, wd, wp))
        )
    ]
    for load in loads:
        load.start()
    loads[0].wait()
    e0 = mm(pix_ref[...], we[...]) + vec_ref[0:1, :D] + place_ref[...]
    e0_ref[...] = e0
    hat, unused = norm_rows(e0)
    n1 = (hat * vec_ref[1:2, :D] + vec_ref[2:3, :D]).astype(B)
    loads[1].wait()
    for i, bias in enumerate((vec_ref[3:4, :D], 0.0, vec_ref[4:5, :D])):
        part = slice(i * D, (i + 1) * D)
        qkv_ref[:, part] = (mm(n1, wq[:, part]) + bias).astype(B)
    marks = (qm_ref[...], km_ref[...])
    for j in range(HEADS // 2):
        unused, unused, v, qs, ks = enc_pair(qkv_ref, marks, j)
        scores = [mm(ks[i], qs[i], NT) for i in range(2)]
        outs = [mm(v, softmax_keys(s)[0].astype(B), TN) for s in scores]
        a_ref[:, j * 128 : (j + 1) * 128] = jnp.where(low_rows(v.shape[0]), outs[0], outs[1]).T.astype(B)
    loads[2].wait()
    x1 = e0 + mm(a_ref[...], wo[...]) + vec_ref[5:6, :D]
    x1_ref[...] = x1
    hat, unused = norm_rows(x1)
    n2 = (hat * vec_ref[6:7, :D] + vec_ref[7:8, :D]).astype(B)
    loads[3].wait()
    loads[4].wait()
    x2 = x1 + vec_ref[9:10, :D]
    for i in range(4):
        part = slice(i * D, (i + 1) * D)
        h = mm(n2, wu[:, part]) + vec_ref[8:9, part]
        h_ref[:, part] = h
        x2 += mm((h * gelu_parts(h)[0]).astype(B), wd[part, :])
    x2_ref[...] = x2
    hat, unused = norm_rows(x2)
    loads[5].wait()
    latent_ref[...] = mm((hat * vec_ref[10:11, :D] + vec_ref[11:12, :D]).astype(B), wp[...])


def enc_forward(pixels, places, q_marks, k_marks, vec, mats):
    rows = pixels.shape[0]
    hbm, vmem = pl.BlockSpec(memory_space=pl.ANY), pl.BlockSpec(memory_space=pltpu.VMEM)
    outs = [(DD, F), (D, F), (3 * D, B), (D, B), (D, F), (FF, F), (D, F)]
    return pl.pallas_call(
        enc_forward_kernel,
        in_specs=[vmem] * 5 + [hbm] * 6,
        out_specs=[vmem] * 7,
        out_shape=[jax.ShapeDtypeStruct((rows, width), kind) for width, kind in outs],
        scratch_shapes=[pltpu.VMEM(m.shape, B) for m in mats] + [pltpu.SemaphoreType.DMA((6,))],
        compiler_params=pltpu.CompilerParams(vmem_limit_bytes=VMEM_LIMIT),
        cost_estimate=pl.CostEstimate(flops=15 * 10**9, bytes_accessed=20 << 20, transcendentals=0),
        name="enc_forward",
    )(pixels, places, q_marks, k_marks, vec, *mats)


def put_product(lin, top, row, left, right):
    m, c = left.shape[0], right.shape[1] // 128
    step = min(m, 768)
    most = top[...]
    for r in range(0, m, step):
        for first in range(0, c, 2):
            last = min(first + 2, c)
            value = mm(left[r : r + step, :], right[:, first * 128 : last * 128])
            for i in range(first, last):
                piece = value[:, (i - first) * 128 : (i - first + 1) * 128]
                lin[pl.ds(row + r * c + i, step, stride=c), :] = piece
                most = jnp.maximum(most, jnp.max(jnp.abs(piece).reshape(-1, 8, 128), axis=0))
    top[...] = most


def put_vector(lin, top, row, value):
    for i in range(value.shape[1] // 128):
        piece = value[:, i * 128 : (i + 1) * 128]
        lin[pl.ds(row + i, 1), :] = piece
        top[0:1, :] = jnp.maximum(top[0:1, :], jnp.abs(piece))


def turned(value):
    return value.astype(F).T.astype(B)


def flush_start(lin, base, segments, core, kept, away, sem):
    for c in range(2):

        @pl.when(core == c)
        def _():
            for source, count, s, h, k, y, to in segments:
                target = (kept if h == c else away)[k]
                pltpu.make_async_copy(
                    lin.at[pl.ds(source - base, count)], target.at[s, y, pl.ds(to, count)], sem
                ).start()


def flush_wait(lin, segments, sem):
    count = sum(segment[1] for segment in segments)
    pltpu.make_async_copy(lin.at[pl.ds(0, count)], lin.at[pl.ds(0, count)], sem).wait()


def enc_back_one_kernel(
    base, rows_of, cuts, core_ref, vis_ref, live_ref, dx0_ref, x1_ref, h_ref, x2_ref, vec_ref, wu_hbm, wd_hbm, wp_hbm,
    dx1_ref, top_ref, *refs,
):
    chunks = (len(refs) - 7) // 2
    kept, away = refs[:chunks], refs[chunks : 2 * chunks]
    lin, wu, wd, wp, dl_ref, dh_ref, sems = refs[-7:]
    loads = [
        pltpu.make_async_copy(source, target, sems.at[i])
        for i, (source, target) in enumerate(zip((wp_hbm, wd_hbm, wu_hbm), (wp, wd, wu)))
    ]
    for load in loads:
        load.start()
    top_ref[...] = jnp.zeros_like(top_ref)
    upb, down, db, fg, fb, proj, end, last = (r - base for r in rows_of[1:])

    def take_slot(i, carry):
        at = pl.ds(jnp.minimum(vis_ref[i], ROWS - 1), 1)
        dl_ref[pl.ds(i, 1), :] = dx0_ref[at, :] * live_ref[i]
        return carry

    lax.fori_loop(0, dl_ref.shape[0], take_slot, 0, unroll=8)
    dl = dl_ref[...].astype(B)
    hatf, invf = norm_rows(x2_ref[...])
    put_product(lin, top_ref, proj, turned(hatf * vec_ref[10:11, :D] + vec_ref[11:12, :D]), dl)
    lin[pl.ds(end, lin.shape[0] - end), :] = jnp.zeros((lin.shape[0] - end, 128), F)
    loads[0].wait()
    dnf = mm(dl, wp[...], NT)
    put_vector(lin, top_ref, fg, total(dnf * hatf))
    put_vector(lin, top_ref, fb, total(dnf))
    dx2 = norm_back(dnf * vec_ref[10:11, :D], hatf, invf)
    put_vector(lin, top_ref, db, total(dx2))
    dx2b = dx2.astype(B)
    loads[1].wait()
    for i in range(4):
        part = slice(i * D, (i + 1) * D)
        h = h_ref[:, part]
        kept_share, slope = gelu_parts(h)
        put_product(lin, top_ref, down + i * D * (D // 128), turned(h * kept_share), dx2b)
        dh = mm(dx2b, wd[part, :], NT) * slope
        put_vector(lin, top_ref, upb + i * (D // 128), total(dh))
        dh_ref[:, part] = dh.astype(B)
    flush_start(lin, base, cuts[0], core_ref[0], kept, away, sems.at[3])
    loads[2].wait()
    hat2, inv2 = norm_rows(x1_ref[...])
    put_product(lin, top_ref, 0, turned(hat2 * vec_ref[6:7, :D] + vec_ref[7:8, :D]), dh_ref[...])
    flush_start(lin, base, cuts[1], core_ref[0], kept, away, sems.at[4])
    dn2 = mm(dh_ref[...], wu[...], NT)
    dx1_ref[0:1, :] = jnp.zeros((1, D), F)
    dx1 = dx2 + norm_back(dn2 * vec_ref[6:7, :D], hat2, inv2)
    count = dx1.shape[0]
    dx1_ref[0:count, :] = dx1
    dx1_ref[count : count + 1, :] = total(dn2 * hat2)
    dx1_ref[count + 1 : count + 2, :] = total(dn2)
    flush_wait(lin, cuts[0], sems.at[3])
    flush_wait(lin, cuts[1], sems.at[4])


def enc_back_two_kernel(
    rows_of, early_of, base_early, cuts, core_ref, dx1_ref, pix_ref, e0_ref, qkv_ref, a_ref, qm_ref, km_ref, vec_ref,
    g_qkv_ref, g_one_ref, wq_hbm, wo_hbm, top_in, *refs,
):
    chunks = (len(refs) - 6) // 4
    top_ref = refs[2 * chunks]
    kept, away = refs[2 * chunks + 1 : 3 * chunks + 1], refs[3 * chunks + 1 : 4 * chunks + 1]
    lin, wq, wo, dp_ref, sems = refs[-5:]
    loads = [
        pltpu.make_async_copy(source, target, sems.at[i])
        for i, (source, target) in enumerate(zip((wo_hbm, wq_hbm), (wo, wq)))
    ]
    for load in loads:
        load.start()
    top_ref[...] = top_in[...]
    embed, eb, g1, b1, qkv, qbias, vbias, out, ob, g2, b2 = rows_of
    count = pix_ref.shape[0]
    dx1 = dx1_ref[0:count, :]
    put_vector(lin, top_ref, g2, dx1_ref[count : count + 1, :])
    put_vector(lin, top_ref, b2, dx1_ref[count + 1 : count + 2, :])
    put_vector(lin, top_ref, ob, total(dx1))
    dx1b = dx1.astype(B)
    put_product(lin, top_ref, out, turned(a_ref[...]), dx1b)
    loads[0].wait()
    da = mm(dx1b, wo[...], NT).astype(B)
    marks = (qm_ref[...], km_ref[...])
    for j in range(HEADS // 2):
        q, k, v, qs, ks = enc_pair(qkv_ref, marks, j)
        low, zero = low_lanes(count), jnp.zeros_like(q)
        dz = halves(low, da[:, j * 128 : (j + 1) * 128], zero)
        scores = [mm(ks[i], qs[i], NT) for i in range(2)]
        dps = [mm(v, d, NT) for d in dz]
        ps, dss, dq = [], [], jnp.zeros((128, count), F)
        for i, keys in enumerate(halves(low, k, zero)):
            p = softmax_keys(scores[i])[0]
            ps.append(p.astype(B))
            dss.append((p * (dps[i] - jnp.sum(p * dps[i], axis=0, keepdims=True))).astype(B))
            dq += mm(keys, dss[i], TN)
        dk = mm(jnp.concatenate(dss, axis=1), jnp.concatenate(halves(low, q, zero), axis=0))
        dv = mm(jnp.concatenate(ps, axis=1), jnp.concatenate(dz, axis=0))
        for i, value in enumerate((dq.T * 0.125, dk, dv)):
            dp_ref[:, i * D + j * 128 : i * D + (j + 1) * 128] = value.astype(B)
    dp = dp_ref[...]
    sums = total(dp.astype(F))
    put_vector(lin, top_ref, qbias, sums[:, :D])
    put_vector(lin, top_ref, vbias, sums[:, 2 * D :])
    hat, inverse = norm_rows(e0_ref[...])
    put_product(lin, top_ref, qkv, turned(hat * vec_ref[1:2, :D] + vec_ref[2:3, :D]), dp)
    loads[1].wait()
    dn = mm(dp, wq[...], NT)
    put_vector(lin, top_ref, g1, total(dn * hat))
    put_vector(lin, top_ref, b1, total(dn))
    de0 = dx1 + norm_back(dn * vec_ref[1:2, :D], hat, inverse)
    put_vector(lin, top_ref, eb, total(de0))
    flush_start(lin, 0, cuts[0], core_ref[0], kept, away, sems.at[2])
    put_product(lin, top_ref, embed, turned(pix_ref[...]), de0.astype(B))
    c = g_qkv_ref.shape[1] // 128
    start = early_of[3]
    most = top_ref[...]
    for i in range(c):
        piece = g_qkv_ref[:, i * 128 : (i + 1) * 128]
        lin[pl.ds(start + i, g_qkv_ref.shape[0], stride=c), :] = piece
        most = jnp.maximum(most, jnp.max(jnp.abs(piece).reshape(-1, 8, 128), axis=0))
    top_ref[...] = most
    one = g_one_ref
    for row, value in zip(
        early_of[:3] + early_of[4:6],
        (one[3:4, :DD], one[0:1, :DD], one[1:2, :DD], one[2:3, :DD], one[2:3, 2 * DD :]),
    ):
        put_vector(lin, top_ref, row, value)
    end = early_of[6]
    lin[pl.ds(end, lin.shape[0] - end), :] = jnp.zeros((lin.shape[0] - end, 128), F)
    flush_start(lin, 0, cuts[1], core_ref[0], kept, away, sems.at[3])
    flush_start(lin, base_early, cuts[2], core_ref[0], kept, away, sems.at[4])
    for i in range(3):
        flush_wait(lin, cuts[i], sems.at[2 + i])


class Flat:
    def __init__(self, sections, wide, narrow, chunks):
        self.wide, self.narrow, self.sections = wide, narrow, sections
        self.spans = [-(-(rows + (0 if rows % 8 == 0 else 7)) // 8) * 8 for unused, rows in sections]
        self.parts = [-(-span // (narrow * 16)) * 16 for span in self.spans]
        self.starts = [sum(self.parts[i + 1 :]) for i in range(len(sections))]
        rows = sum(self.parts)
        step = -(-rows // (chunks * 16)) * 16
        self.chunks = [min(step, rows - i * step) for i in range(chunks)]
        self.shapes = [jax.ShapeDtypeStruct((wide, narrow // 2, count, 128), F) for count in self.chunks]

    def segments(self, section, low, high):
        first, rows = self.sections[section]
        part, span, at = self.parts[section], self.spans[section], self.starts[section]
        out = []
        for s in range(self.wide):
            start = first + s * rows // 8 * 8
            for p in range(self.narrow):
                begin = 0
                for k, count in enumerate(self.chunks):
                    lead = start + p * part - at + begin
                    a = max(low, start + p * part, lead)
                    b = min(high, start + span, start + (p + 1) * part, lead + count)
                    if a < b:
                        out.append((a, b - a, s, p // 2, k, p % 2, a - lead))
                    begin += count
        return out

    def reach(self, section):
        first, rows = self.sections[section]
        return first + (self.wide - 1) * rows // 8 * 8 + self.spans[section]

    def offset(self, section, index):
        return lax.rem(index * self.sections[section][1], 8)

    def of(self, piece, section):
        return piece[self.starts[section] : self.starts[section] + self.parts[section]]

    def squares(self, piece, section, index, part):
        value = self.of(piece, section)
        row = part * self.parts[section] + jnp.arange(value.shape[0], dtype=jnp.int32)[:, None]
        at = self.offset(section, index)
        inside = (row >= at) & (row < at + self.sections[section][1])
        return jnp.sum(jnp.where(inside, value * value, 0.0))

    def take(self, window, section, index):
        return lax.dynamic_slice_in_dim(window, self.offset(section, index), self.sections[section][1])


def enc_back_one(core, visible, live, dx0, saved, vec, mats, flat):
    x1, h, x2 = saved[3:]
    wu, wd, wp = mats[3:]
    rows = x1.shape[0]
    pieces = [p[0] for p in table(ENC_SHAPES)]
    end = pieces[-1] + DD // 128 * D
    total_rows = flat.sections[0][1] * flat.wide
    reach = max(flat.reach(0), total_rows)
    rows_of = tuple(pieces[11:]) + (end, reach)
    base, split = pieces[11], pieces[13]
    smem, vmem, hbm = (
        pl.BlockSpec(memory_space=space) for space in (pltpu.SMEM, pltpu.VMEM, pl.ANY)
    )
    top = jax.ShapeDtypeStruct((8, 128), F)
    cuts = (flat.segments(0, split, reach), flat.segments(0, base, split))
    room = max([reach - base] + [sum(seg[1] for seg in cut) for cut in cuts])
    chunks = len(flat.chunks)
    dx1, top, *out = pl.pallas_call(
        functools.partial(enc_back_one_kernel, base, rows_of, cuts),
        in_specs=[smem] * 3 + [vmem] * 5 + [hbm] * 3,
        out_specs=[vmem] * 2 + [hbm] * (2 * chunks),
        out_shape=[jax.ShapeDtypeStruct((rows + 8, D), F), top] + flat.shapes * 2,
        scratch_shapes=[
            pltpu.VMEM((room, 128), F), pltpu.VMEM(wu.shape, B), pltpu.VMEM(wd.shape, B),
            pltpu.VMEM(wp.shape, B), pltpu.VMEM((rows, DD), F),
            pltpu.VMEM((rows, FF), B), pltpu.SemaphoreType.DMA((5,)),
        ],
        compiler_params=pltpu.CompilerParams(vmem_limit_bytes=VMEM_LIMIT),
        cost_estimate=pl.CostEstimate(flops=20 * 10**9, bytes_accessed=30 << 20, transcendentals=0),
        name="enc_back_one",
    )(core, visible, live, dx0, x1, h, x2, vec, wu, wd, wp)
    return dx1, top, out


def enc_back_two(core, dx1, top, out, saved, pixels, marks, vec, mats, g_qkv, g_one, flat):
    e0, qkv, a = saved[:3]
    wq, wo = mats[1:3]
    rows = pixels.shape[0]
    pieces = [p[0] for p in table(ENC_SHAPES)]
    base = pieces[11]
    early_rows = table(DEC_SHAPES[:6])
    first = flat.sections[1][0]
    last = early_rows[-1][0] + early_rows[-1][2]
    early_of = tuple(base + p[0] for p in early_rows) + (base + last,)
    reach = max(flat.reach(1) - first, last)
    cuts = (
        flat.segments(0, pieces[1] // 8 * 8, base), flat.segments(0, 0, pieces[1] // 8 * 8),
        flat.segments(1, first, first + reach),
    )
    room = max([base + reach] + [sum(seg[1] for seg in cut) for cut in cuts])
    smem, vmem, hbm = (
        pl.BlockSpec(memory_space=space) for space in (pltpu.SMEM, pltpu.VMEM, pl.ANY)
    )
    chunks = len(flat.chunks)
    top, *out = pl.pallas_call(
        functools.partial(enc_back_two_kernel, tuple(pieces[:11]), early_of, first - base, cuts),
        in_specs=[smem] + [vmem] * 10 + [hbm] * 2 + [vmem] + [hbm] * (2 * chunks),
        out_specs=[vmem] + [hbm] * (2 * chunks),
        out_shape=[jax.ShapeDtypeStruct((8, 128), F)] + flat.shapes * 2,
        input_output_aliases={14 + i: 1 + i for i in range(2 * chunks)},
        scratch_shapes=[
            pltpu.VMEM((room, 128), F), pltpu.VMEM(wq.shape, B), pltpu.VMEM(wo.shape, B),
            pltpu.VMEM((rows, 3 * D), B), pltpu.SemaphoreType.DMA((5,)),
        ],
        compiler_params=pltpu.CompilerParams(vmem_limit_bytes=VMEM_LIMIT),
        cost_estimate=pl.CostEstimate(flops=15 * 10**9, bytes_accessed=30 << 20, transcendentals=0),
        name="enc_back_two",
    )(core, dx1, pixels, e0, qkv, a, *marks, vec, g_qkv, g_one, wq, wo, top, *out)
    return out[:chunks], out[chunks:], top


def table(shapes, row=0):
    out = []
    for s in shapes:
        m, c = (s[0], s[1] // 128) if len(s) == 2 else (1, s[0] // 128)
        out.append((row, m, c))
        row += m * c
    return out


def job_rows(m, c, most):
    return max(n for n in range(16, m + 1, 16) if m % n == 0 and n * c <= most)


def split_rows(shard, shares, note):
    out, place, first = [], 0, 0
    for i in range(len(shares) + 1):
        rows = shard * shares[i] / 100 if i < len(shares) else (shard - first) / 4
        rows = math.ceil(rows / 16) * 16
        used = rows - 1 if note and i == 0 else rows
        out.append((place, first, 4, rows, used))
        place, first = place + 4 * rows, first + 4 * used
    return out


def unpack_kernel(pieces, groups, leads, ways, span, wide, mine_ref, *refs):
    mats = [p for p in pieces if p[1] > 1]
    sources = [refs[4 * g : 4 * g + 4] for g in range(len(groups))]
    refs = refs[4 * len(groups) :]
    outs, vec_ref = refs[: len(mats)], refs[len(mats)]
    buf, lin, in_sem, out_sem = refs[len(mats) + 1 : len(mats) + 5]
    stages = refs[len(mats) + 5 :]
    bits = wide.bit_length()
    plans, size = [], 0
    for (place, first, parts, rows, used), lead in zip(groups, leads):
        plan = []
        for i in range(parts):
            a, b = first + i * used, min(first + (i + 1) * used, span)
            if a < b:
                plan.append((i // 2, i % 2, lead, rows, size, a, b - a))
                size += rows
        plans.append(plan)

    for g, (plan, (last, way)) in enumerate(zip(plans, ways)):
        for core in range(2):
            for side in range(2):

                @pl.when((mine_ref[0] == core) & (mine_ref[1 + g] == side))
                def _():
                    for s in range(wide):
                        for c, y, low, rows, to, at, count in plan:
                            index = [s >> (bits - 2 - j) & 1 for j in range(bits - 1)] + [y]
                            source = sources[g][2 * (c != core) + (index[last] != side)]
                            index = sum(index[j] << (len(way) - 1 - i) for i, j in enumerate(way))
                            pltpu.make_async_copy(
                                source.at[index, pl.ds(low, rows)], buf.at[s, pl.ds(to, rows)], in_sem.at[s]
                            ).start()

    for s in range(wide):
        pltpu.make_async_copy(buf.at[s, pl.ds(0, size)], buf.at[s, pl.ds(0, size)], in_sem.at[s]).wait()
        for plan in plans:
            for c, y, low, rows, to, at, count in plan:
                lin[pl.ds(s * span + at, count), :] = buf[s, pl.ds(to, rows), :].astype(F)[:count]

    vec_ref[...] = jnp.zeros_like(vec_ref)
    v = 0
    for row, m, c in pieces:
        if m == 1:
            for j in range(c):
                vec_ref[v : v + 1, j * 128 : (j + 1) * 128] = lin[pl.ds(row + j, 1), :]
            v += 1
    open_stores = []
    for k, (row, m, c) in enumerate(mats):
        stage, out = stages[k], outs[k]
        n = stage.shape[1]
        jobs = m // n

        def store(j, slot, k=k, stage=stage, out=out, n=n):
            return pltpu.make_async_copy(
                stage.at[slot], out.at[pl.ds(pl.multiple_of(j * n, 16), n)], out_sem.at[k, slot]
            )

        def job(j, carry):
            slot = lax.rem(j, SLOTS)

            @pl.when(j >= SLOTS)
            def _():
                store(j - SLOTS, slot).wait()

            for i in range(c):
                rows = pl.ds(row + i + j * (n * c), n, stride=c)
                stage[slot, :, i * 128 : (i + 1) * 128] = lin[rows, :].astype(B)
            store(j, slot).start()
            return carry

        lax.fori_loop(0, jobs, job, 0)
        open_stores += [(store, j) for j in range(max(jobs - SLOTS, 0), jobs)]
    for store, j in open_stores:
        store(j, j % SLOTS).wait()


def unpack_flat(arrays, groups, leads, ways, mine, span, wide, shapes, name):
    pieces = table(shapes)
    mats = [s for s in shapes if len(s) == 2]
    vectors = [s for s in shapes if len(s) == 1]
    width = max(s[0] for s in vectors)
    count = -(-len(vectors) // 8) * 8
    hbm = pl.BlockSpec(memory_space=pl.ANY)
    stages = [pltpu.VMEM((SLOTS, job_rows(s[0], s[1] // 128, 1152), s[1]), B) for s in mats]
    room = groups[-1][0] + groups[-1][2] * groups[-1][3]
    return pl.pallas_call(
        functools.partial(unpack_kernel, pieces, groups, leads, ways, span, wide),
        in_specs=[pl.BlockSpec(memory_space=pltpu.SMEM)] + [hbm] * len(arrays),
        out_specs=[hbm] * len(mats) + [pl.BlockSpec(memory_space=pltpu.VMEM)],
        out_shape=[jax.ShapeDtypeStruct(s, B) for s in mats] + [jax.ShapeDtypeStruct((count, width), F)],
        scratch_shapes=[
            pltpu.VMEM((wide, room, 128), B), pltpu.VMEM((wide * span, 128), F),
            pltpu.SemaphoreType.DMA((wide,)), pltpu.SemaphoreType.DMA((len(mats), SLOTS)),
        ] + stages,
        compiler_params=pltpu.CompilerParams(vmem_limit_bytes=VMEM_LIMIT),
        cost_estimate=pl.CostEstimate(flops=0, bytes_accessed=wide * span * 1536, transcendentals=0),
        name=name,
    )(mine, *arrays)


def pack_kernel(pieces, segments, core_ref, *refs):
    mats = [p for p in pieces if p[1] > 1]
    ins, vec_ref = refs[: len(mats)], refs[len(mats)]
    top_ref, *out = refs[len(mats) + 1 : -2]
    kept, away = out[: len(out) // 2], out[len(out) // 2 :]
    lin, sem = refs[-2:]
    first, end = pieces[0][0], pieces[-1][0] + pieces[-1][1] * pieces[-1][2]
    lin[pl.ds(0, first), :] = jnp.zeros((first, 128), F)
    lin[pl.ds(end, lin.shape[0] - end), :] = jnp.zeros((lin.shape[0] - end, 128), F)
    top_ref[...] = jnp.zeros_like(top_ref)
    k, v = 0, 0
    for row, m, c in pieces:
        if m == 1:
            put_vector(lin, top_ref, row, vec_ref[v : v + 1, : c * 128])
            v += 1
            continue
        most = top_ref[...]
        for i in range(c):
            piece = ins[k][:, i * 128 : (i + 1) * 128]
            lin[pl.ds(row + i, m, stride=c), :] = piece
            most = jnp.maximum(most, jnp.max(jnp.abs(piece).reshape(-1, 8, 128), axis=0))
        top_ref[...] = most
        k += 1
    flush_start(lin, 0, segments, core_ref[0], kept, away, sem)
    flush_wait(lin, segments, sem)


def pack_late(mats, vectors, pieces, flat, core, name):
    hbm, vmem = pl.BlockSpec(memory_space=pl.ANY), pl.BlockSpec(memory_space=pltpu.VMEM)
    segments = flat.segments(0, 0, flat.reach(0))
    room = max(flat.reach(0), flat.wide * flat.sections[0][1], sum(seg[1] for seg in segments))
    chunks = len(flat.chunks)
    unused, *out = pl.pallas_call(
        functools.partial(pack_kernel, pieces, segments),
        in_specs=[pl.BlockSpec(memory_space=pltpu.SMEM)] + [vmem] * (len(mats) + 1),
        out_specs=[vmem] + [hbm] * (2 * chunks),
        out_shape=[jax.ShapeDtypeStruct((8, 128), F)] + flat.shapes * 2,
        scratch_shapes=[pltpu.VMEM((room, 128), F), pltpu.SemaphoreType.DMA],
        compiler_params=pltpu.CompilerParams(vmem_limit_bytes=VMEM_LIMIT),
        cost_estimate=pl.CostEstimate(flops=0, bytes_accessed=30 << 20, transcendentals=0),
        name=name,
    )(core, *mats, vectors)
    return out[:chunks], out[chunks:]


class Links:
    def __init__(self, mesh):
        self.narrow, self.wide = mesh.shape["narrow"], mesh.shape["wide"]
        self.wide_bits = [("wide", b) for b in reversed(range(self.wide.bit_length() - 1))]
        self.x, self.upper = self.wide_bits[-1], self.wide_bits[:-1]
        self.y, self.core = ("narrow", 1), ("narrow", 0)

    def mine(self, bit):
        return (lax.axis_index(bit[0]) >> bit[1]) & 1

    def swap(self, value, bit):
        mask = 1 << bit[1] if bit[0] == "wide" else self.wide << bit[1]
        pairs = [(i, i ^ mask) for i in range(self.narrow * self.wide)]
        return lax.ppermute(value, AXES, pairs)

    def everyone(self, value, bits):
        for bit in bits:
            value = value + self.swap(value, bit)
        return value

    def gather(self, value, order):
        group = Group(self, value, order)
        while group.order:
            group.step()
        return group.value

    def scatter_parts(self, kept, other, bound=None):
        axes = self.wide_bits + [self.y]
        parts, orders = [], [[self.x, self.y] + self.upper, [self.y, self.x] + self.upper]
        for i, (one, two) in enumerate(zip(kept, other)):
            one, two = (v.reshape((2,) * len(axes) + v.shape[2:]) for v in (one, two))
            parts.append(Part(self, one, two, axes, orders[i % 2], bound))
        return parts


class Group:
    def __init__(self, links, value, order):
        self.links, self.value, self.order, self.have = links, value, list(order), []

    def step(self):
        bit = self.order.pop(0)
        other = self.links.swap(self.value, bit)
        low = self.links.mine(bit) == 0
        self.have.insert(0, bit)
        self.value = jnp.stack([jnp.where(low, self.value, other), jnp.where(low, other, self.value)])


class Part:
    def __init__(self, links, kept, other, axes, order, bound):
        self.links, self.kept, self.other, self.axes, self.order = links, kept, other, list(axes), list(order)
        self.bound, self.rows, self.received = bound, kept.shape[-2], None

    def away(self):
        self.arrive()
        bit = self.order[0]
        self.place, self.index = self.axes.index(bit), self.links.mine(bit)
        value = self.take(1 - self.index)
        if self.bound is None or len(self.order) == 1:
            return value
        power = jnp.clip(jnp.floor(14.0 - jnp.log2(jnp.maximum(self.bound, 1e-30))), -100.0, 100.0)
        note = jnp.broadcast_to(power, value.shape[:-2] + (8, 128))
        return jnp.concatenate([value * jnp.exp2(power), note], axis=-2).astype(jnp.float16)

    def take(self, index):
        cut = lambda value: lax.dynamic_index_in_dim(value, index, self.place, keepdims=False)[..., : self.rows, :]
        return cut(self.kept) + cut(self.other)

    def exchange(self, away):
        bit = self.order.pop(0)
        self.kept, self.received = self.take(self.index), self.links.swap(away, bit)
        self.axes.pop(self.place)

    def arrive(self, token=()):
        if self.received is None:
            return
        received, self.received = after(self.received, *token), None
        if received.dtype == jnp.float16:
            power = received[(0,) * (received.ndim - 2) + (self.rows, 0)].astype(F)
            received = received[..., : self.rows, :].astype(F) * jnp.exp2(-power)
            self.bound = self.bound + jnp.exp2(15.0 - power)
        self.other = received

    def finish(self):
        while self.order:
            self.exchange(self.away())
        self.arrive()
        return self.kept + self.other


def after(value, *others):
    return lax.optimization_barrier((value,) + others)[0]


def gather_params(enc, dec, note, links):
    orders = (
        links.upper[:-1] + [links.x, links.y] + links.upper[-1:],
        links.upper + [links.x, links.y], links.upper + [links.y, links.x],
    )
    tables = split_rows(enc.shape[0], (8.5, 8), False), split_rows(dec.shape[0], (8.5, 8), True)
    part = links.mine(links.core) * 2 + links.mine(links.y)
    padded = [
        jnp.pad(v, ((0, t[-1][1] + 4 * t[-1][4] - v.shape[0]), (0, 0))) for v, t in zip((enc, dec), tables)
    ]
    arrays, ways, mine = [], [], [links.mine(links.core)]
    for g, order in enumerate(orders):
        pieces = []
        for v, t in zip(padded, tables):
            unused, first, parts, rows, used = t[g]
            pieces.append(lax.dynamic_slice_in_dim(v, first + part * used, used))
            if used < rows:
                pieces.append(note)
        group = Group(links, jnp.concatenate(pieces), order)
        while len(group.order) > 1:
            group.step()
        last = group.order[0]
        both = [group.value, links.swap(group.value, last)]
        both += [links.swap(v, links.core) for v in both]
        arrays += [v.reshape((-1,) + v.shape[-2:]) for v in both]
        bits = links.wide_bits + [links.y]
        ways.append((bits.index(last), tuple(bits.index(b) for b in group.have)))
        mine.append(links.mine(last))
    at = tables[0][0][3] + tables[1][0][4]
    notes = sum(jnp.sum(v[:, at, :2].astype(F), axis=0) for v in arrays[:4])
    return arrays, tables, tuple(ways), jnp.stack(mine).astype(jnp.int32), notes


def join_shard(piece, links):
    return links.gather(piece, [links.y, links.core])


def adamw_update(master, gradient, moment_one, moment_two, clip_scale):
    gradient = gradient * clip_scale
    moment_one = BETA_ONE * moment_one + (1.0 - BETA_ONE) * gradient
    moment_two = BETA_TWO * moment_two + (1.0 - BETA_TWO) * gradient * gradient
    first_hat = moment_one / (1.0 - BETA_ONE**STEP)
    second_hat = moment_two / (1.0 - BETA_TWO**STEP)
    updated = master - learn_rate * (
        first_hat / (jnp.sqrt(second_hat) + EPSILON) + weight_decay * master
    )
    return (moment_one, moment_two, updated)


def body(
    links, vis_pixels, target, clip_lens, vis_index, params_enc, m_enc, v_enc, params_dec, m_dec, v_dec
):
    lengths = clip_lens[0]
    visible = vis_index[0]
    mine, core = lax.axis_index("wide"), links.mine(links.core).astype(jnp.int32).reshape(1)
    enc_shard, dec_shard = (v.shape[0] // 128 for v in (params_enc, params_dec))
    segment, clip_place, slot_live, shown_flag, counted = layout(lengths, visible, target.shape[0])

    here = jnp.sum(counted).astype(jnp.int32)
    note = jnp.pad(jnp.stack([here // 64, here % 64]), (0, 126))[None, :].astype(B)
    arrays, tables, ways, sides, notes = gather_params(
        params_enc.astype(B).reshape(-1, 128), params_dec.astype(B).reshape(-1, 128), note, links
    )
    *enc_mats, enc_vec = unpack_flat(
        arrays, tables[0], (0, 0, 0), ways, sides, enc_shard, links.wide, ENC_SHAPES, "unpack_enc"
    )
    masked_count = notes[0] * 64.0 + notes[1]
    cotangent = 1.0 / masked_count

    segment, clip_place, shown_flag, counted = (
        v[:ROWS] for v in (segment, clip_place, shown_flag, counted)
    )
    rows = jnp.stack([counted, counted * (cotangent * (2.0 / PIX)), 1.0 - shown_flag], axis=1)
    rows = jnp.pad(rows, ((0, 0), (0, 125)))
    lane = jnp.arange(128, dtype=jnp.int32)[None, :] % 64

    def marks_of(labels):
        mark = lane == labels[:, None]
        return mark.astype(B), jnp.where(mark | (lane > 3), 0.0, -1e30).astype(B)

    q_marks, k_marks = marks_of(segment)
    slot_segment, slot_place = slot_layout(lengths, visible)
    slot_marks = marks_of(slot_segment)

    latent, *saved = enc_forward(vis_pixels, sinusoid(slot_place, D), *slot_marks, enc_vec, enc_mats)
    arrays[0] = after(arrays[0], latent)
    *dec_mats, dec_vec = unpack_flat(
        arrays, tables[1], tuple(t[3] for t in tables[0]), ways, sides, dec_shard, links.wide, DEC_SHAPES, "unpack_dec"
    )
    w_qkv, w_out, w_up, w_down, w_head = dec_mats
    bias = jnp.concatenate([dec_vec[3, :DD], jnp.zeros((DD,), F), dec_vec[4, :DD]])
    vec_one = stack_rows([dec_vec[1, :DD], dec_vec[2, :DD], bias], 3 * DD)
    vec_two = jnp.concatenate([dec_vec[5:13], jnp.zeros((8, DFF), F)])
    x0, qkv = qkv_forward(
        visible, slot_live, latent, sinusoid(clip_place, DD), rows, w_qkv, vec_one, dec_vec
    )
    a, lse = attend_forward(qkv, q_marks, k_marks)
    da, dx1, dd, g_out, g_up, g_down, g_head, g_two = mlp_both(
        x0, a, target, rows, w_out, w_up, w_down, w_head, vec_two
    )

    late_flat = Flat([(0, dec_shard)], links.wide, links.narrow, 2)
    kept, away = pack_late(
        [g_out, g_up, g_down, g_head], g_two, table(DEC_SHAPES)[6:], late_flat, core, "pack_dec"
    )
    back = lambda da, h: attend_back(qkv, q_marks, k_marks, da, lse, dd, h)
    da, away = lax.optimization_barrier((da, away))
    late = links.scatter_parts(kept, [links.swap(v, links.core) for v in away])
    dqkv = [back(da, 0)]
    for h in (1, 2):
        sent = [part.away() for part in late]
        da, sent, dqkv = lax.optimization_barrier((da, sent, dqkv))
        dqkv = dqkv + [back(da, h)]
        for part, value in zip(late, sent):
            part.exchange(value)
    sent = [part.away() for part in late]
    dx1, sent, dqkv = lax.optimization_barrier((dx1, sent, dqkv))
    dx0, g_qkv, g_one = qkv_back(x0, dx1, dqkv, rows, w_qkv, vec_one)
    for part, value in zip(late, sent):
        part.exchange(value)

    early = table(DEC_SHAPES[:6])
    early_count = early[-1][0] + early[-1][2]
    flat = Flat(
        [(0, enc_shard), (enc_shard * links.wide, -(-early_count // (8 * links.wide)) * 8)], links.wide, links.narrow, 2
    )
    dx1, top, out = enc_back_one(core, visible, slot_live, dx0, saved, enc_vec, enc_mats, flat)
    sent = [part.away() for part in late]
    dx1, sent = lax.optimization_barrier((dx1, sent))
    kept, away, top = enc_back_two(
        core, dx1, top, out, saved, vis_pixels, slot_marks, enc_vec, enc_mats, g_qkv, g_one, flat
    )
    for part, value in zip(late, sent):
        part.exchange(value)
    beside = links.swap(top, links.core)
    first = [links.swap(after(v, beside), links.core) for v in away[:1]]
    second = [links.swap(after(v, *first), links.core) for v in away[1:]]
    parts = links.scatter_parts(kept, first + second, jnp.max(top + beside))
    for unused in range(len(parts[0].order)):
        for part in parts:
            part.exchange(part.away())
    piece_dec = jnp.concatenate([part.finish() for part in late])
    chunks = [part.finish() for part in parts]
    piece = jnp.concatenate(chunks)

    part = links.mine(links.core) * 2 + links.mine(links.y)
    squares = flat.squares(piece, 0, mine, part) + flat.squares(piece, 1, mine, part)
    squares += late_flat.squares(piece_dec, 0, mine, part)
    sums = links.everyone(jnp.stack([squares, jnp.sum(g_two[8]) / PIX]), [links.y])
    chunks[-1] = after(chunks[-1], sums)
    sides = [links.swap(chunk, links.y) for chunk in chunks]
    sums = links.everyone(sums, [links.core] + links.wide_bits[:-1])
    sides[-1] = after(sides[-1], sums)
    squares, loss_sum = links.everyone(sums, links.wide_bits[-1:])
    low = links.mine(links.y) == 0
    joined = [
        jnp.stack([jnp.where(low, one, two), jnp.where(low, two, one)]) for one, two in zip(chunks, sides)
    ]
    joined = jnp.concatenate([links.gather(v, [links.core]) for v in joined], axis=2)
    joined = joined[:, :, flat.starts[0] :].reshape(-1, 128)
    joined_late = join_shard(piece_dec, links).reshape(-1, 128)
    grad_norm = jnp.sqrt(squares)
    clip_scale = jnp.minimum(1.0, clip_norm / (grad_norm + 1e-06))
    order = links.upper + [links.x, links.y, links.core]
    everywhere = links.gather(chunks[0][: flat.parts[1]], order)
    places = [order[::-1].index(bit) for bit in links.wide_bits + [links.core, links.y]]
    everywhere = everywhere.transpose(places + [len(places), len(places) + 1]).reshape(links.wide, -1, 128)
    early_sum = everywhere[:, : flat.sections[1][1]].reshape(-1, 128)
    early_sum = jnp.pad(early_sum, ((0, dec_shard), (0, 0)))
    start = jnp.minimum(mine * dec_shard, early_sum.shape[0] - dec_shard)
    grad_enc = flat.take(joined, 0, mine).reshape(-1)
    grad_dec = late_flat.take(joined_late, 0, mine) + lax.dynamic_slice_in_dim(early_sum, start, dec_shard)
    enc_one, enc_two, enc_new = adamw_update(params_enc, grad_enc, m_enc, v_enc, clip_scale)
    dec_one, dec_two, dec_new = adamw_update(
        params_dec, grad_dec.reshape(-1), m_dec, v_dec, clip_scale
    )
    return (loss_sum, masked_count, grad_norm, enc_one, enc_two, enc_new, dec_one, dec_two, dec_new)


def solution(mesh):
    placed = (P(AXES, None),) * 4 + (P("wide"),) * 6
    return jax.shard_map(
        functools.partial(body, Links(mesh)),
        mesh=mesh,
        in_specs=placed,
        out_specs=(P(), P(), P()) + (P("wide"),) * 6,
        check_vma=False,
    )
```
